32 devices in a mesh: gx: 8 (over y, x, core), gy: 4 (over z).
Axes of the slice: x: 2, y: 2, z: 4, core: 2. Of those that a mesh axis runs over, the one named last changes fastest.
Arguments:
- u_now: float32 [3, 6, 64, 512], P(None, None, 'gx', 'gy'), may hold values from -6 to 6
- u_prev: float32 [3, 6, 64, 512], P(None, None, 'gx', 'gy'), may hold values from -6 to 6
- lame_lambda: float32 [6, 64, 512], P(None, 'gx', 'gy'), may hold values from 0.5 to 1.5
- lame_mu: float32 [6, 64, 512], P(None, 'gx', 'gy'), may hold values from 0.3 to 1
- buoyancy: float32 [6, 64, 512], P(None, 'gx', 'gy'), may hold values from 0.5 to 1
- q_now: float32 [2048, 128], P(('gx', 'gy')), may hold values from -3 to 3
- q_prev: float32 [2048, 128], P(('gx', 'gy')), may hold values from -3 to 3
- archetype: int32 [2048], P(('gx', 'gy')), may hold values from 0 to 7
- stiffness: float32 [8, 128, 128], replicated, may hold values from -1.2 to 14, as said below
- couple: float32 [8, 3, 128], replicated, may hold values from -1.5 to 1.5
- counts: int32 [8, 4, 4], P('gx'), may hold values from 1 to 16, as said below
- footprint: int32 [8, 4, 256], P('gx', 'gy'), may hold values from 0 to 1023, as said below
Outputs:
- u_last: float32 [3, 6, 64, 512], P(None, None, 'gx', 'gy')
- u_before: float32 [3, 6, 64, 512], P(None, None, 'gx', 'gy')
- q_last: float32 [2048, 128], P(('gx', 'gy'))
- q_before: float32 [2048, 128], P(('gx', 'gy'))
The draws below stay inside these ranges and needn't reach their ends.
Inputs may be any that keep to these rules, and one draw needn't show every extreme that they name: `stiffness`: symmetric, one matrix for each archetype. `counts`: at most 16; in every tile row some owner column receives 16 from every home column. `footprint`: the 4 cells of a slot form a 2 x 2 square of the home tile's surface, numbered x * 128 + y.
All inputs are finite; a program needn't handle non-finite values.
Results may differ from the reference program's by a relative error of at most 0.0001.
Values sent between devices are 32-bit elements; how exact they have to be, the bound alone decides.
A program may use at most 64 MiB of HBM per device.

```python
import functools
import math
import jax
import jax.numpy as jnp
from jax import lax

CX = 8
CY = 128
NZ = 6
SLOTS_PER_OWNER = 16
FRAME_FREEDOMS = 128
ARCH = 8
FOOTPRINT_CELLS = 4
STEPS = 2
NX = 64
NY = 512
DEVICE_SLOTS = 64
BUILDINGS = 2048
N_GX = 8
N_GY = 4


def draw_stiffness(key, part):
    key_off, key_diag = jax.random.split(jax.random.fold_in(key, 11))
    offdiag = jnp.clip(0.35 * jax.random.normal(key_off, (ARCH, FRAME_FREEDOMS, FRAME_FREEDOMS), jnp.float32), -1.2, 1.2)
    symmetric = 0.5 * (offdiag + jnp.swapaxes(offdiag, 1, 2))
    diagonal = jax.random.uniform(key_diag, (ARCH, FRAME_FREEDOMS), jnp.float32, 10.0, 14.0)
    identity = jnp.eye(FRAME_FREEDOMS, dtype=jnp.float32)
    return symmetric * (1.0 - identity) + diagonal[:, :, None] * identity


def draw_counts(key, part):
    key_base, key_full = jax.random.split(jax.random.fold_in(key, 23))
    base_counts = jax.random.randint(key_base, (N_GX, N_GY, N_GY), 1, SLOTS_PER_OWNER + 1)
    full_owner = jax.random.randint(key_full, (N_GX,), 0, N_GY)
    chosen = jnp.arange(N_GY, dtype=jnp.int32)[None, None, :] == full_owner[:, None, None]
    return jnp.where(chosen, SLOTS_PER_OWNER, base_counts).astype(jnp.int32)


def draw_footprint(key, part):
    key_x, key_y = jax.random.split(jax.random.fold_in(key, 37))
    corner_x = jax.random.randint(key_x, (N_GX, N_GY, N_GY * SLOTS_PER_OWNER, 1), 0, CX - 1)
    corner_y = jax.random.randint(key_y, (N_GX, N_GY, N_GY * SLOTS_PER_OWNER, 1), 0, CY - 1)
    corner_x = corner_x.at[:, :, 0].set(0).at[:, :, -1].set(CX - 2)
    corner_y = corner_y.at[:, :, 0].set(0).at[:, :, -1].set(CY - 2)
    offset_x = jnp.array([0, 0, 1, 1], dtype=jnp.int32)
    offset_y = jnp.array([0, 1, 0, 1], dtype=jnp.int32)
    cells = (corner_x + offset_x) * CY + (corner_y + offset_y)
    return cells.reshape(N_GX, N_GY, N_GY * SLOTS_PER_OWNER * FOOTPRINT_CELLS).astype(jnp.int32)


def touch_ends(values, rng, least, top_value):
    longest = values.shape.index(max(values.shape))
    spots = []
    for shift in (0, 1):
        where = [jax.random.randint(jax.random.fold_in(rng, axis), (), 0, length) for axis, length in enumerate(values.shape)]
        where[longest] = (where[longest] + shift) % values.shape[longest]
        spots.append(tuple(where))
    return values.at[spots[0]].set(least).at[spots[1]].set(top_value)


def levels(stream_key, extent, cuts, low, top_value):
    loudness, own = 1.0, jax.random.fold_in(stream_key, 6)
    for position, shards_of in cuts:
        draws = jnp.exp(jax.random.uniform(jax.random.fold_in(own, position), (shards_of,), jnp.float32, low / len(cuts), top_value / len(cuts)))
        loudness = loudness * jnp.repeat(draws, extent[position] // shards_of).reshape([-1 if axis == position else 1 for axis in range(len(extent))])
    return loudness


def centred(rng, dims, deviation, bound, shards=(), kind=jnp.bfloat16):
    result = jax.random.normal(rng, dims, jnp.float32) * deviation
    if len(shards) > 0:
        result = levels(rng, dims, shards, -0.22, 0.18) * result
    return jnp.clip(result, min=-bound, max=bound).astype(kind)


def setup_inputs(seed: int = 0) -> dict:
    seeds = jax.random.split(jax.random.key(seed), 13)
    u_now = centred(seeds[0], (3, NZ, NX, NY), 1.0, 6.0, ((2, 8), (3, 4)), jnp.float32)
    u_prev = centred(seeds[1], (3, NZ, NX, NY), 1.0, 6.0, ((2, 8), (3, 4)), jnp.float32)
    lame_lambda = jnp.clip(jnp.exp(math.log(1.5) - 1.0986123 * jax.random.uniform(seeds[2], (NZ, NX, NY), jnp.float32) ** levels(seeds[2], (NZ, NX, NY), ((1, 8), (2, 4)), -0.2, 0.2)), 0.5, 1.5)
    lame_mu = jnp.clip(jnp.exp(math.log(1.0) - 1.2039728 * jax.random.uniform(seeds[3], (NZ, NX, NY), jnp.float32) ** levels(seeds[3], (NZ, NX, NY), ((1, 8), (2, 4)), -0.2, 0.2)), 0.3, 1.0)
    buoyancy = jnp.clip(jnp.exp(math.log(1.0) - 0.6931472 * jax.random.uniform(seeds[4], (NZ, NX, NY), jnp.float32) ** levels(seeds[4], (NZ, NX, NY), ((1, 8), (2, 4)), -0.2, 0.2)), 0.5, 1.0)
    q_now = centred(seeds[5], (BUILDINGS, FRAME_FREEDOMS), 0.5, 3.0, ((0, 32),), jnp.float32)
    q_prev = centred(seeds[6], (BUILDINGS, FRAME_FREEDOMS), 0.5, 3.0, ((0, 32),), jnp.float32)
    archetype = touch_ends(jax.random.randint(seeds[7], (BUILDINGS,), 0, ARCH), jax.random.fold_in(seeds[7], 1), 0, ARCH - 1).astype(jnp.int32)
    stiffness = draw_stiffness(jax.random.fold_in(seeds[12], 71), 0)
    couple = centred(seeds[9], (ARCH, 3, FRAME_FREEDOMS), 0.3, 1.5, (), jnp.float32)
    counts = draw_counts(jax.random.fold_in(seeds[12], 71), 0)
    footprint = draw_footprint(jax.random.fold_in(seeds[12], 71), 0)
    return {"u_now": u_now, "u_prev": u_prev, "lame_lambda": lame_lambda, "lame_mu": lame_mu, "buoyancy": buoyancy, "q_now": q_now, "q_prev": q_prev, "archetype": archetype, "stiffness": stiffness, "couple": couple, "counts": counts, "footprint": footprint}


time_step = 0.25


def derive(padded, along):
    field = padded
    for other in (1, 2, 3):
        if other != along:
            field = lax.slice_in_dim(field, 2, field.shape[other] - 2, axis=other)
    length = field.shape[along] - 4

    def window(offset):
        return lax.slice_in_dim(field, offset, offset + length, axis=along)

    return (8.0 * (window(3) - window(1)) - (window(4) - window(0))) / 12.0


def stress_of(padded, lam_field, mu_field):
    grad_x = derive(padded, 2)
    grad_y = derive(padded, 3)
    grad_z = derive(padded, 1)
    trace = grad_x[0] + grad_y[1] + grad_z[2]
    return jnp.stack([
        lam_field * trace + 2.0 * mu_field * grad_x[0],
        lam_field * trace + 2.0 * mu_field * grad_y[1],
        lam_field * trace + 2.0 * mu_field * grad_z[2],
        mu_field * (grad_y[0] + grad_x[1]),
        mu_field * (grad_z[0] + grad_x[2]),
        mu_field * (grad_z[1] + grad_y[2])])


def divergence(padded):
    grad_x = derive(padded, 2)
    grad_y = derive(padded, 3)
    grad_z = derive(padded, 1)
    return jnp.stack([
        grad_x[0] + grad_y[3] + grad_z[4],
        grad_x[3] + grad_y[1] + grad_z[5],
        grad_x[4] + grad_y[5] + grad_z[2]])


def building_group(stiffness, couple, inputs):
    frame_state, prior_frame_state, kinds, ground_motion = inputs
    stiff_sel = stiffness[kinds]
    couple_sel = couple[kinds]
    highest = lax.Precision.HIGHEST
    stiff_term = jnp.einsum('bij,bj->bi', stiff_sel, frame_state, precision=highest)
    shear_force = jnp.einsum('bcj,bj->bc', couple_sel, frame_state, precision=highest)
    drive = jnp.einsum('bcj,bc->bj', couple_sel, ground_motion, precision=highest)
    next_frame_state = 2.0 * frame_state - prior_frame_state + (time_step * time_step) * (drive - stiff_term)
    return next_frame_state, shear_force


def scatter_tile(cells, contrib):
    return jnp.zeros((3, CX * CY), jnp.float32).at[:, cells].add(contrib)


def reference(u_now, u_prev, lame_lambda, lame_mu, buoyancy, q_now, q_prev, archetype, stiffness, couple, counts, footprint):
    building_groups = N_GX * N_GY
    building_slot_index = jnp.arange(SLOTS_PER_OWNER, dtype=jnp.int32)
    active_slots = (building_slot_index[None, None, None, :] < counts[:, :, :, None]).astype(jnp.float32).reshape(N_GX, N_GY, DEVICE_SLOTS)
    index_padded_wide = jnp.broadcast_to(footprint[:, :, None, :], (N_GX, N_GY, 3, DEVICE_SLOTS * FOOTPRINT_CELLS))
    field, older = u_now, u_prev
    frame_state, prior_frame_state = q_now, q_prev
    advance_group = functools.partial(building_group, stiffness, couple)
    scatter_all = jax.vmap(jax.vmap(scatter_tile))
    for counter in range(STEPS):
        surface = field[:, 0].reshape(3, N_GX, CX, N_GY, CY).transpose(1, 3, 0, 2, 4).reshape(N_GX, N_GY, 3, CX * CY)
        entry_values = jnp.take_along_axis(surface, index_padded_wide, axis=3)
        base_layer = entry_values.reshape(N_GX, N_GY, 3, DEVICE_SLOTS, FOOTPRINT_CELLS).sum(axis=4) / FOOTPRINT_CELLS * active_slots[:, :, None, :]
        ground_motion = base_layer.reshape(N_GX, N_GY, 3, N_GY, SLOTS_PER_OWNER).transpose(0, 3, 1, 4, 2).reshape(building_groups, DEVICE_SLOTS, 3)
        next_frame_state, shear_force = lax.map(advance_group, (frame_state.reshape(building_groups, DEVICE_SLOTS, FRAME_FREEDOMS), prior_frame_state.reshape(building_groups, DEVICE_SLOTS, FRAME_FREEDOMS), archetype.reshape(building_groups, DEVICE_SLOTS), ground_motion))
        home_shear_force = shear_force.reshape(N_GX, N_GY, N_GY, SLOTS_PER_OWNER, 3).transpose(0, 2, 4, 1, 3).reshape(N_GX, N_GY, 3, DEVICE_SLOTS) * active_slots[:, :, None, :]
        contrib = jnp.repeat(home_shear_force / FOOTPRINT_CELLS, FOOTPRINT_CELLS, axis=3)
        force_tiles = scatter_all(footprint, contrib)
        force = force_tiles.reshape(N_GX, N_GY, 3, CX, CY).transpose(2, 0, 3, 1, 4).reshape(3, NX, NY)
        padded = jnp.pad(field, ((0, 0), (2, 2), (2, 2), (2, 2)))
        stress = stress_of(padded, lame_lambda, lame_mu)
        total = divergence(jnp.pad(stress, ((0, 0), (2, 2), (2, 2), (2, 2))))
        total = total.at[:, 0].add(force)
        field_new = 2.0 * field - older + (time_step * time_step) * (buoyancy * total)
        older, field = field, field_new
        prior_frame_state, frame_state = frame_state, next_frame_state.reshape(BUILDINGS, FRAME_FREEDOMS)
    return field, older, frame_state, prior_frame_state
```

```python
import functools

import jax
import jax.numpy as jnp
from jax import lax
from jax.experimental import pallas as pl
from jax.experimental.pallas import tpu as pltpu
from jax.sharding import PartitionSpec as P

FOOTPRINT_CELLS = 4
STEPS = 2
TIME_STEP = 0.25
RIM = 4
MESH = pl.DeviceIdType.MESH
F32 = jnp.float32
BF16 = jnp.bfloat16

X_DIRS = ((1, 0), (-1, 0))
Y_DIRS = ((-1, 1), (-1, -1), (0, 1), (0, -1), (1, 1), (1, -1))


def iota(shape, dim):
    return lax.broadcasted_iota(jnp.int32, shape, dim)


def split(value):
    high = value.astype(BF16)
    return high, (value - high.astype(F32)).astype(BF16)


def pack_x(fields):
    half = fields.shape[0] // 2
    first, second = fields[:half], fields[half:]
    upper = iota((1, 8, 128), 1) < RIM
    to_next = jnp.where(upper, pltpu.roll(first, RIM, 1), second)
    to_before = jnp.where(upper, first, pltpu.roll(second, RIM, 1))
    return to_next, to_before


def unpack_x(from_before, from_next):
    upper = iota((1, 8, 128), 1) < RIM
    first = jnp.where(upper, from_next, pltpu.roll(from_before, RIM, 1))
    second = jnp.where(upper, pltpu.roll(from_next, RIM, 1), from_before)
    return jnp.concatenate([first, second], axis=0)


def pack_y(fields):
    count = fields.shape[0]
    lane = iota((8, 128), 1)
    tiles = []
    for start in range(0, count, 16):
        tile = jnp.zeros((8, 128), F32)
        for k in range(start, min(start + 16, count)):
            place = 8 * (k - start)
            moved = pltpu.roll(fields[k], (place + RIM) % 128, 1)
            tile = jnp.where((lane >= place) & (lane < place + 8), moved, tile)
        tiles.append(tile)
    return jnp.stack(tiles)


def unpack_y(tiles, count):
    slabs = []
    for k in range(count):
        slabs.append(pltpu.roll(tiles[k // 16], (124 - 8 * (k % 16)) % 128, 1))
    return jnp.stack(slabs)


def slope(here, other, axis, both):
    size = here.shape[axis]
    place = iota((1,) * (here.ndim - 2) + (8, 128), axis)

    def shifted(mine, theirs, shift):
        entering = place < shift if shift > 0 else place >= size + shift
        return pltpu.roll(jnp.where(entering, theirs, mine), (-shift) % size, axis)

    def slope_of(mine, theirs):
        return 8.0 * (shifted(mine, theirs, 1) - shifted(mine, theirs, -1)) - (
            shifted(mine, theirs, 2) - shifted(mine, theirs, -2)
        )

    if both:
        return slope_of(here, other), slope_of(other, here)
    return slope_of(here, other)


def slope_z(field):
    nothing = jnp.zeros((2,) + field.shape[1:], F32)
    padded = jnp.concatenate([nothing, field, nothing], axis=0)
    n = field.shape[0]
    return 8.0 * (padded[3 : n + 3] - padded[1 : n + 1]) - (padded[4 : n + 4] - padded[:n])


def divergence(u, rim_x, rim_y, corner, lam, mu, lam_x, mu_x, lam_y, mu_y):
    ux, uy, uz = u[0], u[1], u[2]
    x_x, x_xh = slope(ux, rim_x[0], 1, True)
    y_x, y_xh = slope(uy, rim_x[1], 1, True)
    z_x, z_xh = slope(uz, rim_x[2], 1, True)
    x_y, x_yh = slope(ux, rim_y[0], 2, True)
    y_y, y_yh = slope(uy, rim_y[1], 2, True)
    z_y, z_yh = slope(uz, rim_y[2], 2, True)
    x_z, y_z, z_z = slope_z(ux), slope_z(uy), slope_z(uz)
    spread = lam * (x_x + y_y + z_z)
    s_xx = spread + 2.0 * mu * x_x
    s_yy = spread + 2.0 * mu * y_y
    s_zz = spread + 2.0 * mu * z_z
    s_xy = mu * (x_y + y_x)
    s_xz = mu * (x_z + z_x)
    s_yz = mu * (y_z + z_y)
    x_yr = slope(rim_x[0], corner[0], 2, False)
    y_yr = slope(rim_x[1], corner[1], 2, False)
    x_zr, z_zr = slope_z(rim_x[0]), slope_z(rim_x[2])
    s_xx_r = lam_x * (x_xh + y_yr + z_zr) + 2.0 * mu_x * x_xh
    s_xy_r = mu_x * (x_yr + y_xh)
    s_xz_r = mu_x * (x_zr + z_xh)
    x_xc = slope(rim_y[0], corner[0], 1, False)
    y_xc = slope(rim_y[1], corner[1], 1, False)
    y_zc, z_zc = slope_z(rim_y[1]), slope_z(rim_y[2])
    s_yy_c = lam_y * (x_xc + y_yh + z_zc) + 2.0 * mu_y * y_yh
    s_xy_c = mu_y * (x_yh + y_xc)
    s_yz_c = mu_y * (y_zc + z_yh)
    total_x = slope(s_xx, s_xx_r, 1, False) + slope(s_xy, s_xy_c, 2, False) + slope_z(s_xz)
    total_y = slope(s_xy, s_xy_r, 1, False) + slope(s_yy, s_yy_c, 2, False) + slope_z(s_yz)
    total_z = slope(s_xz, s_xz_r, 1, False) + slope(s_yz, s_yz_c, 2, False) + slope_z(s_zz)
    return jnp.stack([total_x, total_y, total_z])


def kernel(
    rows,
    owners,
    u_hbm,
    u_prev_hbm,
    lam_hbm,
    mu_hbm,
    buoy_hbm,
    q_hbm,
    q_prev_hbm,
    arch_hbm,
    stiff_hbm,
    couple_hbm,
    counts_hbm,
    cells_hbm,
    u_last_ref,
    u_before_ref,
    q_last_ref,
    q_before_ref,
    xs0,
    xs1,
    xr0,
    xr1,
    ys,
    yr,
    a_out,
    a_in,
    w_out,
    w_in,
    p_out,
    p_in,
    table,
    u_ref,
    u_prev_ref,
    lam_ref,
    mu_ref,
    buoy_ref,
    q_ref,
    q_prev_ref,
    arch_ref,
    stiff_ref,
    couple_ref,
    counts_ref,
    cells_ref,
    loaded,
    x_send,
    x_recv,
    y_send,
    y_recv,
    b_send,
    b_recv,
    entered,
):
    r, h = lax.axis_index("gx"), lax.axis_index("gy")
    nz = lam_ref.shape[0]
    slots = q_ref.shape[0]
    capacity = slots // owners
    kinds = stiff_ref.shape[0]
    freedoms = q_ref.shape[1]
    dt2 = TIME_STEP * TIME_STEP
    xs, xr = (xs0, xs1), (xr0, xr1)

    def target(direction):
        dx, dy = direction
        there = None
        for d, me, n in ((dx, r, rows), (dy, h, owners)):
            if d:
                ok = me + d < n if d > 0 else me > 0
                there = ok if there is None else there & ok
        return there, (r + dx, h + dy)

    def source(direction):
        return target((-direction[0], -direction[1]))

    loads = {}

    def start_loads(pairs):
        for source_ref, ref in pairs:
            copy = pltpu.make_async_copy(source_ref, ref, loaded.at[len(loads)])
            copy.start()
            loads[id(ref)] = copy

    start_loads(
        (
            (q_hbm, q_ref),
            (couple_hbm, couple_ref),
            (arch_hbm, arch_ref),
            (u_hbm, u_ref),
        )
    )
    peers = X_DIRS + tuple(d for d in Y_DIRS if d[0])

    barrier = pltpu.get_barrier_semaphore()
    arrivals = h + (h + 1 < owners).astype(jnp.int32)
    for step in range(1, owners):
        other = lax.rem(h + step, owners)

        @pl.when((h + step < owners) | (step == owners - 1))
        def _(other=other):
            pl.semaphore_signal(barrier, inc=1, device_id=(r, other), device_id_type=MESH)

    for direction in peers:
        there, device = target(direction)
        arrivals = arrivals + there.astype(jnp.int32)

        @pl.when(there)
        def _(device=device):
            pl.semaphore_signal(barrier, inc=1, device_id=device, device_id_type=MESH)

    start_loads(
        (
            (lam_hbm, lam_ref),
            (mu_hbm, mu_ref),
            (stiff_hbm, stiff_ref),
            (q_prev_hbm, q_prev_ref),
            (cells_hbm, cells_ref),
            (counts_hbm, counts_ref),
            (buoy_hbm, buoy_ref),
            (u_prev_hbm, u_prev_ref),
        )
    )

    for slot, direction in enumerate(X_DIRS):
        there, _ = source(direction)

        @pl.when(jnp.logical_not(there))
        def _(slot=slot):
            for buffer in xr:
                buffer[slot] = jnp.zeros(buffer.shape[1:], F32)

    for slot, direction in enumerate(Y_DIRS):
        there, _ = source(direction)

        @pl.when(jnp.logical_not(there))
        def _(slot=slot):
            for turn in range(STEPS):
                yr[turn, slot] = jnp.zeros(yr.shape[2:], F32)

    def load(ref):
        loads[id(ref)].wait()
        return ref[...]

    def x_copy(turn, slot, device):
        return pltpu.make_async_remote_copy(
            src_ref=xs[turn].at[slot],
            dst_ref=xr[turn].at[slot],
            send_sem=x_send.at[turn, slot],
            recv_sem=x_recv.at[turn, slot],
            device_id=device,
            device_id_type=MESH,
        )

    def y_copy(turn, slot, device):
        return pltpu.make_async_remote_copy(
            src_ref=ys.at[turn],
            dst_ref=yr.at[turn, slot],
            send_sem=y_send.at[turn, slot],
            recv_sem=y_recv.at[turn, slot],
            device_id=device,
            device_id_type=MESH,
        )

    messages = ((a_out, a_in), (w_out, w_in), (p_out, p_in))

    def b_copy(which, step):
        other = lax.rem(h + step, owners)
        out, into = messages[which]
        return pltpu.make_async_remote_copy(
            src_ref=out if which == 0 else out.at[other],
            dst_ref=into.at[h],
            send_sem=b_send.at[which, step],
            recv_sem=b_recv.at[which, step],
            device_id=(r, other),
            device_id_type=MESH,
        )

    def b_arrival(which, step):
        other = lax.rem(h + owners - step, owners)
        out, into = messages[which]
        return pltpu.make_async_remote_copy(
            src_ref=out if which == 0 else out.at[other],
            dst_ref=into.at[other],
            send_sem=b_send.at[which, step],
            recv_sem=b_recv.at[which, step],
            device_id=(r, other),
            device_id_type=MESH,
        )

    def send_rims(turn):
        for copy, dirs in ((x_copy, X_DIRS), (y_copy, Y_DIRS)):
            for slot, direction in enumerate(dirs):
                there, device = target(direction)

                @pl.when(there)
                def _(copy=copy, slot=slot, device=device):
                    copy(turn, slot, device).start()

    def wait_rims(turn):
        for copy, dirs in ((x_copy, X_DIRS), (y_copy, Y_DIRS)):
            for slot, direction in enumerate(dirs):
                there, device = source(direction)

                @pl.when(there)
                def _(copy=copy, slot=slot, device=device):
                    copy(turn, slot, device).wait_recv()

    def wait_sends():
        for turn in range(STEPS):
            for copy, dirs in ((x_copy, X_DIRS), (y_copy, Y_DIRS)):
                for slot, direction in enumerate(dirs):
                    there, device = target(direction)

                    @pl.when(there)
                    def _(copy=copy, slot=slot, device=device, turn=turn):
                        copy(turn, slot, device).wait_send()

        for which in range(len(messages)):
            for step in range(1, owners):
                b_copy(which, step).wait_send()

    def put_rims(turn, fields):
        to_next, to_before = pack_x(fields)
        xs[turn][0] = to_next
        xs[turn][1] = to_before
        tiles = pack_y(fields)
        ys[turn, : tiles.shape[0]] = tiles

    def take_rims(turn, count):
        rim_x = unpack_x(xr[turn][0], xr[turn][1])
        column = (iota((1, 8, 128), 2) & 7) < RIM
        before = jnp.where(column, yr[turn, 4], yr[turn, 5])
        beside = jnp.where(column, yr[turn, 2], yr[turn, 3])
        after = jnp.where(column, yr[turn, 0], yr[turn, 1])
        corner = jnp.where(iota((1, 8, 128), 1) < RIM, after, before)
        return rim_x, unpack_y(beside, count), unpack_y(corner, 3 * nz)

    def send_buildings(which):
        for step in range(owners // 2, 0, -1):
            b_copy(which, step).start()
            if owners - step != step:
                b_copy(which, owners - step).start()

    def take_buildings(which):
        for step in range(1, owners):
            b_arrival(which, step).wait_recv()
        into = messages[which][1]
        return into[...].reshape(slots, into.shape[2])

    lane = iota((slots, 128), 1)
    part = lane & 31
    slot_row = iota((slots, 1), 0)
    square = (slots, slots)

    couple = load(couple_ref)
    arch = jnp.sum(
        jnp.where(iota(square, 0) == iota(square, 1), load(arch_ref).astype(F32), 0.0),
        axis=1,
        keepdims=True,
    )
    is_kind = [arch == float(a) for a in range(kinds)]
    coupling = []
    for c in range(3):
        chosen = jnp.zeros((slots, freedoms), F32)
        for a in range(kinds):
            chosen = jnp.where(is_kind[a], couple[c, a : a + 1, :], chosen)
        coupling.append(chosen)

    def couple_sum(c, state):
        return jnp.sum(coupling[c] * state, axis=1, keepdims=True)

    q = load(q_ref)
    shear = [couple_sum(c, q) for c in range(3)]
    shear = jnp.where(part < 8, shear[0], jnp.where(part < 16, shear[1], shear[2]))
    shear = shear.reshape(owners, capacity, 128)
    group = iota((capacity, 128), 1) // 32
    for t in range(a_out.shape[1] // 128):
        tile = shear[4 * t]
        for k in range(1, 4):
            if 4 * t + k < owners:
                tile = jnp.where(group == k, shear[4 * t + k], tile)
        a_out[:, 128 * t : 128 * (t + 1)] = tile
    a_in[h] = a_out[...]

    u = load(u_ref)
    lam, mu = load(lam_ref) * (1.0 / 144.0), load(mu_ref) * (1.0 / 144.0)
    put_rims(0, jnp.concatenate([u.reshape(3 * nz, 8, 128), lam, mu], axis=0))
    pl.semaphore_wait(barrier, arrivals)
    for step in range(1, owners - 1):
        other = lax.rem(h + step, owners)

        @pl.when(h + step >= owners)
        def _(step=step, other=other):
            pl.semaphore_signal(
                entered.at[owners - step], inc=1, device_id=(r, other), device_id_type=MESH
            )

    for step in range(1, owners):

        @pl.when((h + step >= owners) | (step == 1))
        def _(step=step):
            b_copy(0, step).start()

    send_rims(0)

    cells = load(cells_ref)[0].astype(F32)
    wide = (slots, slots * FOOTPRINT_CELLS)
    own = (iota(wide, 1) // FOOTPRINT_CELLS) == iota(wide, 0)
    corner_cell = jnp.min(jnp.where(own, cells, 1e9), axis=1, keepdims=True)
    corner_x = jnp.floor(corner_cell * (1.0 / 128.0))
    corner_y = corner_cell - 128.0 * corner_x
    along_y = lane.astype(F32) - corner_y
    in_y = ((along_y == 0.0) | (along_y == 1.0)).astype(F32)
    window_y = in_y.astype(BF16)
    along_x = (lane & 7).astype(F32) - corner_x
    loads[id(counts_ref)].wait()
    row_counts = counts_ref[0, pl.ds(h, 1), :].astype(F32)
    pairs = (slots, owners)
    live_count = jnp.sum(
        jnp.where(iota(pairs, 0) // capacity == iota(pairs, 1), row_counts, 0.0),
        axis=1,
        keepdims=True,
    )
    live = (slot_row % capacity).astype(F32) < live_count
    weight = jnp.where(
        live & ((along_x == 0.0) | (along_x == 1.0)) & (part < 24), 1.0 / FOOTPRINT_CELLS, 0.0
    )
    base_weight = jnp.where(lane < 64, weight, 0.0)
    mine = [(lane < 64) & (part >= 8 * c) & (part < 8 * c + 8) for c in range(3)]

    def group_sum(c, value):
        return jnp.sum(jnp.where(mine[c], value, 0.0), axis=1, keepdims=True)

    def surface_motion(field):
        surface = field[:, 0]
        high = surface.astype(BF16).astype(F32)
        nothing = jnp.zeros((8, 128), F32)
        stacked = jnp.concatenate(
            [high.reshape(24, 128), nothing, (surface - high).reshape(24, 128), nothing]
            + [nothing] * 8,
            axis=0,
        ).astype(BF16)
        gathered = lax.dot_general(
            window_y, stacked, (((1,), (1,)), ((), ())), preferred_element_type=F32
        )
        return gathered * base_weight

    def surface_force(pull):
        high = pull.astype(BF16).astype(F32)
        pull = jnp.where((lane & 32) == 0, high, pull - high)
        spread = lax.dot_general(
            pull.T.astype(BF16), window_y, (((1,), (0,)), ((), ())), preferred_element_type=F32
        )
        return (spread[0:24] + spread[32:56]).reshape(3, 8, 128)

    def drive_of(base):
        drive = coupling[0] * base[0]
        for c in range(1, 3):
            drive = drive + coupling[c] * base[c]
        return drive

    def stiff_term(state):
        high, low = split(state)
        stacked = jnp.concatenate([high.astype(F32), low.astype(F32)], axis=0)
        twice = jnp.concatenate([arch, arch], axis=0)
        spread = jnp.concatenate(
            [jnp.where(twice == float(a), stacked, 0.0).astype(BF16) for a in range(kinds)],
            axis=1,
        )
        product = jnp.dot(spread, table[...], preferred_element_type=F32)
        product = product[:, :freedoms] + product[:, freedoms:]
        return product[:slots] + product[slots:]

    base = surface_motion(u)
    home_base = [group_sum(c, base) for c in range(3)]

    gain = load(buoy_ref) * dt2
    overlap_left, overlap_right = [], []
    for x in range(8):
        there = live & ((corner_x == float(x)) | (corner_x == float(x - 1)))
        window = jnp.where(there, in_y, 0.0)
        overlap_right.append(window)
        overlap_left.append(window * (gain[0, x : x + 1, :] * (1.0 / FOOTPRINT_CELLS**2)))
    left_high, left_low = split(jnp.concatenate(overlap_left, axis=1))
    right = jnp.concatenate(overlap_right, axis=1)
    width = w_out.shape[2]
    blank = [jnp.zeros((64, right.shape[1]), F32)]
    spare = width - 64 - slots
    after = [jnp.zeros((spare, right.shape[1]), F32)] if spare else []
    right = jnp.concatenate(blank + [right] + after, axis=0).astype(BF16)
    nt = (((1,), (1,)), ((), ()))
    overlap = lax.dot_general(left_high, right, nt, preferred_element_type=F32)
    overlap = overlap + lax.dot_general(left_low, right, nt, preferred_element_type=F32)

    stiff_high, stiff_low = split(load(stiff_ref).reshape(kinds * freedoms, freedoms))
    table[:, :freedoms] = stiff_high
    table[:, freedoms:] = stiff_low
    coasting = 2.0 * q - load(q_prev_ref) - dt2 * stiff_term(q)
    fields = base
    columns = [couple_sum(c, coasting) for c in range(3)]
    pairs_of = ((0, 0), (0, 1), (0, 2), (1, 1), (1, 2), (2, 2))
    columns += [dt2 * couple_sum(c, coupling[d]) for c, d in pairs_of]
    places = (24, 25, 26, 27, 28, 29, 30, 31, 56)
    for place, column in zip(places, columns):
        fields = jnp.where(lane == place, column, fields)
    first = jnp.where(lane < 64, fields, overlap[:, :128])
    if width > 128:
        first = jnp.concatenate([first, overlap[:, 128:]], axis=1)
    w_out[...] = first.reshape(owners, capacity, width)
    w_in[h] = w_out[h]
    for step in range(2, owners):

        @pl.when(h + step < owners)
        def _(step=step):
            pl.semaphore_wait(entered.at[step], 1)
            b_copy(0, step).start()

    send_buildings(1)

    u_old = load(u_prev_ref)

    shape = (3, nz, 8, 128)

    def push(turn, field, lam_mu):
        count = (5 if turn == 0 else 3) * nz
        rim_x, rim_y, corner = take_rims(turn, count)
        if turn == 0:
            lam_mu = rim_x[3 * nz :], rim_y[3 * nz :]
        lam_mu_x, lam_mu_y = lam_mu
        total = divergence(
            field,
            rim_x[: 3 * nz].reshape(shape),
            rim_y[: 3 * nz].reshape(shape),
            corner.reshape(shape),
            lam,
            mu,
            lam_mu_x[:nz],
            lam_mu_x[nz:],
            lam_mu_y[:nz],
            lam_mu_y[nz:],
        )
        return total, lam_mu

    def on_surface(field, force):
        return jnp.concatenate([field[:, :1] + (gain[0] * force)[:, None], field[:, 1:]], axis=1)

    wait_rims(0)
    total, lam_mu = push(0, u, None)
    free = 2.0 * u - u_old + gain * total
    p_out[...] = surface_motion(free).reshape(owners, capacity, 128)
    p_in[h] = p_out[h]
    send_buildings(2)

    shears = take_buildings(0)
    pull = jnp.zeros((slots, 128), F32)
    for t in range(a_out.shape[1] // 128):
        here = (lane // 32 + 4 * t) == h
        pull = pull + jnp.where(here, shears[:, 128 * t : 128 * (t + 1)], 0.0)
    pull = pull + pltpu.roll(pull, 64, 1)
    pull = pull + pltpu.roll(pull, 32, 1)
    u_new = on_surface(free, surface_force(pull * weight))
    u, u_old = u_new, u
    put_rims(1, u.reshape(3 * nz, 8, 128))
    send_rims(1)
    u_before_ref[...] = u

    words = take_buildings(1)
    low_words = words[:, :128]
    drive = drive_of([group_sum(c, low_words) for c in range(3)])
    q, q_old = coasting + dt2 * drive, q
    q_before_ref[...] = q
    stiff = stiff_term(q)

    gram = {}
    for place, pair in zip(places[3:], pairs_of):
        gram[pair] = gram[pair[::-1]] = low_words[:, place : place + 1]
    later = []
    for c in range(3):
        value = low_words[:, 24 + c : 25 + c]
        for d in range(3):
            value = value + gram[c, d] * home_base[d]
        later.append(value)
    later = jnp.where(part < 8, later[0], jnp.where(part < 16, later[1], later[2]))
    force = surface_force(later * weight)

    left_high, left_low = split(words)
    blank = [jnp.zeros((64, shears.shape[1]), F32)]
    after = [jnp.zeros((spare, shears.shape[1]), F32)] if spare else []
    right = jnp.concatenate(blank + [shears] + after, axis=0)
    right_high, right_low = split(right)
    moved = jnp.dot(left_high, right_high, preferred_element_type=F32)
    moved = moved + jnp.dot(left_low, right_high, preferred_element_type=F32)
    moved = moved + jnp.dot(left_high, right_low, preferred_element_type=F32)
    moved_lane = iota(moved.shape, 1)
    moved_row = iota(moved.shape, 0) // capacity * 32
    moved = [
        jnp.sum(jnp.where(moved_lane == moved_row + 8 * c, moved, 0.0), axis=1, keepdims=True)
        for c in range(3)
    ]
    q_free = 2.0 * q - q_old + dt2 * (drive_of(moved) - stiff)
    u_free = on_surface(2.0 * u - u_old, force)

    wait_rims(1)
    total, _ = push(1, u, lam_mu)
    u_last_ref[...] = u_free + gain * total

    motion = take_buildings(2)
    q_last_ref[...] = q_free + dt2 * drive_of([group_sum(c, motion) for c in range(3)])
    wait_sends()


def shards(
    rows,
    owners,
    u_now,
    u_prev,
    lame_lambda,
    lame_mu,
    buoyancy,
    q_now,
    q_prev,
    archetype,
    stiffness,
    couple,
    counts,
    footprint,
):
    nz = lame_mu.shape[0]
    slots, freedoms = q_now.shape
    capacity = slots // owners
    kinds = stiffness.shape[0]
    pairs = (5 * nz) // 2, (3 * nz) // 2
    a_width = -(-32 * owners // 128) * 128
    w_width = -(-(64 + slots) // 128) * 128
    vmem = pl.BlockSpec(memory_space=pltpu.VMEM)
    hbm = pl.BlockSpec(memory_space=pltpu.HBM)
    dma = pltpu.SemaphoreType.DMA
    operands = (
        u_now,
        u_prev,
        lame_lambda,
        lame_mu,
        buoyancy,
        q_now,
        q_prev,
        archetype.reshape(1, slots),
        stiffness,
        couple.transpose(1, 0, 2),
        counts,
        footprint,
    )
    results = (
        jax.ShapeDtypeStruct(u_now.shape, F32),
        jax.ShapeDtypeStruct(u_now.shape, F32),
        jax.ShapeDtypeStruct(q_now.shape, F32),
        jax.ShapeDtypeStruct(q_now.shape, F32),
    )
    held = pl.pallas_call(
        functools.partial(kernel, rows, owners),
        out_shape=tuple(pltpu.VMEM(result.shape, result.dtype) for result in results),
        in_specs=[hbm] * len(operands),
        out_specs=(vmem,) * 4,
        scratch_shapes=[
            pltpu.VMEM((2, pairs[0], 8, 128), F32),
            pltpu.VMEM((2, pairs[1], 8, 128), F32),
            pltpu.VMEM((2, pairs[0], 8, 128), F32),
            pltpu.VMEM((2, pairs[1], 8, 128), F32),
            pltpu.VMEM((STEPS, 2, 8, 128), F32),
            pltpu.VMEM((STEPS, len(Y_DIRS), 2, 8, 128), F32),
            pltpu.VMEM((capacity, a_width), F32),
            pltpu.VMEM((owners, capacity, a_width), F32),
            pltpu.VMEM((owners, capacity, w_width), F32),
            pltpu.VMEM((owners, capacity, w_width), F32),
            pltpu.VMEM((owners, capacity, 128), F32),
            pltpu.VMEM((owners, capacity, 128), F32),
            pltpu.VMEM((kinds * freedoms, 2 * freedoms), BF16),
        ]
        + [pltpu.VMEM(operand.shape, operand.dtype) for operand in operands]
        + [
            dma((len(operands),)),
            dma((STEPS, 2)),
            dma((STEPS, 2)),
            dma((STEPS, len(Y_DIRS))),
            dma((STEPS, len(Y_DIRS))),
            dma((3, owners)),
            dma((3, owners)),
            pltpu.SemaphoreType.REGULAR((owners,)),
        ],
        compiler_params=pltpu.CompilerParams(
            collective_id=0, has_side_effects=True, vmem_limit_bytes=60 * 1024 * 1024
        ),
    )(*operands)
    return pl.pallas_call(
        store,
        out_shape=results,
        in_specs=[vmem] * 4,
        out_specs=(hbm,) * 4,
        scratch_shapes=[dma((4,))],
        compiler_params=pltpu.CompilerParams(vmem_limit_bytes=1024 * 1024),
    )(*held)


def store(*refs):
    copies = [
        pltpu.make_async_copy(refs[k], refs[4 + k], refs[8].at[k]) for k in range(4)
    ]
    for copy in copies:
        copy.start()
    for copy in copies:
        copy.wait()


def solution(mesh):
    return jax.shard_map(
        functools.partial(shards, mesh.shape["gx"], mesh.shape["gy"]),
        mesh=mesh,
        in_specs=(
            P(None, None, "gx", "gy"),
            P(None, None, "gx", "gy"),
            P(None, "gx", "gy"),
            P(None, "gx", "gy"),
            P(None, "gx", "gy"),
            P(("gx", "gy"), None),
            P(("gx", "gy"), None),
            P(("gx", "gy")),
            P(),
            P(),
            P("gx", None, None),
            P("gx", "gy", None),
        ),
        out_specs=(
            P(None, None, "gx", "gy"),
            P(None, None, "gx", "gy"),
            P(("gx", "gy"), None),
            P(("gx", "gy"), None),
        ),
        check_vma=False,
    )
```

```python
import functools

import jax
import jax.numpy as jnp
from jax import lax
from jax.experimental import pallas as pl
from jax.experimental.pallas import tpu as pltpu
from jax.sharding import PartitionSpec as P

FOOTPRINT_CELLS = 4
STEPS = 2
TIME_STEP = 0.25
RIM = 4
MESH = pl.DeviceIdType.MESH
F32 = jnp.float32
BF16 = jnp.bfloat16

X_DIRS = ((1, 0), (-1, 0))
Y_DIRS = ((-1, 1), (-1, -1), (0, 1), (0, -1), (1, 1), (1, -1))


def iota(shape, dim):
    return lax.broadcasted_iota(jnp.int32, shape, dim)


def split(value):
    high = value.astype(BF16)
    return high, (value - high.astype(F32)).astype(BF16)


def pack_x(fields):
    half = fields.shape[0] // 2
    first, second = fields[:half], fields[half:]
    upper = iota((1, 8, 128), 1) < RIM
    to_next = jnp.where(upper, pltpu.roll(first, RIM, 1), second)
    to_before = jnp.where(upper, first, pltpu.roll(second, RIM, 1))
    return to_next, to_before


def unpack_x(from_before, from_next):
    upper = iota((1, 8, 128), 1) < RIM
    first = jnp.where(upper, from_next, pltpu.roll(from_before, RIM, 1))
    second = jnp.where(upper, pltpu.roll(from_next, RIM, 1), from_before)
    return jnp.concatenate([first, second], axis=0)


def pack_y(fields):
    lane = iota((8, 128), 1)
    ahead, behind = jnp.zeros((8, 128), F32), jnp.zeros((8, 128), F32)
    for k in range(fields.shape[0]):
        place = RIM * k
        moved = pltpu.roll(fields[k], (place + RIM) % 128, 1)
        ahead = jnp.where((lane >= place) & (lane < place + RIM), moved, ahead)
        behind = jnp.where((lane >= place + RIM) & (lane < place + 2 * RIM), moved, behind)
    return ahead, behind


def unpack_y(ahead, behind, count):
    odd = (iota((8, 128), 1) & RIM) != 0
    tiles = jnp.where(odd, behind, ahead), jnp.where(odd, ahead, behind)
    slabs = []
    for k in range(count):
        slabs.append(pltpu.roll(tiles[k % 2], (124 - RIM * k) % 128, 1))
    return jnp.stack(slabs)


def slope(here, other, axis, both):
    size = here.shape[axis]
    place = iota((1,) * (here.ndim - 2) + (8, 128), axis)

    def shifted(mine, theirs, shift):
        entering = place < shift if shift > 0 else place >= size + shift
        return pltpu.roll(jnp.where(entering, theirs, mine), (-shift) % size, axis)

    def slope_of(mine, theirs):
        return 8.0 * (shifted(mine, theirs, 1) - shifted(mine, theirs, -1)) - (
            shifted(mine, theirs, 2) - shifted(mine, theirs, -2)
        )

    if both:
        return slope_of(here, other), slope_of(other, here)
    return slope_of(here, other)


def slope_z(field):
    nothing = jnp.zeros((2,) + field.shape[1:], F32)
    padded = jnp.concatenate([nothing, field, nothing], axis=0)
    n = field.shape[0]
    return 8.0 * (padded[3 : n + 3] - padded[1 : n + 1]) - (padded[4 : n + 4] - padded[:n])


def divergence(u, rim_x, rim_y, corner, lam, mu, lam_x, mu_x, lam_y, mu_y):
    ux, uy, uz = u[0], u[1], u[2]
    x_x, x_xh = slope(ux, rim_x[0], 1, True)
    y_x, y_xh = slope(uy, rim_x[1], 1, True)
    z_x, z_xh = slope(uz, rim_x[2], 1, True)
    x_y, x_yh = slope(ux, rim_y[0], 2, True)
    y_y, y_yh = slope(uy, rim_y[1], 2, True)
    z_y, z_yh = slope(uz, rim_y[2], 2, True)
    x_z, y_z, z_z = slope_z(ux), slope_z(uy), slope_z(uz)
    spread = lam * (x_x + y_y + z_z)
    s_xx = spread + 2.0 * mu * x_x
    s_yy = spread + 2.0 * mu * y_y
    s_zz = spread + 2.0 * mu * z_z
    s_xy = mu * (x_y + y_x)
    s_xz = mu * (x_z + z_x)
    s_yz = mu * (y_z + z_y)
    x_yr = slope(rim_x[0], corner[0], 2, False)
    y_yr = slope(rim_x[1], corner[1], 2, False)
    x_zr, z_zr = slope_z(rim_x[0]), slope_z(rim_x[2])
    s_xx_r = lam_x * (x_xh + y_yr + z_zr) + 2.0 * mu_x * x_xh
    s_xy_r = mu_x * (x_yr + y_xh)
    s_xz_r = mu_x * (x_zr + z_xh)
    x_xc = slope(rim_y[0], corner[0], 1, False)
    y_xc = slope(rim_y[1], corner[1], 1, False)
    y_zc, z_zc = slope_z(rim_y[1]), slope_z(rim_y[2])
    s_yy_c = lam_y * (x_xc + y_yh + z_zc) + 2.0 * mu_y * y_yh
    s_xy_c = mu_y * (x_yh + y_xc)
    s_yz_c = mu_y * (y_zc + z_yh)
    total_x = slope(s_xx, s_xx_r, 1, False) + slope(s_xy, s_xy_c, 2, False) + slope_z(s_xz)
    total_y = slope(s_xy, s_xy_r, 1, False) + slope(s_yy, s_yy_c, 2, False) + slope_z(s_yz)
    total_z = slope(s_xz, s_xz_r, 1, False) + slope(s_yz, s_yz_c, 2, False) + slope_z(s_zz)
    return jnp.stack([total_x, total_y, total_z])


def kernel(
    rows,
    owners,
    u_hbm,
    u_prev_hbm,
    lam_hbm,
    mu_hbm,
    buoy_hbm,
    q_hbm,
    q_prev_hbm,
    arch_hbm,
    stiff_hbm,
    couple_hbm,
    counts_hbm,
    cells_hbm,
    u_last_ref,
    u_before_ref,
    q_last_ref,
    q_before_ref,
    xs0,
    xs1,
    xr0,
    xr1,
    ys,
    yr,
    cr,
    a_out,
    a_in,
    w_out,
    w_in,
    p_out,
    p_in,
    table,
    u_ref,
    u_prev_ref,
    lam_ref,
    mu_ref,
    buoy_ref,
    q_ref,
    q_prev_ref,
    arch_ref,
    stiff_ref,
    couple_ref,
    counts_ref,
    cells_ref,
    loaded,
    x_send,
    x_recv,
    y_send,
    y_recv,
    b_send,
    b_recv,
    entered,
):
    r, h = lax.axis_index("gx"), lax.axis_index("gy")
    nz = lam_ref.shape[0]
    slots = q_ref.shape[0]
    capacity = slots // owners
    kinds = stiff_ref.shape[0]
    freedoms = q_ref.shape[1]
    dt2 = TIME_STEP * TIME_STEP
    xs, xr = (xs0, xs1), (xr0, xr1)

    def target(direction):
        dx, dy = direction
        there = None
        for d, me, n in ((dx, r, rows), (dy, h, owners)):
            if d:
                ok = me + d < n if d > 0 else me > 0
                there = ok if there is None else there & ok
        return there, (r + dx, h + dy)

    def source(direction):
        return target((-direction[0], -direction[1]))

    loads = {}

    def start_loads(pairs):
        for source_ref, ref in pairs:
            copy = pltpu.make_async_copy(source_ref, ref, loaded.at[len(loads)])
            copy.start()
            loads[id(ref)] = copy

    start_loads(
        (
            (q_hbm, q_ref),
            (couple_hbm, couple_ref),
            (arch_hbm, arch_ref),
            (u_hbm, u_ref),
        )
    )
    peers = X_DIRS + tuple(d for d in Y_DIRS if d[0])

    barrier = pltpu.get_barrier_semaphore()
    arrivals = h + (h + 1 < owners).astype(jnp.int32)
    for step in range(1, owners):
        other = lax.rem(h + step, owners)

        @pl.when((h + step < owners) | (step == owners - 1))
        def _(other=other):
            pl.semaphore_signal(barrier, inc=1, device_id=(r, other), device_id_type=MESH)

    for direction in peers:
        there, device = target(direction)
        arrivals = arrivals + there.astype(jnp.int32)

        @pl.when(there)
        def _(device=device):
            pl.semaphore_signal(barrier, inc=1, device_id=device, device_id_type=MESH)

    start_loads(
        (
            (lam_hbm, lam_ref),
            (mu_hbm, mu_ref),
            (stiff_hbm, stiff_ref),
            (q_prev_hbm, q_prev_ref),
            (cells_hbm, cells_ref),
            (counts_hbm, counts_ref),
            (buoy_hbm, buoy_ref),
            (u_prev_hbm, u_prev_ref),
        )
    )

    def half(ref, dx):
        return ref if dx == 0 else ref.at[pl.ds(RIM if dx > 0 else 0, RIM)]

    def y_place(turn, direction):
        dx, dy = direction
        k = 0 if dy > 0 else 1
        return half((cr if dx else yr).at[turn, k], dx)

    for slot, direction in enumerate(X_DIRS):
        there, _ = source(direction)

        @pl.when(jnp.logical_not(there))
        def _(slot=slot):
            for buffer in xr:
                buffer[slot] = jnp.zeros(buffer.shape[1:], F32)

    for slot, direction in enumerate(Y_DIRS):
        there, _ = source(direction)

        @pl.when(jnp.logical_not(there))
        def _(direction=direction):
            for turn in range(STEPS):
                ref = y_place(turn, direction)
                ref[...] = jnp.zeros(ref.shape, F32)

    def load(ref):
        loads[id(ref)].wait()
        return ref[...]

    def x_copy(turn, slot, device):
        return pltpu.make_async_remote_copy(
            src_ref=xs[turn].at[slot],
            dst_ref=xr[turn].at[slot],
            send_sem=x_send.at[turn, slot],
            recv_sem=x_recv.at[turn, slot],
            device_id=device,
            device_id_type=MESH,
        )

    def y_copy(turn, slot, device):
        return pltpu.make_async_remote_copy(
            src_ref=half(ys.at[turn, 0 if Y_DIRS[slot][1] > 0 else 1], Y_DIRS[slot][0]),
            dst_ref=y_place(turn, Y_DIRS[slot]),
            send_sem=y_send.at[turn, slot],
            recv_sem=y_recv.at[turn, slot],
            device_id=device,
            device_id_type=MESH,
        )

    messages = ((a_out, a_in), (w_out, w_in), (p_out, p_in))

    def b_copy(which, step):
        other = lax.rem(h + step, owners)
        out, into = messages[which]
        return pltpu.make_async_remote_copy(
            src_ref=out if which == 0 else out.at[other],
            dst_ref=into.at[h],
            send_sem=b_send.at[which, step],
            recv_sem=b_recv.at[which, step],
            device_id=(r, other),
            device_id_type=MESH,
        )

    def b_arrival(which, step):
        other = lax.rem(h + owners - step, owners)
        out, into = messages[which]
        return pltpu.make_async_remote_copy(
            src_ref=out if which == 0 else out.at[other],
            dst_ref=into.at[other],
            send_sem=b_send.at[which, step],
            recv_sem=b_recv.at[which, step],
            device_id=(r, other),
            device_id_type=MESH,
        )

    def send_rims(turn):
        for copy, dirs in ((x_copy, X_DIRS), (y_copy, Y_DIRS)):
            for slot, direction in enumerate(dirs):
                there, device = target(direction)

                @pl.when(there)
                def _(copy=copy, slot=slot, device=device):
                    copy(turn, slot, device).start()

    def wait_rims(turn):
        for copy, dirs in ((x_copy, X_DIRS), (y_copy, Y_DIRS)):
            for slot, direction in enumerate(dirs):
                there, device = source(direction)

                @pl.when(there)
                def _(copy=copy, slot=slot, device=device):
                    copy(turn, slot, device).wait_recv()

    def wait_sends():
        for turn in range(STEPS):
            for copy, dirs in ((x_copy, X_DIRS), (y_copy, Y_DIRS)):
                for slot, direction in enumerate(dirs):
                    there, device = target(direction)

                    @pl.when(there)
                    def _(copy=copy, slot=slot, device=device, turn=turn):
                        copy(turn, slot, device).wait_send()

        for which in range(len(messages)):
            for step in range(1, owners):
                b_copy(which, step).wait_send()

    def put_rims(turn, fields):
        to_next, to_before = pack_x(fields)
        xs[turn][0] = to_next
        xs[turn][1] = to_before
        ys[turn, 0], ys[turn, 1] = pack_y(fields)

    def take_rims(turn, count):
        rim_x = unpack_x(xr[turn][0], xr[turn][1])
        rim_y = unpack_y(yr[turn, 0], yr[turn, 1], count)
        return rim_x, rim_y, unpack_y(cr[turn, 0], cr[turn, 1], 3 * nz)

    def send_buildings(which):
        for step in range(owners // 2, 0, -1):
            b_copy(which, step).start()
            if owners - step != step:
                b_copy(which, owners - step).start()

    def take_buildings(which):
        for step in range(1, owners):
            b_arrival(which, step).wait_recv()
        into = messages[which][1][...]
        if into.shape[1] < capacity:
            into = jnp.concatenate([into, pltpu.roll(into, into.shape[2] // 2, 2)], axis=1)
        return into.reshape(slots, into.shape[2])

    lane = iota((slots, 128), 1)
    part = lane & 31
    slot_row = iota((slots, 1), 0)
    square = (slots, slots)

    couple = load(couple_ref)
    arch = jnp.sum(
        jnp.where(iota(square, 0) == iota(square, 1), load(arch_ref).astype(F32), 0.0),
        axis=1,
        keepdims=True,
    )
    is_kind = [arch == float(a) for a in range(kinds)]
    coupling = []
    for c in range(3):
        chosen = jnp.zeros((slots, freedoms), F32)
        for a in range(kinds):
            chosen = jnp.where(is_kind[a], couple[c, a : a + 1, :], chosen)
        coupling.append(chosen)

    def couple_sum(c, state):
        return jnp.sum(coupling[c] * state, axis=1, keepdims=True)

    q = load(q_ref)
    shear = [couple_sum(c, q) for c in range(3)]
    word = lane & 15
    shear = jnp.where(word < 4, shear[0], jnp.where(word < 8, shear[1], shear[2]))
    shear = shear.reshape(owners, 2, 8, 128)
    group = iota((8, 128), 1) // 16
    a_width = a_out.shape[1]
    for t in range(a_width // 128):
        tile = jnp.zeros((8, 128), F32)
        for k in range(8):
            which, home = divmod(8 * t + k, a_width // 32)
            if home < owners:
                tile = jnp.where(group == k, shear[home, which], tile)
        a_out[:, 128 * t : 128 * (t + 1)] = tile
    a_in[h] = a_out[...]

    u = load(u_ref)
    lam, mu = load(lam_ref) * (1.0 / 144.0), load(mu_ref) * (1.0 / 144.0)
    put_rims(0, jnp.concatenate([u.reshape(3 * nz, 8, 128), lam, mu], axis=0))
    pl.semaphore_wait(barrier, arrivals)
    for step in range(1, owners - 1):
        other = lax.rem(h + step, owners)

        @pl.when(h + step >= owners)
        def _(step=step, other=other):
            pl.semaphore_signal(
                entered.at[owners - step], inc=1, device_id=(r, other), device_id_type=MESH
            )

    for step in range(1, owners):

        @pl.when((h + step >= owners) | (step == 1))
        def _(step=step):
            b_copy(0, step).start()

    send_rims(0)

    cells = load(cells_ref)[0].astype(F32)
    wide = (slots, slots * FOOTPRINT_CELLS)
    own = (iota(wide, 1) // FOOTPRINT_CELLS) == iota(wide, 0)
    corner_cell = jnp.min(jnp.where(own, cells, 1e9), axis=1, keepdims=True)
    corner_x = jnp.floor(corner_cell * (1.0 / 128.0))
    corner_y = corner_cell - 128.0 * corner_x
    along_y = lane.astype(F32) - corner_y
    in_y = ((along_y == 0.0) | (along_y == 1.0)).astype(F32)
    window_y = in_y.astype(BF16)
    along_x = (lane & 7).astype(F32) - corner_x
    loads[id(counts_ref)].wait()
    row_counts = counts_ref[0, pl.ds(h, 1), :].astype(F32)
    pairs = (slots, owners)
    live_count = jnp.sum(
        jnp.where(iota(pairs, 0) // capacity == iota(pairs, 1), row_counts, 0.0),
        axis=1,
        keepdims=True,
    )
    live = (slot_row % capacity).astype(F32) < live_count
    weight = jnp.where(
        live & ((along_x == 0.0) | (along_x == 1.0)) & (part < 24), 1.0 / FOOTPRINT_CELLS, 0.0
    )
    base_weight = jnp.where(lane < 64, weight, 0.0)
    mine = [(lane < 64) & (part >= 8 * c) & (part < 8 * c + 8) for c in range(3)]

    def group_sum(c, value):
        return jnp.sum(jnp.where(mine[c], value, 0.0), axis=1, keepdims=True)

    def surface_motion(field):
        surface = field[:, 0]
        high = surface.astype(BF16).astype(F32)
        nothing = jnp.zeros((8, 128), F32)
        stacked = jnp.concatenate(
            [high.reshape(24, 128), nothing, (surface - high).reshape(24, 128), nothing]
            + [nothing] * 8,
            axis=0,
        ).astype(BF16)
        gathered = lax.dot_general(
            window_y, stacked, (((1,), (1,)), ((), ())), preferred_element_type=F32
        )
        return gathered * base_weight

    def halves(pull):
        high = pull.astype(BF16).astype(F32)
        return jnp.where((lane & 32) == 0, high, pull - high)

    def surface_force(pull):
        spread = lax.dot_general(
            pull.T.astype(BF16), window_y, (((1,), (0,)), ((), ())), preferred_element_type=F32
        )
        return (spread[0:24] + spread[32:56]).reshape(3, 8, 128)

    def drive_of(base):
        drive = coupling[0] * base[0]
        for c in range(1, 3):
            drive = drive + coupling[c] * base[c]
        return drive

    def stiff_term(state):
        high, low = split(state)
        stacked = jnp.concatenate([high.astype(F32), low.astype(F32)], axis=0)
        twice = jnp.concatenate([arch, arch], axis=0)
        spread = jnp.concatenate(
            [jnp.where(twice == float(a), stacked, 0.0).astype(BF16) for a in range(kinds)],
            axis=1,
        )
        product = jnp.dot(spread, table[...], preferred_element_type=F32)
        product = product[:, :freedoms] + product[:, freedoms:]
        return product[:slots] + product[slots:]

    base = surface_motion(u)
    home_base = [group_sum(c, base) for c in range(3)]

    gain = load(buoy_ref) * dt2
    overlap_left, overlap_right = [], []
    for x in range(8):
        there = live & ((corner_x == float(x)) | (corner_x == float(x - 1)))
        window = jnp.where(there, in_y, 0.0)
        overlap_right.append(window)
        overlap_left.append(window * (gain[0, x : x + 1, :] * (1.0 / FOOTPRINT_CELLS**2)))
    left_high, left_low = split(jnp.concatenate(overlap_left, axis=1))
    right = jnp.concatenate(overlap_right, axis=1)
    width = w_out.shape[2]
    blank = [jnp.zeros((64, right.shape[1]), F32)]
    spare = width - 64 - slots
    after = [jnp.zeros((spare, right.shape[1]), F32)] if spare else []
    right = jnp.concatenate(blank + [right] + after, axis=0).astype(BF16)
    nt = (((1,), (1,)), ((), ()))
    overlap = lax.dot_general(left_high, right, nt, preferred_element_type=F32)
    overlap = overlap + lax.dot_general(left_low, right, nt, preferred_element_type=F32)

    stiff_high, stiff_low = split(load(stiff_ref).reshape(kinds * freedoms, freedoms))
    table[:, :freedoms] = stiff_high
    table[:, freedoms:] = stiff_low
    coasting = 2.0 * q - load(q_prev_ref) - dt2 * stiff_term(q)
    fields = base
    columns = [couple_sum(c, coasting) for c in range(3)]
    pairs_of = ((0, 0), (0, 1), (0, 2), (1, 1), (1, 2), (2, 2))
    columns += [dt2 * couple_sum(c, coupling[d]) for c, d in pairs_of]
    places = (24, 25, 26, 27, 28, 29, 30, 31, 56)
    for place, column in zip(places, columns):
        fields = jnp.where(lane == place, column, fields)
    first = jnp.where(lane < 64, fields, overlap[:, :128])
    if width > 128:
        first = jnp.concatenate([first, overlap[:, 128:]], axis=1)
    w_out[...] = first.reshape(owners, capacity, width)
    w_in[h] = w_out[h]
    for step in range(2, owners):

        @pl.when(h + step < owners)
        def _(step=step):
            pl.semaphore_wait(entered.at[step], 1)
            b_copy(0, step).start()

    send_buildings(1)

    u_old = load(u_prev_ref)

    shape = (3, nz, 8, 128)

    def push(turn, field, lam_mu):
        count = (5 if turn == 0 else 3) * nz
        rim_x, rim_y, corner = take_rims(turn, count)
        if turn == 0:
            lam_mu = rim_x[3 * nz :], rim_y[3 * nz :]
        lam_mu_x, lam_mu_y = lam_mu
        total = divergence(
            field,
            rim_x[: 3 * nz].reshape(shape),
            rim_y[: 3 * nz].reshape(shape),
            corner.reshape(shape),
            lam,
            mu,
            lam_mu_x[:nz],
            lam_mu_x[nz:],
            lam_mu_y[:nz],
            lam_mu_y[nz:],
        )
        return total, lam_mu

    def on_surface(field, force):
        return jnp.concatenate([field[:, :1] + (gain[0] * force)[:, None], field[:, 1:]], axis=1)

    picked = (2 * a_width, 128)
    place, column = iota(picked, 0), iota(picked, 1)
    word = 16 * h + 4 * ((column & 31) // 8)
    word = jnp.where(column < 32, word, word + a_width)
    chosen = ((place == word) & (column < 64) & ((column & 31) < 24)).astype(F32).astype(BF16)

    wait_rims(0)
    total, lam_mu = push(0, u, None)
    free = 2.0 * u - u_old + gain * total
    motion = surface_motion(free).reshape(owners, 2, 8, 128)
    p_out[...] = jnp.where(
        iota((owners, 8, 128), 2) < 64, motion[:, 0], pltpu.roll(motion[:, 1], 64, 2)
    )
    p_in[h] = p_out[h]
    send_buildings(2)

    shears = take_buildings(0)
    shears_high, shears_low = split(shears)
    pull = jnp.dot(
        jnp.concatenate([shears_high, shears_low], axis=1), chosen, preferred_element_type=F32
    )
    u_new = on_surface(free, surface_force(pull * weight))
    u, u_old = u_new, u
    put_rims(1, u.reshape(3 * nz, 8, 128))
    send_rims(1)
    u_before_ref[...] = u

    words = take_buildings(1)
    low_words = words[:, :128]
    drive = drive_of([group_sum(c, low_words) for c in range(3)])
    q, q_old = coasting + dt2 * drive, q
    q_before_ref[...] = q
    stiff = stiff_term(q)

    gram = {}
    for place, pair in zip(places[3:], pairs_of):
        gram[pair] = gram[pair[::-1]] = low_words[:, place : place + 1]
    later = []
    for c in range(3):
        value = low_words[:, 24 + c : 25 + c]
        for d in range(3):
            value = value + gram[c, d] * home_base[d]
        later.append(value)
    later = jnp.where(part < 8, later[0], jnp.where(part < 16, later[1], later[2]))
    force = surface_force(halves(later * weight))

    left_high, left_low = split(words)
    blank = [jnp.zeros((64, shears.shape[1]), F32)]
    after = [jnp.zeros((spare, shears.shape[1]), F32)] if spare else []
    right = jnp.concatenate(blank + [shears] + after, axis=0)
    right_high, right_low = split(right)
    moved = jnp.dot(left_high, right_high, preferred_element_type=F32)
    moved = moved + jnp.dot(left_low, right_high, preferred_element_type=F32)
    moved = moved + jnp.dot(left_high, right_low, preferred_element_type=F32)
    moved_lane = iota(moved.shape, 1)
    moved_row = iota(moved.shape, 0) // capacity * 16
    moved = [
        jnp.sum(jnp.where(moved_lane == moved_row + 4 * c, moved, 0.0), axis=1, keepdims=True)
        for c in range(3)
    ]
    q_free = 2.0 * q - q_old + dt2 * (drive_of(moved) - stiff)
    u_free = on_surface(2.0 * u - u_old, force)

    wait_rims(1)
    total, _ = push(1, u, lam_mu)
    u_last_ref[...] = u_free + gain * total

    motion = take_buildings(2)
    q_last_ref[...] = q_free + dt2 * drive_of([group_sum(c, motion) for c in range(3)])
    wait_sends()


def shards(
    rows,
    owners,
    u_now,
    u_prev,
    lame_lambda,
    lame_mu,
    buoyancy,
    q_now,
    q_prev,
    archetype,
    stiffness,
    couple,
    counts,
    footprint,
):
    nz = lame_mu.shape[0]
    slots, freedoms = q_now.shape
    capacity = slots // owners
    kinds = stiffness.shape[0]
    pairs = (5 * nz) // 2, (3 * nz) // 2
    a_width = -(-32 * owners // 128) * 128
    w_width = -(-(64 + slots) // 128) * 128
    vmem = pl.BlockSpec(memory_space=pltpu.VMEM)
    hbm = pl.BlockSpec(memory_space=pltpu.HBM)
    dma = pltpu.SemaphoreType.DMA
    operands = (
        u_now,
        u_prev,
        lame_lambda,
        lame_mu,
        buoyancy,
        q_now,
        q_prev,
        archetype.reshape(1, slots),
        stiffness,
        couple.transpose(1, 0, 2),
        counts,
        footprint,
    )
    results = (
        jax.ShapeDtypeStruct(u_now.shape, F32),
        jax.ShapeDtypeStruct(u_now.shape, F32),
        jax.ShapeDtypeStruct(q_now.shape, F32),
        jax.ShapeDtypeStruct(q_now.shape, F32),
    )
    held = pl.pallas_call(
        functools.partial(kernel, rows, owners),
        out_shape=tuple(pltpu.VMEM(result.shape, result.dtype) for result in results),
        in_specs=[hbm] * len(operands),
        out_specs=(vmem,) * 4,
        scratch_shapes=[
            pltpu.VMEM((2, pairs[0], 8, 128), F32),
            pltpu.VMEM((2, pairs[1], 8, 128), F32),
            pltpu.VMEM((2, pairs[0], 8, 128), F32),
            pltpu.VMEM((2, pairs[1], 8, 128), F32),
            pltpu.VMEM((STEPS, 2, 8, 128), F32),
            pltpu.VMEM((STEPS, 2, 8, 128), F32),
            pltpu.VMEM((STEPS, 2, 8, 128), F32),
            pltpu.VMEM((8, a_width), F32),
            pltpu.VMEM((owners, 8, a_width), F32),
            pltpu.VMEM((owners, capacity, w_width), F32),
            pltpu.VMEM((owners, capacity, w_width), F32),
            pltpu.VMEM((owners, 8, 128), F32),
            pltpu.VMEM((owners, 8, 128), F32),
            pltpu.VMEM((kinds * freedoms, 2 * freedoms), BF16),
        ]
        + [pltpu.VMEM(operand.shape, operand.dtype) for operand in operands]
        + [
            dma((len(operands),)),
            dma((STEPS, 2)),
            dma((STEPS, 2)),
            dma((STEPS, len(Y_DIRS))),
            dma((STEPS, len(Y_DIRS))),
            dma((3, owners)),
            dma((3, owners)),
            pltpu.SemaphoreType.REGULAR((owners,)),
        ],
        compiler_params=pltpu.CompilerParams(
            collective_id=0, has_side_effects=True, vmem_limit_bytes=60 * 1024 * 1024
        ),
    )(*operands)
    return pl.pallas_call(
        store,
        out_shape=results,
        in_specs=[vmem] * 4,
        out_specs=(hbm,) * 4,
        scratch_shapes=[dma((4,))],
        compiler_params=pltpu.CompilerParams(vmem_limit_bytes=1024 * 1024),
    )(*held)


def store(*refs):
    copies = [
        pltpu.make_async_copy(refs[k], refs[4 + k], refs[8].at[k]) for k in range(4)
    ]
    for copy in copies:
        copy.start()
    for copy in copies:
        copy.wait()


def solution(mesh):
    return jax.shard_map(
        functools.partial(shards, mesh.shape["gx"], mesh.shape["gy"]),
        mesh=mesh,
        in_specs=(
            P(None, None, "gx", "gy"),
            P(None, None, "gx", "gy"),
            P(None, "gx", "gy"),
            P(None, "gx", "gy"),
            P(None, "gx", "gy"),
            P(("gx", "gy"), None),
            P(("gx", "gy"), None),
            P(("gx", "gy")),
            P(),
            P(),
            P("gx", None, None),
            P("gx", "gy", None),
        ),
        out_specs=(
            P(None, None, "gx", "gy"),
            P(None, None, "gx", "gy"),
            P(("gx", "gy"), None),
            P(("gx", "gy"), None),
        ),
        check_vma=False,
    )
```

```python
import functools

import jax
import jax.numpy as jnp
from jax import lax
from jax.experimental import pallas as pl
from jax.experimental.pallas import tpu as pltpu
from jax.sharding import PartitionSpec as P

FOOTPRINT_CELLS = 4
STEPS = 2
TIME_STEP = 0.25
RIM = 4
MESH = pl.DeviceIdType.MESH
F32 = jnp.float32
BF16 = jnp.bfloat16

X_DIRS = ((1, 0), (-1, 0))
Y_DIRS = ((-1, 1), (-1, -1), (0, 1), (0, -1), (1, 1), (1, -1))


def iota(shape, dim):
    return lax.broadcasted_iota(jnp.int32, shape, dim)


def split(value):
    high = value.astype(BF16)
    return high, (value - high.astype(F32)).astype(BF16)


def pack_x(fields):
    half = fields.shape[0] // 2
    first, second = fields[:half], fields[half:]
    upper = iota((1, 8, 128), 1) < RIM
    to_next = jnp.where(upper, pltpu.roll(first, RIM, 1), second)
    to_before = jnp.where(upper, first, pltpu.roll(second, RIM, 1))
    return to_next, to_before


def unpack_x(from_before, from_next):
    upper = iota((1, 8, 128), 1) < RIM
    first = jnp.where(upper, from_next, pltpu.roll(from_before, RIM, 1))
    second = jnp.where(upper, pltpu.roll(from_next, RIM, 1), from_before)
    return jnp.concatenate([first, second], axis=0)


def pack_y(fields):
    lane = iota((8, 128), 1)
    ahead, behind = jnp.zeros((8, 128), F32), jnp.zeros((8, 128), F32)
    for k in range(fields.shape[0]):
        place = RIM * k
        moved = pltpu.roll(fields[k], (place + RIM) % 128, 1)
        ahead = jnp.where((lane >= place) & (lane < place + RIM), moved, ahead)
        behind = jnp.where((lane >= place + RIM) & (lane < place + 2 * RIM), moved, behind)
    return ahead, behind


def unpack_y(ahead, behind, count):
    odd = (iota((8, 128), 1) & RIM) != 0
    tiles = jnp.where(odd, behind, ahead), jnp.where(odd, ahead, behind)
    slabs = []
    for k in range(count):
        slabs.append(pltpu.roll(tiles[k % 2], (124 - RIM * k) % 128, 1))
    return jnp.stack(slabs)


def slope(here, other, axis, both):
    size = here.shape[axis]
    place = iota((1,) * (here.ndim - 2) + (8, 128), axis)

    def shifted(mine, theirs, shift):
        entering = place < shift if shift > 0 else place >= size + shift
        return pltpu.roll(jnp.where(entering, theirs, mine), (-shift) % size, axis)

    def slope_of(mine, theirs):
        return 8.0 * (shifted(mine, theirs, 1) - shifted(mine, theirs, -1)) - (
            shifted(mine, theirs, 2) - shifted(mine, theirs, -2)
        )

    if both:
        return slope_of(here, other), slope_of(other, here)
    return slope_of(here, other)


def slope_z(field):
    nothing = jnp.zeros((2,) + field.shape[1:], F32)
    padded = jnp.concatenate([nothing, field, nothing], axis=0)
    n = field.shape[0]
    return 8.0 * (padded[3 : n + 3] - padded[1 : n + 1]) - (padded[4 : n + 4] - padded[:n])


def divergence(u, rim_x, rim_y, corner, lam, mu, lam_x, mu_x, lam_y, mu_y):
    ux, uy, uz = u[0], u[1], u[2]
    x_x, x_xh = slope(ux, rim_x[0], 1, True)
    y_x, y_xh = slope(uy, rim_x[1], 1, True)
    z_x, z_xh = slope(uz, rim_x[2], 1, True)
    x_y, x_yh = slope(ux, rim_y[0], 2, True)
    y_y, y_yh = slope(uy, rim_y[1], 2, True)
    z_y, z_yh = slope(uz, rim_y[2], 2, True)
    x_z, y_z, z_z = slope_z(ux), slope_z(uy), slope_z(uz)
    spread = lam * (x_x + y_y + z_z)
    s_xx = spread + 2.0 * mu * x_x
    s_yy = spread + 2.0 * mu * y_y
    s_zz = spread + 2.0 * mu * z_z
    s_xy = mu * (x_y + y_x)
    s_xz = mu * (x_z + z_x)
    s_yz = mu * (y_z + z_y)
    x_yr = slope(rim_x[0], corner[0], 2, False)
    y_yr = slope(rim_x[1], corner[1], 2, False)
    x_zr, z_zr = slope_z(rim_x[0]), slope_z(rim_x[2])
    s_xx_r = lam_x * (x_xh + y_yr + z_zr) + 2.0 * mu_x * x_xh
    s_xy_r = mu_x * (x_yr + y_xh)
    s_xz_r = mu_x * (x_zr + z_xh)
    x_xc = slope(rim_y[0], corner[0], 1, False)
    y_xc = slope(rim_y[1], corner[1], 1, False)
    y_zc, z_zc = slope_z(rim_y[1]), slope_z(rim_y[2])
    s_yy_c = lam_y * (x_xc + y_yh + z_zc) + 2.0 * mu_y * y_yh
    s_xy_c = mu_y * (x_yh + y_xc)
    s_yz_c = mu_y * (y_zc + z_yh)
    total_x = slope(s_xx, s_xx_r, 1, False) + slope(s_xy, s_xy_c, 2, False) + slope_z(s_xz)
    total_y = slope(s_xy, s_xy_r, 1, False) + slope(s_yy, s_yy_c, 2, False) + slope_z(s_yz)
    total_z = slope(s_xz, s_xz_r, 1, False) + slope(s_yz, s_yz_c, 2, False) + slope_z(s_zz)
    return jnp.stack([total_x, total_y, total_z])


def kernel(
    rows,
    owners,
    u_hbm,
    u_prev_hbm,
    lam_hbm,
    mu_hbm,
    buoy_hbm,
    q_hbm,
    q_prev_hbm,
    arch_hbm,
    stiff_hbm,
    couple_hbm,
    counts_hbm,
    cells_hbm,
    u_last_ref,
    u_before_ref,
    q_last_ref,
    q_before_ref,
    xs0,
    xs1,
    xr0,
    xr1,
    ys,
    yr,
    cr,
    a_out,
    a_in,
    w_out,
    w_in,
    p_out,
    p_in,
    table,
    frame_ref,
    near_ref,
    wide_ref,
    far_ref,
    arch_ref,
    counts_ref,
    cells_ref,
    loaded,
    sent,
    arrived,
    entered,
):
    r, h = lax.axis_index("gx"), lax.axis_index("gy")
    nz = lam_hbm.shape[0]
    slots, freedoms = q_hbm.shape
    capacity = slots // owners
    kinds = couple_hbm.shape[0] // 3
    dt2 = TIME_STEP * TIME_STEP
    xs, xr = (xs0, xs1), (xr0, xr1)

    def target(direction):
        dx, dy = direction
        there = None
        for d, me, n in ((dx, r, rows), (dy, h, owners)):
            if d:
                ok = me + d < n if d > 0 else me > 0
                there = ok if there is None else there & ok
        return there, (r + dx, h + dy)

    def source(direction):
        return target((-direction[0], -direction[1]))

    loads = {}

    def start_load(name, ref, parts):
        sem = loaded.at[len(loads)]
        start, places = 0, {}
        for part, source_ref in parts:
            size = source_ref.shape[0]
            into = ref if len(parts) == 1 else ref.at[pl.ds(start, size)]
            pltpu.make_async_copy(source_ref, into, sem).start()
            places[part] = into
            start += size
        loads[name] = [pltpu.make_async_copy(ref, ref, sem)], places

    start_load("frame", frame_ref, (("q", q_hbm), ("couple", couple_hbm)))
    start_load("arch", arch_ref, (("arch", arch_hbm),))
    start_load("near", near_ref, (("u", u_hbm), ("lam", lam_hbm), ("mu", mu_hbm)))
    peers = X_DIRS + tuple(d for d in Y_DIRS if d[0])

    barrier = pltpu.get_barrier_semaphore()
    arrivals = h + (h + 1 < owners).astype(jnp.int32)
    for step in range(1, owners):
        other = lax.rem(h + step, owners)

        @pl.when((h + step < owners) | (step == owners - 1))
        def _(other=other):
            pl.semaphore_signal(barrier, inc=1, device_id=(r, other), device_id_type=MESH)

    for direction in peers:
        there, device = target(direction)
        arrivals = arrivals + there.astype(jnp.int32)

        @pl.when(there)
        def _(device=device):
            pl.semaphore_signal(barrier, inc=1, device_id=device, device_id_type=MESH)

    start_load("cells", cells_ref, (("cells", cells_hbm),))
    start_load("counts", counts_ref, (("counts", counts_hbm),))
    start_load("far", far_ref, (("u_prev", u_prev_hbm), ("buoy", buoy_hbm)))
    start_load("wide", wide_ref, (("stiff", stiff_hbm), ("q_prev", q_prev_hbm)))

    def half(ref, dx):
        return ref if dx == 0 else ref.at[pl.ds(RIM if dx > 0 else 0, RIM)]

    def y_place(turn, direction):
        dx, dy = direction
        k = 0 if dy > 0 else 1
        return half((cr if dx else yr).at[turn, k], dx)

    for slot, direction in enumerate(X_DIRS):
        there, _ = source(direction)

        @pl.when(jnp.logical_not(there))
        def _(slot=slot):
            for buffer in xr:
                buffer[slot] = jnp.zeros(buffer.shape[1:], F32)

    for slot, direction in enumerate(Y_DIRS):
        there, _ = source(direction)

        @pl.when(jnp.logical_not(there))
        def _(direction=direction):
            for turn in range(STEPS):
                ref = y_place(turn, direction)
                ref[...] = jnp.zeros(ref.shape, F32)

    def load(part):
        for copies, places in loads.values():
            if part in places:
                while copies:
                    copies.pop().wait()
                return places[part]

    def wait_rows(sem, count):
        rows_of = wide_ref.at[pl.ds(0, count)]
        pltpu.make_async_copy(rows_of, rows_of, sem).wait()

    def wait_rows_of_rims(sem, turns):
        for nx in (1, 2):
            for ny in (1, 2):
                count = 0
                for turn in turns:
                    count += nx * xs[turn].shape[1] * 8 + ny * 8 + nx * ny * RIM
                sides = [target(d)[0].astype(jnp.int32) for d in X_DIRS + ((0, 1), (0, -1))]

                @pl.when((sides[0] + sides[1] == nx) & (sides[2] + sides[3] == ny))
                def _(count=count):
                    wait_rows(sem, count)

    def x_copy(turn, slot, device):
        return pltpu.make_async_remote_copy(
            src_ref=xs[turn].at[slot],
            dst_ref=xr[turn].at[slot],
            send_sem=sent.at[0],
            recv_sem=arrived.at[turn],
            device_id=device,
            device_id_type=MESH,
        )

    def y_copy(turn, slot, device):
        return pltpu.make_async_remote_copy(
            src_ref=half(ys.at[turn, 0 if Y_DIRS[slot][1] > 0 else 1], Y_DIRS[slot][0]),
            dst_ref=y_place(turn, Y_DIRS[slot]),
            send_sem=sent.at[0],
            recv_sem=arrived.at[turn],
            device_id=device,
            device_id_type=MESH,
        )

    messages = ((a_out, a_in), (w_out, w_in), (p_out, p_in))

    def b_copy(which, step):
        other = lax.rem(h + step, owners)
        out, into = messages[which]
        return pltpu.make_async_remote_copy(
            src_ref=out if which == 0 else out.at[other],
            dst_ref=into.at[h],
            send_sem=sent.at[1],
            recv_sem=arrived.at[STEPS + which],
            device_id=(r, other),
            device_id_type=MESH,
        )

    def send_rims(turn):
        for copy, dirs in ((x_copy, X_DIRS), (y_copy, Y_DIRS)):
            for slot, direction in enumerate(dirs):
                there, device = target(direction)

                @pl.when(there)
                def _(copy=copy, slot=slot, device=device):
                    copy(turn, slot, device).start()

    def wait_rims(turn):
        wait_rows_of_rims(arrived.at[turn], (turn,))

    def wait_sends():
        wait_rows_of_rims(sent.at[0], range(STEPS))
        size = 0
        for out, into in messages:
            size += into.shape[1] * into.shape[2] // 128
        wait_rows(sent.at[1], (owners - 1) * size)

    def put_rims(turn, fields):
        to_next, to_before = pack_x(fields)
        xs[turn][0] = to_next
        xs[turn][1] = to_before
        ys[turn, 0], ys[turn, 1] = pack_y(fields)

    def take_rims(turn, count):
        rim_x = unpack_x(xr[turn][0], xr[turn][1])
        rim_y = unpack_y(yr[turn, 0], yr[turn, 1], count)
        return rim_x, rim_y, unpack_y(cr[turn, 0], cr[turn, 1], 3 * nz)

    def send_buildings(which):
        for step in range(owners // 2, 0, -1):
            b_copy(which, step).start()
            if owners - step != step:
                b_copy(which, owners - step).start()

    def take_buildings(which):
        into = messages[which][1]
        others = into.at[pl.ds(0, owners - 1)]
        pltpu.make_async_copy(others, others, arrived.at[STEPS + which]).wait()
        into = into[...]
        if into.shape[1] < capacity:
            into = jnp.concatenate([into, pltpu.roll(into, into.shape[2] // 2, 2)], axis=1)
        return into.reshape(slots, into.shape[2])

    lane = iota((slots, 128), 1)
    part = lane & 31
    slot_row = iota((slots, 1), 0)
    square = (slots, slots)

    couple = load("couple")[...].reshape(3, kinds, freedoms)
    arch = jnp.sum(
        jnp.where(iota(square, 0) == iota(square, 1), load("arch")[...].astype(F32), 0.0),
        axis=1,
        keepdims=True,
    )
    is_kind = [arch == float(a) for a in range(kinds)]
    coupling = []
    for c in range(3):
        chosen = jnp.zeros((slots, freedoms), F32)
        for a in range(kinds):
            chosen = jnp.where(is_kind[a], couple[c, a : a + 1, :], chosen)
        coupling.append(chosen)

    def couple_sum(c, state):
        return jnp.sum(coupling[c] * state, axis=1, keepdims=True)

    q = load("q")[...]
    shear = [couple_sum(c, q) for c in range(3)]
    word = lane & 15
    shear = jnp.where(word < 4, shear[0], jnp.where(word < 8, shear[1], shear[2]))
    shear = shear.reshape(owners, 2, 8, 128)
    group = iota((8, 128), 1) // 16
    a_width = a_out.shape[1]
    for t in range(a_width // 128):
        tile = jnp.zeros((8, 128), F32)
        for k in range(8):
            which, home = divmod(8 * t + k, a_width // 32)
            if home < owners:
                tile = jnp.where(group == k, shear[home, which], tile)
        a_out[:, 128 * t : 128 * (t + 1)] = tile
    a_in[h] = a_out[...]

    u = load("u")[...].reshape(3, nz, 8, 128)
    lam, mu = load("lam")[...] * (1.0 / 144.0), load("mu")[...] * (1.0 / 144.0)
    put_rims(0, jnp.concatenate([u.reshape(3 * nz, 8, 128), lam, mu], axis=0))
    pl.semaphore_wait(barrier, arrivals)
    for step in range(1, owners - 1):
        other = lax.rem(h + step, owners)

        @pl.when(h + step >= owners)
        def _(step=step, other=other):
            pl.semaphore_signal(
                entered.at[owners - step - 2], inc=1, device_id=(r, other), device_id_type=MESH
            )

    for step in range(1, owners):

        @pl.when((h + step >= owners) | (step == 1))
        def _(step=step):
            b_copy(0, step).start()

    send_rims(0)

    cells = load("cells")[0].astype(F32)
    wide = (slots, slots * FOOTPRINT_CELLS)
    own = (iota(wide, 1) // FOOTPRINT_CELLS) == iota(wide, 0)
    corner_cell = jnp.min(jnp.where(own, cells, 1e9), axis=1, keepdims=True)
    corner_x = jnp.floor(corner_cell * (1.0 / 128.0))
    corner_y = corner_cell - 128.0 * corner_x
    along_y = lane.astype(F32) - corner_y
    in_y = ((along_y == 0.0) | (along_y == 1.0)).astype(F32)
    window_y = in_y.astype(BF16)
    along_x = (lane & 7).astype(F32) - corner_x
    row_counts = load("counts")[0, pl.ds(h, 1), :].astype(F32)
    pairs = (slots, owners)
    live_count = jnp.sum(
        jnp.where(iota(pairs, 0) // capacity == iota(pairs, 1), row_counts, 0.0),
        axis=1,
        keepdims=True,
    )
    live = (slot_row % capacity).astype(F32) < live_count
    weight = jnp.where(
        live & ((along_x == 0.0) | (along_x == 1.0)) & (part < 24), 1.0 / FOOTPRINT_CELLS, 0.0
    )
    base_weight = jnp.where(lane < 64, weight, 0.0)
    mine = [(lane < 64) & (part >= 8 * c) & (part < 8 * c + 8) for c in range(3)]

    def group_sum(c, value):
        return jnp.sum(jnp.where(mine[c], value, 0.0), axis=1, keepdims=True)

    def surface_motion(field):
        surface = field[:, 0]
        high = surface.astype(BF16).astype(F32)
        nothing = jnp.zeros((8, 128), F32)
        stacked = jnp.concatenate(
            [high.reshape(24, 128), nothing, (surface - high).reshape(24, 128), nothing]
            + [nothing] * 8,
            axis=0,
        ).astype(BF16)
        gathered = lax.dot_general(
            window_y, stacked, (((1,), (1,)), ((), ())), preferred_element_type=F32
        )
        return gathered * base_weight

    def halves(pull):
        high = pull.astype(BF16).astype(F32)
        return jnp.where((lane & 32) == 0, high, pull - high)

    def surface_force(pull):
        spread = lax.dot_general(
            pull.T.astype(BF16), window_y, (((1,), (0,)), ((), ())), preferred_element_type=F32
        )
        return (spread[0:24] + spread[32:56]).reshape(3, 8, 128)

    def drive_of(base):
        drive = coupling[0] * base[0]
        for c in range(1, 3):
            drive = drive + coupling[c] * base[c]
        return drive

    def stiff_term(state):
        high, low = split(state)
        stacked = jnp.concatenate([high.astype(F32), low.astype(F32)], axis=0)
        twice = jnp.concatenate([arch, arch], axis=0)
        spread = jnp.concatenate(
            [jnp.where(twice == float(a), stacked, 0.0).astype(BF16) for a in range(kinds)],
            axis=1,
        )
        product = jnp.dot(spread, table[...], preferred_element_type=F32)
        product = product[:, :freedoms] + product[:, freedoms:]
        return product[:slots] + product[slots:]

    base = surface_motion(u)
    home_base = [group_sum(c, base) for c in range(3)]

    gain = load("buoy")[...] * dt2
    overlap_left, overlap_right = [], []
    for x in range(8):
        there = live & ((corner_x == float(x)) | (corner_x == float(x - 1)))
        window = jnp.where(there, in_y, 0.0)
        overlap_right.append(window)
        overlap_left.append(window * (gain[0, x : x + 1, :] * (1.0 / FOOTPRINT_CELLS**2)))
    left_high, left_low = split(jnp.concatenate(overlap_left, axis=1))
    right = jnp.concatenate(overlap_right, axis=1)
    width = w_out.shape[2]
    blank = [jnp.zeros((64, right.shape[1]), F32)]
    spare = width - 64 - slots
    after = [jnp.zeros((spare, right.shape[1]), F32)] if spare else []
    right = jnp.concatenate(blank + [right] + after, axis=0).astype(BF16)
    nt = (((1,), (1,)), ((), ()))
    overlap = lax.dot_general(left_high, right, nt, preferred_element_type=F32)
    overlap = overlap + lax.dot_general(left_low, right, nt, preferred_element_type=F32)

    stiff_high, stiff_low = split(load("stiff")[...])
    table[:, :freedoms] = stiff_high
    table[:, freedoms:] = stiff_low
    coasting = 2.0 * q - load("q_prev")[...] - dt2 * stiff_term(q)
    fields = base
    columns = [couple_sum(c, coasting) for c in range(3)]
    pairs_of = ((0, 0), (0, 1), (0, 2), (1, 1), (1, 2), (2, 2))
    columns += [dt2 * couple_sum(c, coupling[d]) for c, d in pairs_of]
    places = (24, 25, 26, 27, 28, 29, 30, 31, 56)
    for place, column in zip(places, columns):
        fields = jnp.where(lane == place, column, fields)
    first = jnp.where(lane < 64, fields, overlap[:, :128])
    if width > 128:
        first = jnp.concatenate([first, overlap[:, 128:]], axis=1)
    w_out[...] = first.reshape(owners, capacity, width)
    w_in[h] = w_out[h]
    for step in range(2, owners):

        @pl.when(h + step < owners)
        def _(step=step):
            pl.semaphore_wait(entered.at[step - 2], 1)
            b_copy(0, step).start()

    send_buildings(1)

    u_old = load("u_prev")[...].reshape(3, nz, 8, 128)

    shape = (3, nz, 8, 128)

    def push(turn, field, lam_mu):
        count = (5 if turn == 0 else 3) * nz
        rim_x, rim_y, corner = take_rims(turn, count)
        if turn == 0:
            lam_mu = rim_x[3 * nz :], rim_y[3 * nz :]
        lam_mu_x, lam_mu_y = lam_mu
        total = divergence(
            field,
            rim_x[: 3 * nz].reshape(shape),
            rim_y[: 3 * nz].reshape(shape),
            corner.reshape(shape),
            lam,
            mu,
            lam_mu_x[:nz],
            lam_mu_x[nz:],
            lam_mu_y[:nz],
            lam_mu_y[nz:],
        )
        return total, lam_mu

    def on_surface(field, force):
        return jnp.concatenate([field[:, :1] + (gain[0] * force)[:, None], field[:, 1:]], axis=1)

    picked = (2 * a_width, 128)
    place, column = iota(picked, 0), iota(picked, 1)
    word = 16 * h + 4 * ((column & 31) // 8)
    word = jnp.where(column < 32, word, word + a_width)
    chosen = ((place == word) & (column < 64) & ((column & 31) < 24)).astype(F32).astype(BF16)

    wait_rims(0)
    total, lam_mu = push(0, u, None)
    free = 2.0 * u - u_old + gain * total
    motion = surface_motion(free).reshape(owners, 2, 8, 128)
    p_out[...] = jnp.where(
        iota((owners, 8, 128), 2) < 64, motion[:, 0], pltpu.roll(motion[:, 1], 64, 2)
    )
    p_in[h] = p_out[h]
    send_buildings(2)

    shears = take_buildings(0)
    shears_high, shears_low = split(shears)
    pull = jnp.dot(
        jnp.concatenate([shears_high, shears_low], axis=1), chosen, preferred_element_type=F32
    )
    u_new = on_surface(free, surface_force(pull * weight))
    u, u_old = u_new, u
    put_rims(1, u.reshape(3 * nz, 8, 128))
    send_rims(1)
    u_before_ref[...] = u

    words = take_buildings(1)
    low_words = words[:, :128]
    drive = drive_of([group_sum(c, low_words) for c in range(3)])
    q, q_old = coasting + dt2 * drive, q
    q_before_ref[...] = q
    stiff = stiff_term(q)

    gram = {}
    for place, pair in zip(places[3:], pairs_of):
        gram[pair] = gram[pair[::-1]] = low_words[:, place : place + 1]
    later = []
    for c in range(3):
        value = low_words[:, 24 + c : 25 + c]
        for d in range(3):
            value = value + gram[c, d] * home_base[d]
        later.append(value)
    later = jnp.where(part < 8, later[0], jnp.where(part < 16, later[1], later[2]))
    force = surface_force(halves(later * weight))

    left_high, left_low = split(words)
    blank = [jnp.zeros((64, shears.shape[1]), F32)]
    after = [jnp.zeros((spare, shears.shape[1]), F32)] if spare else []
    right = jnp.concatenate(blank + [shears] + after, axis=0)
    right_high, right_low = split(right)
    moved = jnp.dot(left_high, right_high, preferred_element_type=F32)
    moved = moved + jnp.dot(left_low, right_high, preferred_element_type=F32)
    moved = moved + jnp.dot(left_high, right_low, preferred_element_type=F32)
    moved_lane = iota(moved.shape, 1)
    moved_row = iota(moved.shape, 0) // capacity * 16
    moved = [
        jnp.sum(jnp.where(moved_lane == moved_row + 4 * c, moved, 0.0), axis=1, keepdims=True)
        for c in range(3)
    ]
    q_free = 2.0 * q - q_old + dt2 * (drive_of(moved) - stiff)
    u_free = on_surface(2.0 * u - u_old, force)

    wait_rims(1)
    total, _ = push(1, u, lam_mu)
    u_last_ref[...] = u_free + gain * total

    motion = take_buildings(2)
    q_last_ref[...] = q_free + dt2 * drive_of([group_sum(c, motion) for c in range(3)])
    wait_sends()


def shards(
    rows,
    owners,
    u_now,
    u_prev,
    lame_lambda,
    lame_mu,
    buoyancy,
    q_now,
    q_prev,
    archetype,
    stiffness,
    couple,
    counts,
    footprint,
):
    nz = lame_mu.shape[0]
    slots, freedoms = q_now.shape
    capacity = slots // owners
    kinds = stiffness.shape[0]
    pairs = (5 * nz) // 2, (3 * nz) // 2
    a_width = -(-32 * owners // 128) * 128
    w_width = -(-(64 + slots) // 128) * 128
    vmem = pl.BlockSpec(memory_space=pltpu.VMEM)
    hbm = pl.BlockSpec(memory_space=pltpu.HBM)
    dma = pltpu.SemaphoreType.DMA
    tiles = (3 * nz, 8, 128)
    operands = (
        u_now.reshape(tiles),
        u_prev.reshape(tiles),
        lame_lambda,
        lame_mu,
        buoyancy,
        q_now,
        q_prev,
        archetype.reshape(1, slots),
        stiffness.reshape(kinds * freedoms, freedoms),
        couple.transpose(1, 0, 2).reshape(3 * kinds, freedoms),
        counts,
        footprint,
    )
    results = (
        jax.ShapeDtypeStruct(u_now.shape, F32),
        jax.ShapeDtypeStruct(u_now.shape, F32),
        jax.ShapeDtypeStruct(q_now.shape, F32),
        jax.ShapeDtypeStruct(q_now.shape, F32),
    )
    held = pl.pallas_call(
        functools.partial(kernel, rows, owners),
        out_shape=tuple(pltpu.VMEM(result.shape, result.dtype) for result in results),
        in_specs=[hbm] * len(operands),
        out_specs=(vmem,) * 4,
        scratch_shapes=[
            pltpu.VMEM((2, pairs[0], 8, 128), F32),
            pltpu.VMEM((2, pairs[1], 8, 128), F32),
            pltpu.VMEM((2, pairs[0], 8, 128), F32),
            pltpu.VMEM((2, pairs[1], 8, 128), F32),
            pltpu.VMEM((STEPS, 2, 8, 128), F32),
            pltpu.VMEM((STEPS, 2, 8, 128), F32),
            pltpu.VMEM((STEPS, 2, 8, 128), F32),
            pltpu.VMEM((8, a_width), F32),
            pltpu.VMEM((owners, 8, a_width), F32),
            pltpu.VMEM((owners, capacity, w_width), F32),
            pltpu.VMEM((owners, capacity, w_width), F32),
            pltpu.VMEM((owners, 8, 128), F32),
            pltpu.VMEM((owners, 8, 128), F32),
            pltpu.VMEM((kinds * freedoms, 2 * freedoms), BF16),
        ]
        + [
            pltpu.VMEM((slots + 3 * kinds, freedoms), F32),
            pltpu.VMEM((5 * nz, 8, 128), F32),
            pltpu.VMEM((kinds * freedoms + slots, freedoms), F32),
            pltpu.VMEM((4 * nz, 8, 128), F32),
            pltpu.VMEM((1, slots), jnp.int32),
            pltpu.VMEM(counts.shape, jnp.int32),
            pltpu.VMEM(footprint.shape, jnp.int32),
            dma((7,)),
            dma((2,)),
            dma((STEPS + 3,)),
            pltpu.SemaphoreType.REGULAR((owners - 2,)),
        ],
        compiler_params=pltpu.CompilerParams(
            collective_id=0, has_side_effects=True, vmem_limit_bytes=60 * 1024 * 1024
        ),
    )(*operands)
    return pl.pallas_call(
        store,
        out_shape=results,
        in_specs=[vmem] * 4,
        out_specs=(hbm,) * 4,
        scratch_shapes=[dma((4,))],
        compiler_params=pltpu.CompilerParams(vmem_limit_bytes=1024 * 1024),
    )(*held)


def store(*refs):
    copies = [
        pltpu.make_async_copy(refs[k], refs[4 + k], refs[8].at[k]) for k in range(4)
    ]
    for copy in copies:
        copy.start()
    for copy in copies:
        copy.wait()


def solution(mesh):
    return jax.shard_map(
        functools.partial(shards, mesh.shape["gx"], mesh.shape["gy"]),
        mesh=mesh,
        in_specs=(
            P(None, None, "gx", "gy"),
            P(None, None, "gx", "gy"),
            P(None, "gx", "gy"),
            P(None, "gx", "gy"),
            P(None, "gx", "gy"),
            P(("gx", "gy"), None),
            P(("gx", "gy"), None),
            P(("gx", "gy")),
            P(),
            P(),
            P("gx", None, None),
            P("gx", "gy", None),
        ),
        out_specs=(
            P(None, None, "gx", "gy"),
            P(None, None, "gx", "gy"),
            P(("gx", "gy"), None),
            P(("gx", "gy"), None),
        ),
        check_vma=False,
    )
```

```python
import functools

import jax
import jax.numpy as jnp
from jax import lax
from jax.experimental import pallas as pl
from jax.experimental.pallas import tpu as pltpu
from jax.sharding import PartitionSpec as P

FOOTPRINT_CELLS = 4
STEPS = 2
TIME_STEP = 0.25
RIM = 4
MESH = pl.DeviceIdType.MESH
F32 = jnp.float32
BF16 = jnp.bfloat16

X_DIRS = ((1, 0), (-1, 0))
Y_DIRS = ((-1, 1), (-1, -1), (0, 1), (0, -1), (1, 1), (1, -1))
DIRS = X_DIRS + Y_DIRS
HEARD = tuple(d for d in DIRS if d[1] > 0 or d in X_DIRS)


def iota(shape, dim):
    return lax.broadcasted_iota(jnp.int32, shape, dim)


def split(value):
    high = value.astype(BF16)
    return high, (value - high.astype(F32)).astype(BF16)


def pack_x(fields):
    half = fields.shape[0] // 2
    first, second = fields[:half], fields[half:]
    upper = iota((1, 8, 128), 1) < RIM
    to_next = jnp.where(upper, pltpu.roll(first, RIM, 1), second)
    to_before = jnp.where(upper, first, pltpu.roll(second, RIM, 1))
    return to_next, to_before


def unpack_x(from_before, from_next):
    upper = iota((1, 8, 128), 1) < RIM
    first = jnp.where(upper, from_next, pltpu.roll(from_before, RIM, 1))
    second = jnp.where(upper, pltpu.roll(from_next, RIM, 1), from_before)
    return jnp.concatenate([first, second], axis=0)


def pack_y(fields):
    lane = iota((8, 128), 1)
    ahead, behind = jnp.zeros((8, 128), F32), jnp.zeros((8, 128), F32)
    for k in range(fields.shape[0]):
        place = RIM * k
        moved = pltpu.roll(fields[k], (place + RIM) % 128, 1)
        ahead = jnp.where((lane >= place) & (lane < place + RIM), moved, ahead)
        behind = jnp.where((lane >= place + RIM) & (lane < place + 2 * RIM), moved, behind)
    return ahead, behind


def unpack_y(ahead, behind, count):
    odd = (iota((8, 128), 1) & RIM) != 0
    tiles = jnp.where(odd, behind, ahead), jnp.where(odd, ahead, behind)
    slabs = []
    for k in range(count):
        slabs.append(pltpu.roll(tiles[k % 2], (124 - RIM * k) % 128, 1))
    return jnp.stack(slabs)


def slope(here, other, axis, both):
    size = here.shape[axis]
    place = iota((1,) * (here.ndim - 2) + (8, 128), axis)

    def shifted(mine, theirs, shift):
        entering = place < shift if shift > 0 else place >= size + shift
        return pltpu.roll(jnp.where(entering, theirs, mine), (-shift) % size, axis)

    def slope_of(mine, theirs):
        return 8.0 * (shifted(mine, theirs, 1) - shifted(mine, theirs, -1)) - (
            shifted(mine, theirs, 2) - shifted(mine, theirs, -2)
        )

    if both:
        return slope_of(here, other), slope_of(other, here)
    return slope_of(here, other)


def slope_z(field):
    nothing = jnp.zeros((2,) + field.shape[1:], F32)
    padded = jnp.concatenate([nothing, field, nothing], axis=0)
    n = field.shape[0]
    return 8.0 * (padded[3 : n + 3] - padded[1 : n + 1]) - (padded[4 : n + 4] - padded[:n])


def divergence(u, rim_x, rim_y, corner, lam, mu, lam_x, mu_x, lam_y, mu_y):
    ux, uy, uz = u[0], u[1], u[2]
    x_x, x_xh = slope(ux, rim_x[0], 1, True)
    y_x, y_xh = slope(uy, rim_x[1], 1, True)
    z_x, z_xh = slope(uz, rim_x[2], 1, True)
    x_y, x_yh = slope(ux, rim_y[0], 2, True)
    y_y, y_yh = slope(uy, rim_y[1], 2, True)
    z_y, z_yh = slope(uz, rim_y[2], 2, True)
    x_z, y_z, z_z = slope_z(ux), slope_z(uy), slope_z(uz)
    spread = lam * (x_x + y_y + z_z)
    s_xx = spread + 2.0 * mu * x_x
    s_yy = spread + 2.0 * mu * y_y
    s_zz = spread + 2.0 * mu * z_z
    s_xy = mu * (x_y + y_x)
    s_xz = mu * (x_z + z_x)
    s_yz = mu * (y_z + z_y)
    x_yr = slope(rim_x[0], corner[0], 2, False)
    y_yr = slope(rim_x[1], corner[1], 2, False)
    x_zr, z_zr = slope_z(rim_x[0]), slope_z(rim_x[2])
    s_xx_r = lam_x * (x_xh + y_yr + z_zr) + 2.0 * mu_x * x_xh
    s_xy_r = mu_x * (x_yr + y_xh)
    s_xz_r = mu_x * (x_zr + z_xh)
    x_xc = slope(rim_y[0], corner[0], 1, False)
    y_xc = slope(rim_y[1], corner[1], 1, False)
    y_zc, z_zc = slope_z(rim_y[1]), slope_z(rim_y[2])
    s_yy_c = lam_y * (x_xc + y_yh + z_zc) + 2.0 * mu_y * y_yh
    s_xy_c = mu_y * (x_yh + y_xc)
    s_yz_c = mu_y * (y_zc + z_yh)
    total_x = slope(s_xx, s_xx_r, 1, False) + slope(s_xy, s_xy_c, 2, False) + slope_z(s_xz)
    total_y = slope(s_xy, s_xy_r, 1, False) + slope(s_yy, s_yy_c, 2, False) + slope_z(s_yz)
    total_z = slope(s_xz, s_xz_r, 1, False) + slope(s_yz, s_yz_c, 2, False) + slope_z(s_zz)
    return jnp.stack([total_x, total_y, total_z])


def kernel(
    rows,
    owners,
    u_hbm,
    u_prev_hbm,
    lam_hbm,
    mu_hbm,
    buoy_hbm,
    q_hbm,
    q_prev_hbm,
    arch_hbm,
    stiff_hbm,
    couple_hbm,
    counts_hbm,
    cells_hbm,
    u_last_ref,
    u_before_ref,
    q_last_ref,
    q_before_ref,
    xs0,
    xs1,
    xr0,
    xr1,
    ys,
    yr,
    cr,
    a_out,
    a_in,
    w_out,
    w_in,
    p_out,
    p_in,
    table,
    frame_ref,
    near_ref,
    wide_ref,
    far_ref,
    arch_ref,
    counts_ref,
    cells_ref,
    loaded,
    sent,
    arrived,
    entered,
):
    r, h = lax.axis_index("gx"), lax.axis_index("gy")
    nz = lam_hbm.shape[0]
    slots, freedoms = q_hbm.shape
    capacity = slots // owners
    kinds = couple_hbm.shape[0] // 3
    dt2 = TIME_STEP * TIME_STEP
    xs, xr = (xs0, xs1), (xr0, xr1)

    def target(direction):
        dx, dy = direction
        there = None
        for d, me, n in ((dx, r, rows), (dy, h, owners)):
            if d:
                ok = me + d < n if d > 0 else me > 0
                there = ok if there is None else there & ok
        return there, (r + dx, h + dy)

    def source(direction):
        return target((-direction[0], -direction[1]))

    loads = {}

    def start_load(name, ref, parts):
        sem = loaded.at[len(loads)]
        start, places = 0, {}
        for part, source_ref in parts:
            size = source_ref.shape[0]
            into = ref if len(parts) == 1 else ref.at[pl.ds(start, size)]
            pltpu.make_async_copy(source_ref, into, sem).start()
            places[part] = into
            start += size
        loads[name] = [pltpu.make_async_copy(ref, ref, sem)], places

    start_load("frame", frame_ref, (("q", q_hbm), ("couple", couple_hbm)))
    start_load("arch", arch_ref, (("arch", arch_hbm),))
    start_load("near", near_ref, (("u", u_hbm), ("lam", lam_hbm), ("mu", mu_hbm)))
    odd = lax.rem(r, 2) == 1
    even = jnp.logical_not(odd)

    def later(direction):
        dx, dy = direction
        there = target(direction)[0]
        if dy == 0 or direction == (-1, 1):
            return there & odd
        return there if dy > 0 else None

    def earlier(direction):
        dx, dy = direction
        there = target(direction)[0]
        if dy == 0 or direction == (1, -1):
            return there & even
        return there if dy < 0 else None

    barrier = pltpu.get_barrier_semaphore()
    for direction in DIRS:
        if later(direction) is not None:

            @pl.when(later(direction))
            def _(device=target(direction)[1]):
                pl.semaphore_signal(barrier, inc=1, device_id=device, device_id_type=MESH)

    for step in range(2, owners):

        @pl.when(h + step < owners)
        def _(device=(r, h + step)):
            pl.semaphore_signal(barrier, inc=1, device_id=device, device_id_type=MESH)

    arrivals = jnp.maximum(h - 1, 0)
    for direction in DIRS:
        if earlier(direction) is not None:
            arrivals = arrivals + earlier(direction).astype(jnp.int32)

    start_load("cells", cells_ref, (("cells", cells_hbm),))
    start_load("counts", counts_ref, (("counts", counts_hbm),))
    start_load("far", far_ref, (("u_prev", u_prev_hbm), ("buoy", buoy_hbm)))
    start_load("wide", wide_ref, (("stiff", stiff_hbm), ("q_prev", q_prev_hbm)))

    def half(ref, dx):
        return ref if dx == 0 else ref.at[pl.ds(RIM if dx > 0 else 0, RIM)]

    def y_place(turn, direction):
        dx, dy = direction
        k = 0 if dy > 0 else 1
        return half((cr if dx else yr).at[turn, k], dx)

    for slot, direction in enumerate(X_DIRS):
        there, _ = source(direction)

        @pl.when(jnp.logical_not(there))
        def _(slot=slot):
            for buffer in xr:
                buffer[slot] = jnp.zeros(buffer.shape[1:], F32)

    for slot, direction in enumerate(Y_DIRS):
        there, _ = source(direction)

        @pl.when(jnp.logical_not(there))
        def _(direction=direction):
            for turn in range(STEPS):
                ref = y_place(turn, direction)
                ref[...] = jnp.zeros(ref.shape, F32)

    @pl.when(arrivals > 0)
    def _():
        pl.semaphore_wait(barrier, arrivals)

    def tell(direction, about):
        pl.semaphore_signal(
            entered.at[HEARD.index(about)],
            inc=1,
            device_id=target(direction)[1],
            device_id_type=MESH,
        )

    for direction in DIRS:
        if earlier(direction) is not None:

            @pl.when(earlier(direction))
            def _(direction=direction):
                tell(direction, (-direction[0], -direction[1]))

    for step in range(2, owners):

        @pl.when(h >= step)
        def _(step=step):
            pl.semaphore_signal(
                entered.at[len(HEARD) + step - 2],
                inc=1,
                device_id=(r, h - step),
                device_id_type=MESH,
            )

    def load(part):
        for copies, places in loads.values():
            if part in places:
                while copies:
                    copies.pop().wait()
                return places[part]

    def wait_rows(sem, count):
        rows_of = wide_ref.at[pl.ds(0, count)]
        pltpu.make_async_copy(rows_of, rows_of, sem).wait()

    def wait_rows_of_rims(sem, turns):
        for nx in (1, 2):
            for ny in (1, 2):
                count = 0
                for turn in turns:
                    count += nx * xs[turn].shape[1] * 8 + ny * 8 + nx * ny * RIM
                sides = [target(d)[0].astype(jnp.int32) for d in X_DIRS + ((0, 1), (0, -1))]

                @pl.when((sides[0] + sides[1] == nx) & (sides[2] + sides[3] == ny))
                def _(count=count):
                    wait_rows(sem, count)

    def x_copy(turn, slot, device):
        return pltpu.make_async_remote_copy(
            src_ref=xs[turn].at[slot],
            dst_ref=xr[turn].at[slot],
            send_sem=sent.at[0],
            recv_sem=arrived.at[turn],
            device_id=device,
            device_id_type=MESH,
        )

    def y_copy(turn, slot, device):
        return pltpu.make_async_remote_copy(
            src_ref=half(ys.at[turn, 0 if Y_DIRS[slot][1] > 0 else 1], Y_DIRS[slot][0]),
            dst_ref=y_place(turn, Y_DIRS[slot]),
            send_sem=sent.at[0],
            recv_sem=arrived.at[turn],
            device_id=device,
            device_id_type=MESH,
        )

    messages = ((a_out, a_in), (w_out, w_in), (p_out, p_in))

    def b_copy(which, step):
        other = lax.rem(h + step, owners)
        out, into = messages[which]
        return pltpu.make_async_remote_copy(
            src_ref=out if which == 0 else out.at[other],
            dst_ref=into.at[h],
            send_sem=sent.at[1],
            recv_sem=arrived.at[STEPS + which],
            device_id=(r, other),
            device_id_type=MESH,
        )

    def rim_copy(turn, direction):
        _, device = target(direction)
        if direction in X_DIRS:
            return x_copy(turn, X_DIRS.index(direction), device)
        return y_copy(turn, Y_DIRS.index(direction), device)

    def send_rim(turn, direction):
        there, _ = target(direction)

        @pl.when(there)
        def _():
            rim_copy(turn, direction).start()

    def send_rims(turn):
        for direction in X_DIRS + Y_DIRS:
            send_rim(turn, direction)

    def wait_rims(turn):
        wait_rows_of_rims(arrived.at[turn], (turn,))

    def wait_sends():
        wait_rows_of_rims(sent.at[0], range(STEPS))
        size = 0
        for out, into in messages:
            size += into.shape[1] * into.shape[2] // 128
        wait_rows(sent.at[1], (owners - 1) * size)

    def put_rims(turn, fields):
        to_next, to_before = pack_x(fields)
        xs[turn][0] = to_next
        xs[turn][1] = to_before
        ys[turn, 0], ys[turn, 1] = pack_y(fields)

    def take_rims(turn, count):
        rim_x = unpack_x(xr[turn][0], xr[turn][1])
        rim_y = unpack_y(yr[turn, 0], yr[turn, 1], count)
        return rim_x, rim_y, unpack_y(cr[turn, 0], cr[turn, 1], 3 * nz)

    def send_buildings(which):
        for step in range(owners // 2, 0, -1):
            b_copy(which, step).start()
            if owners - step != step:
                b_copy(which, owners - step).start()

    def take_buildings(which):
        into = messages[which][1]
        others = into.at[pl.ds(0, owners - 1)]
        pltpu.make_async_copy(others, others, arrived.at[STEPS + which]).wait()
        into = into[...]
        if into.shape[1] < capacity:
            into = jnp.concatenate([into, pltpu.roll(into, into.shape[2] // 2, 2)], axis=1)
        return into.reshape(slots, into.shape[2])

    lane = iota((slots, 128), 1)
    part = lane & 31
    slot_row = iota((slots, 1), 0)
    square = (slots, slots)

    couple = load("couple")[...].reshape(3, kinds, freedoms)
    arch = jnp.sum(
        jnp.where(iota(square, 0) == iota(square, 1), load("arch")[...].astype(F32), 0.0),
        axis=1,
        keepdims=True,
    )
    is_kind = [arch == float(a) for a in range(kinds)]
    coupling = []
    for c in range(3):
        chosen = jnp.zeros((slots, freedoms), F32)
        for a in range(kinds):
            chosen = jnp.where(is_kind[a], couple[c, a : a + 1, :], chosen)
        coupling.append(chosen)

    def couple_sum(c, state):
        return jnp.sum(coupling[c] * state, axis=1, keepdims=True)

    q = load("q")[...]
    shear = [couple_sum(c, q) for c in range(3)]
    word = lane & 15
    shear = jnp.where(word < 4, shear[0], jnp.where(word < 8, shear[1], shear[2]))
    shear = shear.reshape(owners, 2, 8, 128)
    group = iota((8, 128), 1) // 16
    a_width = a_out.shape[1]
    for t in range(a_width // 128):
        tile = jnp.zeros((8, 128), F32)
        for k in range(8):
            which, home = divmod(8 * t + k, a_width // 32)
            if home < owners:
                tile = jnp.where(group == k, shear[home, which], tile)
        a_out[:, 128 * t : 128 * (t + 1)] = tile
    a_in[h] = a_out[...]

    u = load("u")[...].reshape(3, nz, 8, 128)
    lam, mu = load("lam")[...] * (1.0 / 144.0), load("mu")[...] * (1.0 / 144.0)
    put_rims(0, jnp.concatenate([u.reshape(3 * nz, 8, 128), lam, mu], axis=0))
    for step in range(1, owners):

        @pl.when(h + step >= owners)
        def _(step=step):
            b_copy(0, step).start()

    for direction in DIRS:
        if earlier(direction) is not None:

            @pl.when(earlier(direction))
            def _(direction=direction):
                rim_copy(0, direction).start()

    def send_later(direction, when):
        @pl.when(when)
        def _():
            pl.semaphore_wait(entered.at[HEARD.index(direction)], 1)
            if direction == (0, 1):
                b_copy(0, 1).start()
            rim_copy(0, direction).start()

    send_later((-1, 0), later((-1, 0)))

    cells = load("cells")[0].astype(F32)
    wide = (slots, slots * FOOTPRINT_CELLS)
    own = (iota(wide, 1) // FOOTPRINT_CELLS) == iota(wide, 0)
    corner_cell = jnp.min(jnp.where(own, cells, 1e9), axis=1, keepdims=True)
    corner_x = jnp.floor(corner_cell * (1.0 / 128.0))
    corner_y = corner_cell - 128.0 * corner_x
    along_y = lane.astype(F32) - corner_y
    in_y = ((along_y == 0.0) | (along_y == 1.0)).astype(F32)
    window_y = in_y.astype(BF16)
    along_x = (lane & 7).astype(F32) - corner_x
    row_counts = load("counts")[0, pl.ds(h, 1), :].astype(F32)
    pairs = (slots, owners)
    live_count = jnp.sum(
        jnp.where(iota(pairs, 0) // capacity == iota(pairs, 1), row_counts, 0.0),
        axis=1,
        keepdims=True,
    )
    live = (slot_row % capacity).astype(F32) < live_count
    weight = jnp.where(
        live & ((along_x == 0.0) | (along_x == 1.0)) & (part < 24), 1.0 / FOOTPRINT_CELLS, 0.0
    )
    base_weight = jnp.where(lane < 64, weight, 0.0)
    mine = [(lane < 64) & (part >= 8 * c) & (part < 8 * c + 8) for c in range(3)]

    def group_sum(c, value):
        return jnp.sum(jnp.where(mine[c], value, 0.0), axis=1, keepdims=True)

    def surface_motion(field):
        surface = field[:, 0]
        high = surface.astype(BF16).astype(F32)
        nothing = jnp.zeros((8, 128), F32)
        stacked = jnp.concatenate(
            [high.reshape(24, 128), nothing, (surface - high).reshape(24, 128), nothing]
            + [nothing] * 8,
            axis=0,
        ).astype(BF16)
        gathered = lax.dot_general(
            window_y, stacked, (((1,), (1,)), ((), ())), preferred_element_type=F32
        )
        return gathered * base_weight

    def halves(pull):
        high = pull.astype(BF16).astype(F32)
        return jnp.where((lane & 32) == 0, high, pull - high)

    def surface_force(pull):
        spread = lax.dot_general(
            pull.T.astype(BF16), window_y, (((1,), (0,)), ((), ())), preferred_element_type=F32
        )
        return (spread[0:24] + spread[32:56]).reshape(3, 8, 128)

    def drive_of(base):
        drive = coupling[0] * base[0]
        for c in range(1, 3):
            drive = drive + coupling[c] * base[c]
        return drive

    def stiff_term(state):
        high, low = split(state)
        stacked = jnp.concatenate([high.astype(F32), low.astype(F32)], axis=0)
        twice = jnp.concatenate([arch, arch], axis=0)
        spread = jnp.concatenate(
            [jnp.where(twice == float(a), stacked, 0.0).astype(BF16) for a in range(kinds)],
            axis=1,
        )
        product = jnp.dot(spread, table[...], preferred_element_type=F32)
        product = product[:, :freedoms] + product[:, freedoms:]
        return product[:slots] + product[slots:]

    base = surface_motion(u)
    home_base = [group_sum(c, base) for c in range(3)]

    gain = load("buoy")[...] * dt2
    overlap_left, overlap_right = [], []
    for x in range(8):
        there = live & ((corner_x == float(x)) | (corner_x == float(x - 1)))
        window = jnp.where(there, in_y, 0.0)
        overlap_right.append(window)
        overlap_left.append(window * (gain[0, x : x + 1, :] * (1.0 / FOOTPRINT_CELLS**2)))
    left_high, left_low = split(jnp.concatenate(overlap_left, axis=1))
    right = jnp.concatenate(overlap_right, axis=1)
    width = w_out.shape[2]
    blank = [jnp.zeros((64, right.shape[1]), F32)]
    spare = width - 64 - slots
    after = [jnp.zeros((spare, right.shape[1]), F32)] if spare else []
    right = jnp.concatenate(blank + [right] + after, axis=0).astype(BF16)
    nt = (((1,), (1,)), ((), ()))
    overlap = lax.dot_general(left_high, right, nt, preferred_element_type=F32)
    overlap = overlap + lax.dot_general(left_low, right, nt, preferred_element_type=F32)

    send_later((1, 0), later((1, 0)))
    send_later((0, 1), later((0, 1)))

    for direction, side in (((1, -1), odd), ((-1, 1), even)):

        @pl.when(target(direction)[0] & side)
        def _(direction=direction):
            rim_copy(0, direction).start()

    stiff_high, stiff_low = split(load("stiff")[...])
    table[:, :freedoms] = stiff_high
    table[:, freedoms:] = stiff_low
    coasting = 2.0 * q - load("q_prev")[...] - dt2 * stiff_term(q)
    fields = base
    columns = [couple_sum(c, coasting) for c in range(3)]
    pairs_of = ((0, 0), (0, 1), (0, 2), (1, 1), (1, 2), (2, 2))
    columns += [dt2 * couple_sum(c, coupling[d]) for c, d in pairs_of]
    places = (24, 25, 26, 27, 28, 29, 30, 31, 56)
    for place, column in zip(places, columns):
        fields = jnp.where(lane == place, column, fields)
    first = jnp.where(lane < 64, fields, overlap[:, :128])
    if width > 128:
        first = jnp.concatenate([first, overlap[:, 128:]], axis=1)
    w_out[...] = first.reshape(owners, capacity, width)
    w_in[h] = w_out[h]
    send_later((-1, 1), later((-1, 1)))
    send_later((1, 1), later((1, 1)))
    for step in range(2, owners):

        @pl.when(h + step < owners)
        def _(step=step):
            pl.semaphore_wait(entered.at[len(HEARD) + step - 2], 1)
            b_copy(0, step).start()

    send_buildings(1)

    u_old = load("u_prev")[...].reshape(3, nz, 8, 128)

    shape = (3, nz, 8, 128)

    def push(field, rims, lam_mu, levels):
        fields = [part.reshape(shape)[:, :levels] for part in (field,) + rims]
        return divergence(*fields, *[part[:levels] for part in (lam, mu) + lam_mu])

    def on_surface(field, force):
        return jnp.concatenate([field[:, :1] + (gain[0] * force)[:, None], field[:, 1:]], axis=1)

    picked = (2 * a_width, 128)
    place, column = iota(picked, 0), iota(picked, 1)
    word = 16 * h + 4 * ((column & 31) // 8)
    word = jnp.where(column < 32, word, word + a_width)
    chosen = ((place == word) & (column < 64) & ((column & 31) < 24)).astype(F32).astype(BF16)

    wait_rims(0)
    rim_x, rim_y, corner = take_rims(0, 5 * nz)
    lam_mu = rim_x[3 * nz : 4 * nz], rim_x[4 * nz :], rim_y[3 * nz : 4 * nz], rim_y[4 * nz :]
    rims = rim_x[: 3 * nz], rim_y[: 3 * nz], corner
    coast = 2.0 * u - u_old
    top = push(u, rims, lam_mu, min(nz, 5))[:, :1]
    motion = surface_motion(coast[:, :1] + gain[:1] * top).reshape(owners, 2, 8, 128)
    p_out[...] = jnp.where(
        iota((owners, 8, 128), 2) < 64, motion[:, 0], pltpu.roll(motion[:, 1], 64, 2)
    )
    p_in[h] = p_out[h]

    @pl.when(h >= 0)
    def _():
        send_buildings(2)

    free = coast + gain * push(u, rims, lam_mu, nz)

    shears = take_buildings(0)
    shears_high, shears_low = split(shears)
    pull = jnp.dot(
        jnp.concatenate([shears_high, shears_low], axis=1), chosen, preferred_element_type=F32
    )
    u_new = on_surface(free, surface_force(pull * weight))
    u, u_old = u_new, u
    put_rims(1, u.reshape(3 * nz, 8, 128))
    send_rims(1)
    u_before_ref[...] = u

    words = take_buildings(1)
    low_words = words[:, :128]
    drive = drive_of([group_sum(c, low_words) for c in range(3)])
    q, q_old = coasting + dt2 * drive, q
    q_before_ref[...] = q
    stiff = stiff_term(q)

    gram = {}
    for place, pair in zip(places[3:], pairs_of):
        gram[pair] = gram[pair[::-1]] = low_words[:, place : place + 1]
    later = []
    for c in range(3):
        value = low_words[:, 24 + c : 25 + c]
        for d in range(3):
            value = value + gram[c, d] * home_base[d]
        later.append(value)
    later = jnp.where(part < 8, later[0], jnp.where(part < 16, later[1], later[2]))
    force = surface_force(halves(later * weight))

    left_high, left_low = split(words)
    blank = [jnp.zeros((64, shears.shape[1]), F32)]
    after = [jnp.zeros((spare, shears.shape[1]), F32)] if spare else []
    right = jnp.concatenate(blank + [shears] + after, axis=0)
    right_high, right_low = split(right)
    moved = jnp.dot(left_high, right_high, preferred_element_type=F32)
    moved = moved + jnp.dot(left_low, right_high, preferred_element_type=F32)
    moved = moved + jnp.dot(left_high, right_low, preferred_element_type=F32)
    moved_lane = iota(moved.shape, 1)
    moved_row = iota(moved.shape, 0) // capacity * 16
    moved = [
        jnp.sum(jnp.where(moved_lane == moved_row + 4 * c, moved, 0.0), axis=1, keepdims=True)
        for c in range(3)
    ]
    q_free = 2.0 * q - q_old + dt2 * (drive_of(moved) - stiff)
    u_free = on_surface(2.0 * u - u_old, force)

    wait_rims(1)
    total = push(u, take_rims(1, 3 * nz), lam_mu, nz)
    u_last_ref[...] = u_free + gain * total

    motion = take_buildings(2)
    q_last_ref[...] = q_free + dt2 * drive_of([group_sum(c, motion) for c in range(3)])
    wait_sends()


def shards(
    rows,
    owners,
    u_now,
    u_prev,
    lame_lambda,
    lame_mu,
    buoyancy,
    q_now,
    q_prev,
    archetype,
    stiffness,
    couple,
    counts,
    footprint,
):
    nz = lame_mu.shape[0]
    slots, freedoms = q_now.shape
    capacity = slots // owners
    kinds = stiffness.shape[0]
    pairs = (5 * nz) // 2, (3 * nz) // 2
    a_width = -(-32 * owners // 128) * 128
    w_width = -(-(64 + slots) // 128) * 128
    vmem = pl.BlockSpec(memory_space=pltpu.VMEM)
    hbm = pl.BlockSpec(memory_space=pltpu.HBM)
    dma = pltpu.SemaphoreType.DMA
    tiles = (3 * nz, 8, 128)
    operands = (
        u_now.reshape(tiles),
        u_prev.reshape(tiles),
        lame_lambda,
        lame_mu,
        buoyancy,
        q_now,
        q_prev,
        archetype.reshape(1, slots),
        stiffness.reshape(kinds * freedoms, freedoms),
        couple.transpose(1, 0, 2).reshape(3 * kinds, freedoms),
        counts,
        footprint,
    )
    results = (
        jax.ShapeDtypeStruct(u_now.shape, F32),
        jax.ShapeDtypeStruct(u_now.shape, F32),
        jax.ShapeDtypeStruct(q_now.shape, F32),
        jax.ShapeDtypeStruct(q_now.shape, F32),
    )
    held = pl.pallas_call(
        functools.partial(kernel, rows, owners),
        out_shape=tuple(pltpu.VMEM(result.shape, result.dtype) for result in results),
        in_specs=[hbm] * len(operands),
        out_specs=(vmem,) * 4,
        scratch_shapes=[
            pltpu.VMEM((2, pairs[0], 8, 128), F32),
            pltpu.VMEM((2, pairs[1], 8, 128), F32),
            pltpu.VMEM((2, pairs[0], 8, 128), F32),
            pltpu.VMEM((2, pairs[1], 8, 128), F32),
            pltpu.VMEM((STEPS, 2, 8, 128), F32),
            pltpu.VMEM((STEPS, 2, 8, 128), F32),
            pltpu.VMEM((STEPS, 2, 8, 128), F32),
            pltpu.VMEM((8, a_width), F32),
            pltpu.VMEM((owners, 8, a_width), F32),
            pltpu.VMEM((owners, capacity, w_width), F32),
            pltpu.VMEM((owners, capacity, w_width), F32),
            pltpu.VMEM((owners, 8, 128), F32),
            pltpu.VMEM((owners, 8, 128), F32),
            pltpu.VMEM((kinds * freedoms, 2 * freedoms), BF16),
        ]
        + [
            pltpu.VMEM((slots + 3 * kinds, freedoms), F32),
            pltpu.VMEM((5 * nz, 8, 128), F32),
            pltpu.VMEM((kinds * freedoms + slots, freedoms), F32),
            pltpu.VMEM((4 * nz, 8, 128), F32),
            pltpu.VMEM((1, slots), jnp.int32),
            pltpu.VMEM(counts.shape, jnp.int32),
            pltpu.VMEM(footprint.shape, jnp.int32),
            dma((7,)),
            dma((2,)),
            dma((STEPS + 3,)),
            pltpu.SemaphoreType.REGULAR((len(HEARD) + owners - 2,)),
        ],
        compiler_params=pltpu.CompilerParams(
            collective_id=0, has_side_effects=True, vmem_limit_bytes=60 * 1024 * 1024
        ),
    )(*operands)
    return pl.pallas_call(
        store,
        out_shape=results,
        in_specs=[vmem] * 4,
        out_specs=(hbm,) * 4,
        scratch_shapes=[dma((4,))],
        compiler_params=pltpu.CompilerParams(vmem_limit_bytes=1024 * 1024),
    )(*held)


def store(*refs):
    copies = [
        pltpu.make_async_copy(refs[k], refs[4 + k], refs[8].at[k]) for k in range(4)
    ]
    for copy in copies:
        copy.start()
    for copy in copies:
        copy.wait()


def solution(mesh):
    return jax.shard_map(
        functools.partial(shards, mesh.shape["gx"], mesh.shape["gy"]),
        mesh=mesh,
        in_specs=(
            P(None, None, "gx", "gy"),
            P(None, None, "gx", "gy"),
            P(None, "gx", "gy"),
            P(None, "gx", "gy"),
            P(None, "gx", "gy"),
            P(("gx", "gy"), None),
            P(("gx", "gy"), None),
            P(("gx", "gy")),
            P(),
            P(),
            P("gx", None, None),
            P("gx", "gy", None),
        ),
        out_specs=(
            P(None, None, "gx", "gy"),
            P(None, None, "gx", "gy"),
            P(("gx", "gy"), None),
            P(("gx", "gy"), None),
        ),
        check_vma=False,
    )
```

```python
import functools

import jax
import jax.numpy as jnp
from jax import lax
from jax.experimental import pallas as pl
from jax.experimental.pallas import tpu as pltpu
from jax.sharding import PartitionSpec as P

FOOTPRINT_CELLS = 4
STEPS = 2
TIME_STEP = 0.25
RIM = 4
MESH = pl.DeviceIdType.MESH
F32 = jnp.float32
BF16 = jnp.bfloat16

X_DIRS = ((1, 0), (-1, 0))
Y_DIRS = ((-1, 1), (-1, -1), (0, 1), (0, -1), (1, 1), (1, -1))
DIRS = X_DIRS + Y_DIRS
HEARD = tuple(d for d in DIRS if d[1] > 0 or d in X_DIRS)


def iota(shape, dim):
    return lax.broadcasted_iota(jnp.int32, shape, dim)


def split(value):
    high = value.astype(BF16)
    return high, (value - high.astype(F32)).astype(BF16)


def pack_x(fields):
    half = fields.shape[0] // 2
    first, second = fields[:half], fields[half:]
    upper = iota((1, 8, 128), 1) < RIM
    to_next = jnp.where(upper, pltpu.roll(first, RIM, 1), second)
    to_before = jnp.where(upper, first, pltpu.roll(second, RIM, 1))
    return to_next, to_before


def unpack_x(from_before, from_next):
    upper = iota((1, 8, 128), 1) < RIM
    first = jnp.where(upper, from_next, pltpu.roll(from_before, RIM, 1))
    second = jnp.where(upper, pltpu.roll(from_next, RIM, 1), from_before)
    return jnp.concatenate([first, second], axis=0)


def pack_y(fields):
    lane = iota((8, 128), 1)
    ahead, behind = jnp.zeros((8, 128), F32), jnp.zeros((8, 128), F32)
    for k in range(fields.shape[0]):
        place = RIM * k
        moved = pltpu.roll(fields[k], (place + RIM) % 128, 1)
        ahead = jnp.where((lane >= place) & (lane < place + RIM), moved, ahead)
        behind = jnp.where((lane >= place + RIM) & (lane < place + 2 * RIM), moved, behind)
    return ahead, behind


def unpack_y(ahead, behind, count):
    odd = (iota((8, 128), 1) & RIM) != 0
    tiles = jnp.where(odd, behind, ahead), jnp.where(odd, ahead, behind)
    slabs = []
    for k in range(count):
        slabs.append(pltpu.roll(tiles[k % 2], (124 - RIM * k) % 128, 1))
    return jnp.stack(slabs)


def slope(here, other, axis, both):
    size = here.shape[axis]
    place = iota((1,) * (here.ndim - 2) + (8, 128), axis)

    def shifted(mine, theirs, shift):
        entering = place < shift if shift > 0 else place >= size + shift
        return pltpu.roll(jnp.where(entering, theirs, mine), (-shift) % size, axis)

    def slope_of(mine, theirs):
        return 8.0 * (shifted(mine, theirs, 1) - shifted(mine, theirs, -1)) - (
            shifted(mine, theirs, 2) - shifted(mine, theirs, -2)
        )

    if both:
        return slope_of(here, other), slope_of(other, here)
    return slope_of(here, other)


def slope_z(field):
    nothing = jnp.zeros((2,) + field.shape[1:], F32)
    padded = jnp.concatenate([nothing, field, nothing], axis=0)
    n = field.shape[0]
    return 8.0 * (padded[3 : n + 3] - padded[1 : n + 1]) - (padded[4 : n + 4] - padded[:n])


def divergence(u, rim_x, rim_y, corner, lam, mu, lam_x, mu_x, lam_y, mu_y):
    ux, uy, uz = u[0], u[1], u[2]
    x_x, x_xh = slope(ux, rim_x[0], 1, True)
    y_x, y_xh = slope(uy, rim_x[1], 1, True)
    z_x, z_xh = slope(uz, rim_x[2], 1, True)
    x_y, x_yh = slope(ux, rim_y[0], 2, True)
    y_y, y_yh = slope(uy, rim_y[1], 2, True)
    z_y, z_yh = slope(uz, rim_y[2], 2, True)
    x_z, y_z, z_z = slope_z(ux), slope_z(uy), slope_z(uz)
    spread = lam * (x_x + y_y + z_z)
    s_xx = spread + 2.0 * mu * x_x
    s_yy = spread + 2.0 * mu * y_y
    s_zz = spread + 2.0 * mu * z_z
    s_xy = mu * (x_y + y_x)
    s_xz = mu * (x_z + z_x)
    s_yz = mu * (y_z + z_y)
    x_yr = slope(rim_x[0], corner[0], 2, False)
    y_yr = slope(rim_x[1], corner[1], 2, False)
    x_zr, z_zr = slope_z(rim_x[0]), slope_z(rim_x[2])
    s_xx_r = lam_x * (x_xh + y_yr + z_zr) + 2.0 * mu_x * x_xh
    s_xy_r = mu_x * (x_yr + y_xh)
    s_xz_r = mu_x * (x_zr + z_xh)
    x_xc = slope(rim_y[0], corner[0], 1, False)
    y_xc = slope(rim_y[1], corner[1], 1, False)
    y_zc, z_zc = slope_z(rim_y[1]), slope_z(rim_y[2])
    s_yy_c = lam_y * (x_xc + y_yh + z_zc) + 2.0 * mu_y * y_yh
    s_xy_c = mu_y * (x_yh + y_xc)
    s_yz_c = mu_y * (y_zc + z_yh)
    total_x = slope(s_xx, s_xx_r, 1, False) + slope(s_xy, s_xy_c, 2, False) + slope_z(s_xz)
    total_y = slope(s_xy, s_xy_r, 1, False) + slope(s_yy, s_yy_c, 2, False) + slope_z(s_yz)
    total_z = slope(s_xz, s_xz_r, 1, False) + slope(s_yz, s_yz_c, 2, False) + slope_z(s_zz)
    return jnp.stack([total_x, total_y, total_z])


def kernel(
    rows,
    owners,
    u_hbm,
    u_prev_hbm,
    lam_hbm,
    mu_hbm,
    buoy_hbm,
    q_hbm,
    q_prev_hbm,
    arch_hbm,
    stiff_hbm,
    couple_hbm,
    counts_hbm,
    cells_hbm,
    u_last_ref,
    u_before_ref,
    q_last_ref,
    q_before_ref,
    xs0,
    xs1,
    xr0,
    xr1,
    ys,
    yr,
    cr,
    a_out,
    a_in,
    w_out,
    w_in,
    p_out,
    p_in,
    table,
    frame_ref,
    near_ref,
    wide_ref,
    far_ref,
    arch_ref,
    counts_ref,
    cells_ref,
    loaded,
    sent,
    arrived,
    entered,
):
    r, h = lax.axis_index("gx"), lax.axis_index("gy")
    nz = lam_hbm.shape[0]
    slots, freedoms = q_hbm.shape
    capacity = slots // owners
    kinds = couple_hbm.shape[0] // 3
    dt2 = TIME_STEP * TIME_STEP
    xs, xr = (xs0, xs1), (xr0, xr1)

    def target(direction):
        dx, dy = direction
        there = None
        for d, me, n in ((dx, r, rows), (dy, h, owners)):
            if d:
                ok = me + d < n if d > 0 else me > 0
                there = ok if there is None else there & ok
        return there, (r + dx, h + dy)

    def source(direction):
        return target((-direction[0], -direction[1]))

    loads = {}

    def start_load(name, ref, parts):
        sem = loaded.at[len(loads)]
        start, places = 0, {}
        for part, source_ref in parts:
            size = source_ref.shape[0]
            into = ref if len(parts) == 1 else ref.at[pl.ds(start, size)]
            pltpu.make_async_copy(source_ref, into, sem).start()
            places[part] = into
            start += size
        loads[name] = [pltpu.make_async_copy(ref, ref, sem)], places

    start_load("frame", frame_ref, (("q", q_hbm), ("couple", couple_hbm)))
    start_load("arch", arch_ref, (("arch", arch_hbm),))
    start_load("near", near_ref, (("u", u_hbm), ("lam", lam_hbm), ("mu", mu_hbm)))
    odd = lax.rem(r, 2) == 1
    even = jnp.logical_not(odd)

    def later(direction):
        dx, dy = direction
        there = target(direction)[0]
        if dy == 0 or direction == (-1, 1):
            return there & odd
        return there if dy > 0 else None

    def earlier(direction):
        dx, dy = direction
        there = target(direction)[0]
        if dy == 0 or direction == (1, -1):
            return there & even
        return there if dy < 0 else None

    barrier = pltpu.get_barrier_semaphore()
    for direction in DIRS:
        if later(direction) is not None:

            @pl.when(later(direction))
            def _(device=target(direction)[1]):
                pl.semaphore_signal(barrier, inc=1, device_id=device, device_id_type=MESH)

    for step in range(2, owners):

        @pl.when(h + step < owners)
        def _(device=(r, h + step)):
            pl.semaphore_signal(barrier, inc=1, device_id=device, device_id_type=MESH)

    arrivals = jnp.maximum(h - 1, 0)
    for direction in DIRS:
        if earlier(direction) is not None:
            arrivals = arrivals + earlier(direction).astype(jnp.int32)

    start_load("cells", cells_ref, (("cells", cells_hbm),))
    start_load("counts", counts_ref, (("counts", counts_hbm),))
    start_load("far", far_ref, (("u_prev", u_prev_hbm), ("buoy", buoy_hbm)))
    start_load("wide", wide_ref, (("stiff", stiff_hbm), ("q_prev", q_prev_hbm)))

    def half(ref, dx):
        return ref if dx == 0 else ref.at[pl.ds(RIM if dx > 0 else 0, RIM)]

    def y_place(turn, direction):
        dx, dy = direction
        k = 0 if dy > 0 else 1
        return half((cr if dx else yr).at[turn, k], dx)

    @pl.when(arrivals > 0)
    def _():
        pl.semaphore_wait(barrier, arrivals)

    def tell(direction, about):
        pl.semaphore_signal(
            entered.at[HEARD.index(about)],
            inc=1,
            device_id=target(direction)[1],
            device_id_type=MESH,
        )

    for direction in DIRS:
        if earlier(direction) is not None:

            @pl.when(earlier(direction))
            def _(direction=direction):
                tell(direction, (-direction[0], -direction[1]))

    for step in range(2, owners):

        @pl.when(h >= step)
        def _(step=step):
            pl.semaphore_signal(
                entered.at[len(HEARD) + step - 2],
                inc=1,
                device_id=(r, h - step),
                device_id_type=MESH,
            )

    for slot, direction in enumerate(X_DIRS):
        there, _ = source(direction)

        @pl.when(jnp.logical_not(there))
        def _(slot=slot):
            for buffer in xr:
                buffer[slot] = jnp.zeros(buffer.shape[1:], F32)

    for slot, direction in enumerate(Y_DIRS):
        there, _ = source(direction)

        @pl.when(jnp.logical_not(there))
        def _(direction=direction):
            for turn in range(STEPS):
                ref = y_place(turn, direction)
                ref[...] = jnp.zeros(ref.shape, F32)

    def load(part):
        for copies, places in loads.values():
            if part in places:
                while copies:
                    copies.pop().wait()
                return places[part]

    def wait_rows(sem, count):
        rows_of = wide_ref.at[pl.ds(0, count)]
        pltpu.make_async_copy(rows_of, rows_of, sem).wait()

    def wait_rows_of_rims(sem, turns):
        for nx in (1, 2):
            for ny in (1, 2):
                count = 0
                for turn in turns:
                    count += nx * xs[turn].shape[1] * 8 + ny * 8 + nx * ny * RIM
                sides = [target(d)[0].astype(jnp.int32) for d in X_DIRS + ((0, 1), (0, -1))]

                @pl.when((sides[0] + sides[1] == nx) & (sides[2] + sides[3] == ny))
                def _(count=count):
                    wait_rows(sem, count)

    def x_copy(turn, slot, device):
        return pltpu.make_async_remote_copy(
            src_ref=xs[turn].at[slot],
            dst_ref=xr[turn].at[slot],
            send_sem=sent.at[0],
            recv_sem=arrived.at[turn],
            device_id=device,
            device_id_type=MESH,
        )

    def y_copy(turn, slot, device):
        return pltpu.make_async_remote_copy(
            src_ref=half(ys.at[turn, 0 if Y_DIRS[slot][1] > 0 else 1], Y_DIRS[slot][0]),
            dst_ref=y_place(turn, Y_DIRS[slot]),
            send_sem=sent.at[0],
            recv_sem=arrived.at[turn],
            device_id=device,
            device_id_type=MESH,
        )

    messages = ((a_out, a_in), (w_out, w_in), (p_out, p_in))

    def b_copy(which, step):
        other = lax.rem(h + step, owners)
        out, into = messages[which]
        return pltpu.make_async_remote_copy(
            src_ref=out if which == 0 else out.at[other],
            dst_ref=into.at[h],
            send_sem=sent.at[1],
            recv_sem=arrived.at[STEPS + which],
            device_id=(r, other),
            device_id_type=MESH,
        )

    def rim_copy(turn, direction):
        _, device = target(direction)
        if direction in X_DIRS:
            return x_copy(turn, X_DIRS.index(direction), device)
        return y_copy(turn, Y_DIRS.index(direction), device)

    def send_rim(turn, direction):
        there, _ = target(direction)

        @pl.when(there)
        def _():
            rim_copy(turn, direction).start()

    def send_rims(turn):
        for direction in X_DIRS + Y_DIRS:
            send_rim(turn, direction)

    def wait_rims(turn):
        wait_rows_of_rims(arrived.at[turn], (turn,))

    def wait_sends():
        wait_rows_of_rims(sent.at[0], range(STEPS))
        size = 0
        for out, into in messages:
            size += into.shape[1] * into.shape[2] // 128
        wait_rows(sent.at[1], (owners - 1) * size)

    def put_rims(turn, fields):
        to_next, to_before = pack_x(fields)
        xs[turn][0] = to_next
        xs[turn][1] = to_before
        ys[turn, 0], ys[turn, 1] = pack_y(fields)

    def take_rims(turn, count):
        rim_x = unpack_x(xr[turn][0], xr[turn][1])
        rim_y = unpack_y(yr[turn, 0], yr[turn, 1], count)
        return rim_x, rim_y, unpack_y(cr[turn, 0], cr[turn, 1], 3 * nz)

    def send_buildings(which):
        for step in range(owners // 2, 0, -1):
            b_copy(which, step).start()
            if owners - step != step:
                b_copy(which, owners - step).start()

    def take_buildings(which):
        into = messages[which][1]
        others = into.at[pl.ds(0, owners - 1)]
        pltpu.make_async_copy(others, others, arrived.at[STEPS + which]).wait()
        into = into[...]
        if into.shape[1] < capacity:
            into = jnp.concatenate([into, pltpu.roll(into, into.shape[2] // 2, 2)], axis=1)
        return into.reshape(slots, into.shape[2])

    lane = iota((slots, 128), 1)
    part = lane & 31
    slot_row = iota((slots, 1), 0)
    square = (slots, slots)

    couple = load("couple")[...].reshape(3, kinds, freedoms)
    arch = jnp.sum(
        jnp.where(iota(square, 0) == iota(square, 1), load("arch")[...].astype(F32), 0.0),
        axis=1,
        keepdims=True,
    )
    is_kind = [arch == float(a) for a in range(kinds)]
    coupling = []
    for c in range(3):
        chosen = jnp.zeros((slots, freedoms), F32)
        for a in range(kinds):
            chosen = jnp.where(is_kind[a], couple[c, a : a + 1, :], chosen)
        coupling.append(chosen)

    def couple_sum(c, state):
        return jnp.sum(coupling[c] * state, axis=1, keepdims=True)

    q = load("q")[...]
    shear = [couple_sum(c, q) for c in range(3)]
    word = lane & 15
    shear = jnp.where(word < 4, shear[0], jnp.where(word < 8, shear[1], shear[2]))
    shear = shear.reshape(owners, 2, 8, 128)
    group = iota((8, 128), 1) // 16
    a_width = a_out.shape[1]
    for t in range(a_width // 128):
        tile = jnp.zeros((8, 128), F32)
        for k in range(8):
            which, home = divmod(8 * t + k, a_width // 32)
            if home < owners:
                tile = jnp.where(group == k, shear[home, which], tile)
        a_out[:, 128 * t : 128 * (t + 1)] = tile
    a_in[h] = a_out[...]
    for step in range(1, owners):

        @pl.when(h + step >= owners)
        def _(step=step):
            b_copy(0, step).start()

    u = load("u")[...].reshape(3, nz, 8, 128)
    lam, mu = load("lam")[...] * (1.0 / 144.0), load("mu")[...] * (1.0 / 144.0)
    put_rims(0, jnp.concatenate([u.reshape(3 * nz, 8, 128), lam, mu], axis=0))
    for direction in DIRS:
        if earlier(direction) is not None:

            @pl.when(earlier(direction))
            def _(direction=direction):
                rim_copy(0, direction).start()

    def send_later(direction, when):
        @pl.when(when)
        def _():
            pl.semaphore_wait(entered.at[HEARD.index(direction)], 1)
            if direction == (0, 1):
                b_copy(0, 1).start()
            rim_copy(0, direction).start()

    send_later((-1, 0), later((-1, 0)))

    cells = load("cells")[0].astype(F32)
    wide = (slots, slots * FOOTPRINT_CELLS)
    own = (iota(wide, 1) // FOOTPRINT_CELLS) == iota(wide, 0)
    corner_cell = jnp.min(jnp.where(own, cells, 1e9), axis=1, keepdims=True)
    corner_x = jnp.floor(corner_cell * (1.0 / 128.0))
    corner_y = corner_cell - 128.0 * corner_x
    along_y = lane.astype(F32) - corner_y
    in_y = ((along_y == 0.0) | (along_y == 1.0)).astype(F32)
    window_y = in_y.astype(BF16)
    along_x = (lane & 7).astype(F32) - corner_x
    row_counts = load("counts")[0, pl.ds(h, 1), :].astype(F32)
    pairs = (slots, owners)
    live_count = jnp.sum(
        jnp.where(iota(pairs, 0) // capacity == iota(pairs, 1), row_counts, 0.0),
        axis=1,
        keepdims=True,
    )
    live = (slot_row % capacity).astype(F32) < live_count
    weight = jnp.where(
        live & ((along_x == 0.0) | (along_x == 1.0)) & (part < 24), 1.0 / FOOTPRINT_CELLS, 0.0
    )
    base_weight = jnp.where(lane < 64, weight, 0.0)
    mine = [(lane < 64) & (part >= 8 * c) & (part < 8 * c + 8) for c in range(3)]

    def group_sum(c, value):
        return jnp.sum(jnp.where(mine[c], value, 0.0), axis=1, keepdims=True)

    def surface_motion(field):
        surface = field[:, 0]
        high = surface.astype(BF16).astype(F32)
        nothing = jnp.zeros((8, 128), F32)
        stacked = jnp.concatenate(
            [high.reshape(24, 128), nothing, (surface - high).reshape(24, 128), nothing]
            + [nothing] * 8,
            axis=0,
        ).astype(BF16)
        gathered = lax.dot_general(
            window_y, stacked, (((1,), (1,)), ((), ())), preferred_element_type=F32
        )
        return gathered * base_weight

    def halves(pull):
        high = pull.astype(BF16).astype(F32)
        return jnp.where((lane & 32) == 0, high, pull - high)

    def surface_force(pull):
        spread = lax.dot_general(
            pull.T.astype(BF16), window_y, (((1,), (0,)), ((), ())), preferred_element_type=F32
        )
        return (spread[0:24] + spread[32:56]).reshape(3, 8, 128)

    def drive_of(base):
        drive = coupling[0] * base[0]
        for c in range(1, 3):
            drive = drive + coupling[c] * base[c]
        return drive

    def stiff_term(state):
        high, low = split(state)
        stacked = jnp.concatenate([high.astype(F32), low.astype(F32)], axis=0)
        twice = jnp.concatenate([arch, arch], axis=0)
        spread = jnp.concatenate(
            [jnp.where(twice == float(a), stacked, 0.0).astype(BF16) for a in range(kinds)],
            axis=1,
        )
        product = jnp.dot(spread, table[...], preferred_element_type=F32)
        product = product[:, :freedoms] + product[:, freedoms:]
        return product[:slots] + product[slots:]

    base = surface_motion(u)
    home_base = [group_sum(c, base) for c in range(3)]

    gain = load("buoy")[...] * dt2
    overlap_left, overlap_right = [], []
    for x in range(8):
        there = live & ((corner_x == float(x)) | (corner_x == float(x - 1)))
        window = jnp.where(there, in_y, 0.0)
        overlap_right.append(window)
        overlap_left.append(window * (gain[0, x : x + 1, :] * (1.0 / FOOTPRINT_CELLS**2)))
    left_high, left_low = split(jnp.concatenate(overlap_left, axis=1))
    right = jnp.concatenate(overlap_right, axis=1)
    width = w_out.shape[2]
    blank = [jnp.zeros((64, right.shape[1]), F32)]
    spare = width - 64 - slots
    after = [jnp.zeros((spare, right.shape[1]), F32)] if spare else []
    right = jnp.concatenate(blank + [right] + after, axis=0).astype(BF16)
    nt = (((1,), (1,)), ((), ()))
    overlap = lax.dot_general(left_high, right, nt, preferred_element_type=F32)
    overlap = overlap + lax.dot_general(left_low, right, nt, preferred_element_type=F32)

    def send_corner(direction, side):
        @pl.when(target(direction)[0] & side)
        def _():
            rim_copy(0, direction).start()

    send_later((0, 1), later((0, 1)))
    send_corner((-1, 1), even)
    send_later((-1, 1), later((-1, 1)))
    send_later((1, 0), later((1, 0)))
    send_corner((1, -1), odd)

    stiff_high, stiff_low = split(load("stiff")[...])
    table[:, :freedoms] = stiff_high
    table[:, freedoms:] = stiff_low
    coasting = 2.0 * q - load("q_prev")[...] - dt2 * stiff_term(q)
    fields = base
    columns = [couple_sum(c, coasting) for c in range(3)]
    pairs_of = ((0, 0), (0, 1), (0, 2), (1, 1), (1, 2), (2, 2))
    columns += [dt2 * couple_sum(c, coupling[d]) for c, d in pairs_of]
    places = (24, 25, 26, 27, 28, 29, 30, 31, 56)
    for place, column in zip(places, columns):
        fields = jnp.where(lane == place, column, fields)
    first = jnp.where(lane < 64, fields, overlap[:, :128])
    if width > 128:
        first = jnp.concatenate([first, overlap[:, 128:]], axis=1)
    w_out[...] = first.reshape(owners, capacity, width)
    w_in[h] = w_out[h]
    send_later((1, 1), later((1, 1)))
    for step in range(2, owners):

        @pl.when(h + step < owners)
        def _(step=step):
            pl.semaphore_wait(entered.at[len(HEARD) + step - 2], 1)
            b_copy(0, step).start()

    send_buildings(1)

    u_old = load("u_prev")[...].reshape(3, nz, 8, 128)

    shape = (3, nz, 8, 128)

    def push(field, rims, lam_mu, levels):
        fields = [part.reshape(shape)[:, :levels] for part in (field,) + rims]
        return divergence(*fields, *[part[:levels] for part in (lam, mu) + lam_mu])

    def on_surface(field, force):
        return jnp.concatenate([field[:, :1] + (gain[0] * force)[:, None], field[:, 1:]], axis=1)

    wait_rims(0)
    rim_x, rim_y, corner = take_rims(0, 5 * nz)
    lam_mu = rim_x[3 * nz : 4 * nz], rim_x[4 * nz :], rim_y[3 * nz : 4 * nz], rim_y[4 * nz :]
    rims = rim_x[: 3 * nz], rim_y[: 3 * nz], corner
    coast = 2.0 * u - u_old
    top = push(u, rims, lam_mu, min(nz, 5))[:, :1]
    motion = surface_motion(coast[:, :1] + gain[:1] * top).reshape(owners, 2, 8, 128)
    p_out[...] = jnp.where(
        iota((owners, 8, 128), 2) < 64, motion[:, 0], pltpu.roll(motion[:, 1], 64, 2)
    )
    p_in[h] = p_out[h]

    @pl.when(h >= 0)
    def _():
        send_buildings(2)

    free = coast + gain * push(u, rims, lam_mu, nz)

    shears = take_buildings(0)
    place = iota(shears.shape, 1) - 16 * h
    first = [
        jnp.sum(jnp.where(place == 4 * c, shears, 0.0), axis=1, keepdims=True) for c in range(3)
    ]
    pull = jnp.where(part < 8, first[0], jnp.where(part < 16, first[1], first[2]))
    u_new = on_surface(free, surface_force(halves(pull * weight)))
    u, u_old = u_new, u
    put_rims(1, u.reshape(3 * nz, 8, 128))
    send_rims(1)
    u_before_ref[...] = u

    words = take_buildings(1)
    low_words = words[:, :128]
    drive = drive_of([group_sum(c, low_words) for c in range(3)])
    q, q_old = coasting + dt2 * drive, q
    q_before_ref[...] = q
    stiff = stiff_term(q)

    gram = {}
    for place, pair in zip(places[3:], pairs_of):
        gram[pair] = gram[pair[::-1]] = low_words[:, place : place + 1]
    later = []
    for c in range(3):
        value = low_words[:, 24 + c : 25 + c]
        for d in range(3):
            value = value + gram[c, d] * home_base[d]
        later.append(value)
    later = jnp.where(part < 8, later[0], jnp.where(part < 16, later[1], later[2]))
    force = surface_force(halves(later * weight))

    left_high, left_low = split(words)
    blank = [jnp.zeros((64, shears.shape[1]), F32)]
    after = [jnp.zeros((spare, shears.shape[1]), F32)] if spare else []
    right = jnp.concatenate(blank + [shears] + after, axis=0)
    right_high, right_low = split(right)
    moved = jnp.dot(left_high, right_high, preferred_element_type=F32)
    moved = moved + jnp.dot(left_low, right_high, preferred_element_type=F32)
    moved = moved + jnp.dot(left_high, right_low, preferred_element_type=F32)
    moved_lane = iota(moved.shape, 1)
    moved_row = iota(moved.shape, 0) // capacity * 16
    moved = [
        jnp.sum(jnp.where(moved_lane == moved_row + 4 * c, moved, 0.0), axis=1, keepdims=True)
        for c in range(3)
    ]
    q_free = 2.0 * q - q_old + dt2 * (drive_of(moved) - stiff)
    u_free = on_surface(2.0 * u - u_old, force)

    wait_rims(1)
    total = push(u, take_rims(1, 3 * nz), lam_mu, nz)
    u_last_ref[...] = u_free + gain * total

    motion = take_buildings(2)
    q_last_ref[...] = q_free + dt2 * drive_of([group_sum(c, motion) for c in range(3)])
    wait_sends()


def shards(
    rows,
    owners,
    u_now,
    u_prev,
    lame_lambda,
    lame_mu,
    buoyancy,
    q_now,
    q_prev,
    archetype,
    stiffness,
    couple,
    counts,
    footprint,
):
    nz = lame_mu.shape[0]
    slots, freedoms = q_now.shape
    capacity = slots // owners
    kinds = stiffness.shape[0]
    pairs = (5 * nz) // 2, (3 * nz) // 2
    a_width = -(-32 * owners // 128) * 128
    w_width = -(-(64 + slots) // 128) * 128
    vmem = pl.BlockSpec(memory_space=pltpu.VMEM)
    hbm = pl.BlockSpec(memory_space=pltpu.HBM)
    dma = pltpu.SemaphoreType.DMA
    tiles = (3 * nz, 8, 128)
    operands = (
        u_now.reshape(tiles),
        u_prev.reshape(tiles),
        lame_lambda,
        lame_mu,
        buoyancy,
        q_now,
        q_prev,
        archetype.reshape(1, slots),
        stiffness.reshape(kinds * freedoms, freedoms),
        couple.transpose(1, 0, 2).reshape(3 * kinds, freedoms),
        counts,
        footprint,
    )
    results = (
        jax.ShapeDtypeStruct(u_now.shape, F32),
        jax.ShapeDtypeStruct(u_now.shape, F32),
        jax.ShapeDtypeStruct(q_now.shape, F32),
        jax.ShapeDtypeStruct(q_now.shape, F32),
    )
    held = pl.pallas_call(
        functools.partial(kernel, rows, owners),
        out_shape=tuple(pltpu.VMEM(result.shape, result.dtype) for result in results),
        in_specs=[hbm] * len(operands),
        out_specs=(vmem,) * 4,
        scratch_shapes=[
            pltpu.VMEM((2, pairs[0], 8, 128), F32),
            pltpu.VMEM((2, pairs[1], 8, 128), F32),
            pltpu.VMEM((2, pairs[0], 8, 128), F32),
            pltpu.VMEM((2, pairs[1], 8, 128), F32),
            pltpu.VMEM((STEPS, 2, 8, 128), F32),
            pltpu.VMEM((STEPS, 2, 8, 128), F32),
            pltpu.VMEM((STEPS, 2, 8, 128), F32),
            pltpu.VMEM((8, a_width), F32),
            pltpu.VMEM((owners, 8, a_width), F32),
            pltpu.VMEM((owners, capacity, w_width), F32),
            pltpu.VMEM((owners, capacity, w_width), F32),
            pltpu.VMEM((owners, 8, 128), F32),
            pltpu.VMEM((owners, 8, 128), F32),
            pltpu.VMEM((kinds * freedoms, 2 * freedoms), BF16),
        ]
        + [
            pltpu.VMEM((slots + 3 * kinds, freedoms), F32),
            pltpu.VMEM((5 * nz, 8, 128), F32),
            pltpu.VMEM((kinds * freedoms + slots, freedoms), F32),
            pltpu.VMEM((4 * nz, 8, 128), F32),
            pltpu.VMEM((1, slots), jnp.int32),
            pltpu.VMEM(counts.shape, jnp.int32),
            pltpu.VMEM(footprint.shape, jnp.int32),
            dma((7,)),
            dma((2,)),
            dma((STEPS + 3,)),
            pltpu.SemaphoreType.REGULAR((len(HEARD) + owners - 2,)),
        ],
        compiler_params=pltpu.CompilerParams(
            collective_id=0, has_side_effects=True, vmem_limit_bytes=60 * 1024 * 1024
        ),
    )(*operands)
    return pl.pallas_call(
        store,
        out_shape=results,
        in_specs=[vmem] * 4,
        out_specs=(hbm,) * 4,
        scratch_shapes=[dma((4,))],
        compiler_params=pltpu.CompilerParams(vmem_limit_bytes=1024 * 1024),
    )(*held)


def store(*refs):
    copies = [
        pltpu.make_async_copy(refs[k], refs[4 + k], refs[8].at[k]) for k in range(4)
    ]
    for copy in copies:
        copy.start()
    for copy in copies:
        copy.wait()


def solution(mesh):
    return jax.shard_map(
        functools.partial(shards, mesh.shape["gx"], mesh.shape["gy"]),
        mesh=mesh,
        in_specs=(
            P(None, None, "gx", "gy"),
            P(None, None, "gx", "gy"),
            P(None, "gx", "gy"),
            P(None, "gx", "gy"),
            P(None, "gx", "gy"),
            P(("gx", "gy"), None),
            P(("gx", "gy"), None),
            P(("gx", "gy")),
            P(),
            P(),
            P("gx", None, None),
            P("gx", "gy", None),
        ),
        out_specs=(
            P(None, None, "gx", "gy"),
            P(None, None, "gx", "gy"),
            P(("gx", "gy"), None),
            P(("gx", "gy"), None),
        ),
        check_vma=False,
    )
```

```python
import functools

import jax
import jax.numpy as jnp
from jax import lax
from jax.experimental import pallas as pl
from jax.experimental.pallas import tpu as pltpu
from jax.sharding import PartitionSpec as P

FOOTPRINT_CELLS = 4
STEPS = 2
TIME_STEP = 0.25
RIM = 4
MESH = pl.DeviceIdType.MESH
F32 = jnp.float32
BF16 = jnp.bfloat16

X_DIRS = ((1, 0), (-1, 0))
Y_DIRS = ((-1, 1), (-1, -1), (0, 1), (0, -1), (1, 1), (1, -1))
DIRS = X_DIRS + Y_DIRS
HEARD = tuple(d for d in DIRS if d[1] > 0 or d in X_DIRS)


def iota(shape, dim):
    return lax.broadcasted_iota(jnp.int32, shape, dim)


def split(value):
    high = value.astype(BF16)
    return high, (value - high.astype(F32)).astype(BF16)


def pack_x(fields):
    half = fields.shape[0] // 2
    first, second = fields[:half], fields[half:]
    upper = iota((1, 8, 128), 1) < RIM
    to_next = jnp.where(upper, pltpu.roll(first, RIM, 1), second)
    to_before = jnp.where(upper, first, pltpu.roll(second, RIM, 1))
    return to_next, to_before


def unpack_x(from_before, from_next):
    upper = iota((1, 8, 128), 1) < RIM
    first = jnp.where(upper, from_next, pltpu.roll(from_before, RIM, 1))
    second = jnp.where(upper, pltpu.roll(from_next, RIM, 1), from_before)
    return jnp.concatenate([first, second], axis=0)


def pack_y(fields):
    lane = iota((8, 128), 1)
    ahead, behind = jnp.zeros((8, 128), F32), jnp.zeros((8, 128), F32)
    for k in range(fields.shape[0]):
        place = RIM * k
        moved = pltpu.roll(fields[k], (place + RIM) % 128, 1)
        ahead = jnp.where((lane >= place) & (lane < place + RIM), moved, ahead)
        behind = jnp.where((lane >= place + RIM) & (lane < place + 2 * RIM), moved, behind)
    return ahead, behind


def unpack_y(ahead, behind, count):
    odd = (iota((8, 128), 1) & RIM) != 0
    tiles = jnp.where(odd, behind, ahead), jnp.where(odd, ahead, behind)
    slabs = []
    for k in range(count):
        slabs.append(pltpu.roll(tiles[k % 2], (124 - RIM * k) % 128, 1))
    return jnp.stack(slabs)


def slope(here, other, axis, both):
    size = here.shape[axis]
    place = iota((1,) * (here.ndim - 2) + (8, 128), axis)

    def shifted(mine, theirs, shift):
        entering = place < shift if shift > 0 else place >= size + shift
        return pltpu.roll(jnp.where(entering, theirs, mine), (-shift) % size, axis)

    def slope_of(mine, theirs):
        return 8.0 * (shifted(mine, theirs, 1) - shifted(mine, theirs, -1)) - (
            shifted(mine, theirs, 2) - shifted(mine, theirs, -2)
        )

    if both:
        return slope_of(here, other), slope_of(other, here)
    return slope_of(here, other)


def slope_z(field):
    nothing = jnp.zeros((2,) + field.shape[1:], F32)
    padded = jnp.concatenate([nothing, field, nothing], axis=0)
    n = field.shape[0]
    return 8.0 * (padded[3 : n + 3] - padded[1 : n + 1]) - (padded[4 : n + 4] - padded[:n])


def divergence(u, rim_x, rim_y, corner, lam, mu, lam_x, mu_x, lam_y, mu_y):
    ux, uy, uz = u[0], u[1], u[2]
    x_x, x_xh = slope(ux, rim_x[0], 1, True)
    y_x, y_xh = slope(uy, rim_x[1], 1, True)
    z_x, z_xh = slope(uz, rim_x[2], 1, True)
    x_y, x_yh = slope(ux, rim_y[0], 2, True)
    y_y, y_yh = slope(uy, rim_y[1], 2, True)
    z_y, z_yh = slope(uz, rim_y[2], 2, True)
    x_z, y_z, z_z = slope_z(ux), slope_z(uy), slope_z(uz)
    spread = lam * (x_x + y_y + z_z)
    s_xx = spread + 2.0 * mu * x_x
    s_yy = spread + 2.0 * mu * y_y
    s_zz = spread + 2.0 * mu * z_z
    s_xy = mu * (x_y + y_x)
    s_xz = mu * (x_z + z_x)
    s_yz = mu * (y_z + z_y)
    x_yr = slope(rim_x[0], corner[0], 2, False)
    y_yr = slope(rim_x[1], corner[1], 2, False)
    x_zr, z_zr = slope_z(rim_x[0]), slope_z(rim_x[2])
    s_xx_r = lam_x * (x_xh + y_yr + z_zr) + 2.0 * mu_x * x_xh
    s_xy_r = mu_x * (x_yr + y_xh)
    s_xz_r = mu_x * (x_zr + z_xh)
    x_xc = slope(rim_y[0], corner[0], 1, False)
    y_xc = slope(rim_y[1], corner[1], 1, False)
    y_zc, z_zc = slope_z(rim_y[1]), slope_z(rim_y[2])
    s_yy_c = lam_y * (x_xc + y_yh + z_zc) + 2.0 * mu_y * y_yh
    s_xy_c = mu_y * (x_yh + y_xc)
    s_yz_c = mu_y * (y_zc + z_yh)
    total_x = slope(s_xx, s_xx_r, 1, False) + slope(s_xy, s_xy_c, 2, False) + slope_z(s_xz)
    total_y = slope(s_xy, s_xy_r, 1, False) + slope(s_yy, s_yy_c, 2, False) + slope_z(s_yz)
    total_z = slope(s_xz, s_xz_r, 1, False) + slope(s_yz, s_yz_c, 2, False) + slope_z(s_zz)
    return jnp.stack([total_x, total_y, total_z])


def kernel(
    rows,
    owners,
    u_hbm,
    u_prev_hbm,
    lam_hbm,
    mu_hbm,
    buoy_hbm,
    q_hbm,
    q_prev_hbm,
    arch_hbm,
    stiff_hbm,
    couple_hbm,
    counts_hbm,
    cells_hbm,
    u_last_ref,
    u_before_ref,
    q_last_ref,
    q_before_ref,
    xs0,
    xs1,
    xr0,
    xr1,
    ys,
    yr,
    cr,
    a_out,
    a_in,
    w_out,
    w_in,
    p_out,
    p_in,
    table,
    frame_ref,
    near_ref,
    wide_ref,
    arch_ref,
    counts_ref,
    cells_ref,
    loaded,
    sent,
    arrived,
    entered,
):
    r, h = lax.axis_index("gx"), lax.axis_index("gy")
    nz = lam_hbm.shape[0]
    slots, freedoms = q_hbm.shape
    capacity = slots // owners
    kinds = couple_hbm.shape[0] // 3
    dt2 = TIME_STEP * TIME_STEP
    xs, xr = (xs0, xs1), (xr0, xr1)

    def target(direction):
        dx, dy = direction
        there = None
        for d, me, n in ((dx, r, rows), (dy, h, owners)):
            if d:
                ok = me + d < n if d > 0 else me > 0
                there = ok if there is None else there & ok
        return there, (r + dx, h + dy)

    def source(direction):
        return target((-direction[0], -direction[1]))

    loads = {}

    def start_load(name, ref, parts):
        sem = loaded.at[len(loads)]
        start, places = 0, {}
        for part, source_ref in parts:
            size = source_ref.shape[0]
            into = ref if len(parts) == 1 else ref.at[pl.ds(start, size)]
            pltpu.make_async_copy(source_ref, into, sem).start()
            places[part] = into
            start += size
        loads[name] = [pltpu.make_async_copy(ref, ref, sem)], places

    start_load("frame", frame_ref, (("q", q_hbm), ("couple", couple_hbm)))
    start_load("arch", arch_ref, (("arch", arch_hbm),))
    start_load("near", near_ref, (("u", u_hbm), ("lam", lam_hbm), ("mu", mu_hbm)))
    odd = lax.rem(r, 2) == 1
    even = jnp.logical_not(odd)

    def later(direction):
        dx, dy = direction
        there = target(direction)[0]
        if dy == 0 or direction == (-1, 1):
            return there & odd
        return there if dy > 0 else None

    def earlier(direction):
        dx, dy = direction
        there = target(direction)[0]
        if dy == 0 or direction == (1, -1):
            return there & even
        return there if dy < 0 else None

    barrier = pltpu.get_barrier_semaphore()
    for direction in DIRS:
        if later(direction) is not None:

            @pl.when(later(direction))
            def _(device=target(direction)[1]):
                pl.semaphore_signal(barrier, inc=1, device_id=device, device_id_type=MESH)

    for step in range(2, owners):

        @pl.when(h + step < owners)
        def _(device=(r, h + step)):
            pl.semaphore_signal(barrier, inc=1, device_id=device, device_id_type=MESH)

    arrivals = jnp.maximum(h - 1, 0)
    for direction in DIRS:
        if earlier(direction) is not None:
            arrivals = arrivals + earlier(direction).astype(jnp.int32)

    start_load("cells", cells_ref, (("cells", cells_hbm),))
    start_load("counts", counts_ref, (("counts", counts_hbm),))
    start_load(
        "wide",
        wide_ref,
        (
            ("buoy", buoy_hbm),
            ("stiff", stiff_hbm),
            ("q_prev", q_prev_hbm),
            ("u_prev", u_prev_hbm),
        ),
    )

    def half(ref, dx):
        return ref if dx == 0 else ref.at[pl.ds(RIM if dx > 0 else 0, RIM)]

    def y_place(turn, direction):
        dx, dy = direction
        k = 0 if dy > 0 else 1
        return half((cr if dx else yr).at[turn, k], dx)

    @pl.when(arrivals > 0)
    def _():
        pl.semaphore_wait(barrier, arrivals)

    def tell(direction, about):
        pl.semaphore_signal(
            entered.at[HEARD.index(about)],
            inc=1,
            device_id=target(direction)[1],
            device_id_type=MESH,
        )

    for direction in DIRS:
        if earlier(direction) is not None:

            @pl.when(earlier(direction))
            def _(direction=direction):
                tell(direction, (-direction[0], -direction[1]))

    for step in range(2, owners):

        @pl.when(h >= step)
        def _(step=step):
            pl.semaphore_signal(
                entered.at[len(HEARD) + step - 2],
                inc=1,
                device_id=(r, h - step),
                device_id_type=MESH,
            )

    for slot, direction in enumerate(X_DIRS):
        there, _ = source(direction)

        @pl.when(jnp.logical_not(there))
        def _(slot=slot):
            for buffer in xr:
                buffer[slot] = jnp.zeros(buffer.shape[1:], F32)

    for slot, direction in enumerate(Y_DIRS):
        there, _ = source(direction)

        @pl.when(jnp.logical_not(there))
        def _(direction=direction):
            for turn in range(STEPS):
                ref = y_place(turn, direction)
                ref[...] = jnp.zeros(ref.shape, F32)

    def load(part):
        for copies, places in loads.values():
            if part in places:
                while copies:
                    copies.pop().wait()
                return places[part]

    def wait_rows(sem, count):
        rows_of = wide_ref.at[pl.ds(0, count)]
        pltpu.make_async_copy(rows_of, rows_of, sem).wait()

    def wait_rows_of_rims(sem, turns, others=0):
        for nx in (1, 2):
            for ny in (1, 2):
                count = others
                for turn in turns:
                    count += nx * xs[turn].shape[1] * 8 + ny * 8 + nx * ny * RIM
                sides = [target(d)[0].astype(jnp.int32) for d in X_DIRS + ((0, 1), (0, -1))]

                @pl.when((sides[0] + sides[1] == nx) & (sides[2] + sides[3] == ny))
                def _(count=count):
                    wait_rows(sem, count)

    def x_copy(turn, slot, device):
        return pltpu.make_async_remote_copy(
            src_ref=xs[turn].at[slot],
            dst_ref=xr[turn].at[slot],
            send_sem=sent.at[0],
            recv_sem=arrived.at[turn],
            device_id=device,
            device_id_type=MESH,
        )

    def y_copy(turn, slot, device):
        return pltpu.make_async_remote_copy(
            src_ref=half(ys.at[turn, 0 if Y_DIRS[slot][1] > 0 else 1], Y_DIRS[slot][0]),
            dst_ref=y_place(turn, Y_DIRS[slot]),
            send_sem=sent.at[0],
            recv_sem=arrived.at[turn],
            device_id=device,
            device_id_type=MESH,
        )

    messages = ((a_out, a_in), (w_out, w_in), (p_out, p_in))

    def b_copy(which, step):
        other = lax.rem(h + step, owners)
        out, into = messages[which]
        return pltpu.make_async_remote_copy(
            src_ref=out if which == 0 else out.at[other],
            dst_ref=into.at[h],
            send_sem=sent.at[0],
            recv_sem=arrived.at[STEPS + which],
            device_id=(r, other),
            device_id_type=MESH,
        )

    def rim_copy(turn, direction):
        _, device = target(direction)
        if direction in X_DIRS:
            return x_copy(turn, X_DIRS.index(direction), device)
        return y_copy(turn, Y_DIRS.index(direction), device)

    def send_rim(turn, direction):
        there, _ = target(direction)

        @pl.when(there)
        def _():
            rim_copy(turn, direction).start()

    def send_rims(turn):
        for direction in X_DIRS + Y_DIRS:
            send_rim(turn, direction)

    def wait_rims(turn):
        wait_rows_of_rims(arrived.at[turn], (turn,))

    def wait_sends():
        size = 0
        for out, into in messages:
            size += into.shape[1] * into.shape[2] // 128
        wait_rows_of_rims(sent.at[0], range(STEPS), (owners - 1) * size)

    def put_rims(turn, fields):
        to_next, to_before = pack_x(fields)
        xs[turn][0] = to_next
        xs[turn][1] = to_before
        ys[turn, 0], ys[turn, 1] = pack_y(fields)

    def take_rims(turn, count):
        rim_x = unpack_x(xr[turn][0], xr[turn][1])
        rim_y = unpack_y(yr[turn, 0], yr[turn, 1], count)
        return rim_x, rim_y, unpack_y(cr[turn, 0], cr[turn, 1], 3 * nz)

    def send_buildings(which):
        for step in range(owners // 2, 0, -1):
            b_copy(which, step).start()
            if owners - step != step:
                b_copy(which, owners - step).start()

    def take_buildings(which):
        into = messages[which][1]
        others = into.at[pl.ds(0, owners - 1)]
        pltpu.make_async_copy(others, others, arrived.at[STEPS + which]).wait()
        into = into[...]
        if into.shape[1] < capacity:
            into = jnp.concatenate([into, pltpu.roll(into, into.shape[2] // 2, 2)], axis=1)
        return into.reshape(slots, into.shape[2])

    lane = iota((slots, 128), 1)
    part = lane & 31
    slot_row = iota((slots, 1), 0)
    square = (slots, slots)

    couple = load("couple")[...].reshape(3, kinds, freedoms)
    arch = jnp.sum(
        jnp.where(iota(square, 0) == iota(square, 1), load("arch")[...].astype(F32), 0.0),
        axis=1,
        keepdims=True,
    )
    is_kind = [arch == float(a) for a in range(kinds)]
    coupling = []
    for c in range(3):
        chosen = jnp.zeros((slots, freedoms), F32)
        for a in range(kinds):
            chosen = jnp.where(is_kind[a], couple[c, a : a + 1, :], chosen)
        coupling.append(chosen)

    def couple_sum(c, state):
        return jnp.sum(coupling[c] * state, axis=1, keepdims=True)

    q = load("q")[...]
    shear = [couple_sum(c, q) for c in range(3)]
    word = lane & 15
    shear = jnp.where(word < 4, shear[0], jnp.where(word < 8, shear[1], shear[2]))
    shear = shear.reshape(owners, 2, 8, 128)
    group = iota((8, 128), 1) // 16
    a_width = a_out.shape[1]
    for t in range(a_width // 128):
        tile = jnp.zeros((8, 128), F32)
        for k in range(8):
            which, home = divmod(8 * t + k, a_width // 32)
            if home < owners:
                tile = jnp.where(group == k, shear[home, which], tile)
        a_out[:, 128 * t : 128 * (t + 1)] = tile
    a_in[h] = a_out[...]
    for step in range(1, owners):

        @pl.when(h + step >= owners)
        def _(step=step):
            b_copy(0, step).start()

    u = load("u")[...].reshape(3, nz, 8, 128)
    lam, mu = load("lam")[...] * (1.0 / 144.0), load("mu")[...] * (1.0 / 144.0)
    put_rims(0, jnp.concatenate([u.reshape(3 * nz, 8, 128), lam, mu], axis=0))
    for direction in DIRS:
        if earlier(direction) is not None:

            @pl.when(earlier(direction))
            def _(direction=direction):
                rim_copy(0, direction).start()

    def send_later(direction, when):
        @pl.when(when)
        def _():
            pl.semaphore_wait(entered.at[HEARD.index(direction)], 1)
            if direction == (0, 1):
                b_copy(0, 1).start()
            rim_copy(0, direction).start()

    send_later((-1, 0), later((-1, 0)))

    cells = load("cells")[0].astype(F32)
    wide = (slots, slots * FOOTPRINT_CELLS)
    own = (iota(wide, 1) // FOOTPRINT_CELLS) == iota(wide, 0)
    corner_cell = jnp.min(jnp.where(own, cells, 1e9), axis=1, keepdims=True)
    corner_x = jnp.floor(corner_cell * (1.0 / 128.0))
    corner_y = corner_cell - 128.0 * corner_x
    along_y = lane.astype(F32) - corner_y
    in_y = ((along_y == 0.0) | (along_y == 1.0)).astype(F32)
    window_y = in_y.astype(BF16)
    along_x = (lane & 7).astype(F32) - corner_x
    row_counts = load("counts")[0, pl.ds(h, 1), :].astype(F32)
    pairs = (slots, owners)
    live_count = jnp.sum(
        jnp.where(iota(pairs, 0) // capacity == iota(pairs, 1), row_counts, 0.0),
        axis=1,
        keepdims=True,
    )
    live = (slot_row % capacity).astype(F32) < live_count
    weight = jnp.where(
        live & ((along_x == 0.0) | (along_x == 1.0)) & (part < 24), 1.0 / FOOTPRINT_CELLS, 0.0
    )
    base_weight = jnp.where(lane < 64, weight, 0.0)
    mine = [(lane < 64) & (part >= 8 * c) & (part < 8 * c + 8) for c in range(3)]

    def group_sum(c, value):
        return jnp.sum(jnp.where(mine[c], value, 0.0), axis=1, keepdims=True)

    def surface_motion(field):
        surface = field[:, 0]
        high = surface.astype(BF16).astype(F32)
        nothing = jnp.zeros((8, 128), F32)
        stacked = jnp.concatenate(
            [high.reshape(24, 128), nothing, (surface - high).reshape(24, 128), nothing]
            + [nothing] * 8,
            axis=0,
        ).astype(BF16)
        gathered = lax.dot_general(
            window_y, stacked, (((1,), (1,)), ((), ())), preferred_element_type=F32
        )
        return gathered * base_weight

    def halves(pull):
        high = pull.astype(BF16).astype(F32)
        return jnp.where((lane & 32) == 0, high, pull - high)

    def surface_force(pull):
        spread = lax.dot_general(
            pull.T.astype(BF16), window_y, (((1,), (0,)), ((), ())), preferred_element_type=F32
        )
        return (spread[0:24] + spread[32:56]).reshape(3, 8, 128)

    def drive_of(base):
        drive = coupling[0] * base[0]
        for c in range(1, 3):
            drive = drive + coupling[c] * base[c]
        return drive

    def stiff_term(state):
        high, low = split(state)
        stacked = jnp.concatenate([high.astype(F32), low.astype(F32)], axis=0)
        twice = jnp.concatenate([arch, arch], axis=0)
        spread = jnp.concatenate(
            [jnp.where(twice == float(a), stacked, 0.0).astype(BF16) for a in range(kinds)],
            axis=1,
        )
        product = jnp.dot(spread, table[...], preferred_element_type=F32)
        product = product[:, :freedoms] + product[:, freedoms:]
        return product[:slots] + product[slots:]

    base = surface_motion(u)
    home_base = [group_sum(c, base) for c in range(3)]

    gain = load("buoy")[...].reshape(nz, 8, 128) * dt2
    overlap_left, overlap_right = [], []
    for x in range(8):
        there = live & ((corner_x == float(x)) | (corner_x == float(x - 1)))
        window = jnp.where(there, in_y, 0.0)
        overlap_right.append(window)
        overlap_left.append(window * (gain[0, x : x + 1, :] * (1.0 / FOOTPRINT_CELLS**2)))
    left_high, left_low = split(jnp.concatenate(overlap_left, axis=1))
    right = jnp.concatenate(overlap_right, axis=1)
    width = w_out.shape[2]
    blank = [jnp.zeros((64, right.shape[1]), F32)]
    spare = width - 64 - slots
    after = [jnp.zeros((spare, right.shape[1]), F32)] if spare else []
    right = jnp.concatenate(blank + [right] + after, axis=0).astype(BF16)
    nt = (((1,), (1,)), ((), ()))
    overlap = lax.dot_general(left_high, right, nt, preferred_element_type=F32)
    overlap = overlap + lax.dot_general(left_low, right, nt, preferred_element_type=F32)

    def send_corner(direction, side):
        @pl.when(target(direction)[0] & side)
        def _():
            rim_copy(0, direction).start()

    send_later((0, 1), later((0, 1)))
    send_corner((-1, 1), even)
    send_later((-1, 1), later((-1, 1)))
    send_later((1, 0), later((1, 0)))
    send_corner((1, -1), odd)

    stiff_high, stiff_low = split(load("stiff")[...])
    table[:, :freedoms] = stiff_high
    table[:, freedoms:] = stiff_low
    coasting = 2.0 * q - load("q_prev")[...] - dt2 * stiff_term(q)
    fields = base
    columns = [couple_sum(c, coasting) for c in range(3)]
    pairs_of = ((0, 0), (0, 1), (0, 2), (1, 1), (1, 2), (2, 2))
    columns += [dt2 * couple_sum(c, coupling[d]) for c, d in pairs_of]
    places = (24, 25, 26, 27, 28, 29, 30, 31, 56)
    for place, column in zip(places, columns):
        fields = jnp.where(lane == place, column, fields)
    first = jnp.where(lane < 64, fields, overlap[:, :128])
    if width > 128:
        first = jnp.concatenate([first, overlap[:, 128:]], axis=1)
    w_out[...] = first.reshape(owners, capacity, width)
    w_in[h] = w_out[h]
    send_later((1, 1), later((1, 1)))
    for step in range(2, owners):

        @pl.when(h + step < owners)
        def _(step=step):
            pl.semaphore_wait(entered.at[len(HEARD) + step - 2], 1)
            b_copy(0, step).start()

    send_buildings(1)

    u_old = load("u_prev")[...].reshape(3, nz, 8, 128)

    shape = (3, nz, 8, 128)

    def push(field, rims, lam_mu, levels):
        fields = [part.reshape(shape)[:, :levels] for part in (field,) + rims]
        return divergence(*fields, *[part[:levels] for part in (lam, mu) + lam_mu])

    def on_surface(field, force):
        return jnp.concatenate([field[:, :1] + (gain[0] * force)[:, None], field[:, 1:]], axis=1)

    wait_rims(0)
    rim_x, rim_y, corner = take_rims(0, 5 * nz)
    lam_mu = rim_x[3 * nz : 4 * nz], rim_x[4 * nz :], rim_y[3 * nz : 4 * nz], rim_y[4 * nz :]
    rims = rim_x[: 3 * nz], rim_y[: 3 * nz], corner
    coast = 2.0 * u - u_old
    top = push(u, rims, lam_mu, min(nz, 5))[:, :1]
    motion = surface_motion(coast[:, :1] + gain[:1] * top).reshape(owners, 2, 8, 128)
    p_out[...] = jnp.where(
        iota((owners, 8, 128), 2) < 64, motion[:, 0], pltpu.roll(motion[:, 1], 64, 2)
    )
    p_in[h] = p_out[h]

    @pl.when(h >= 0)
    def _():
        send_buildings(2)

    free = coast + gain * push(u, rims, lam_mu, nz)

    shears = take_buildings(0)
    place = iota(shears.shape, 1) - 16 * h
    first = [
        jnp.sum(jnp.where(place == 4 * c, shears, 0.0), axis=1, keepdims=True) for c in range(3)
    ]
    pull = jnp.where(part < 8, first[0], jnp.where(part < 16, first[1], first[2]))
    u_new = on_surface(free, surface_force(halves(pull * weight)))
    u, u_old = u_new, u
    put_rims(1, u.reshape(3 * nz, 8, 128))
    send_rims(1)
    u_before_ref[...] = u

    words = take_buildings(1)
    low_words = words[:, :128]
    drive = drive_of([group_sum(c, low_words) for c in range(3)])
    q, q_old = coasting + dt2 * drive, q
    q_before_ref[...] = q
    stiff = stiff_term(q)

    gram = {}
    for place, pair in zip(places[3:], pairs_of):
        gram[pair] = gram[pair[::-1]] = low_words[:, place : place + 1]
    later = []
    for c in range(3):
        value = low_words[:, 24 + c : 25 + c]
        for d in range(3):
            value = value + gram[c, d] * home_base[d]
        later.append(value)
    later = jnp.where(part < 8, later[0], jnp.where(part < 16, later[1], later[2]))
    force = surface_force(halves(later * weight))

    left_high, left_low = split(words)
    blank = [jnp.zeros((64, shears.shape[1]), F32)]
    after = [jnp.zeros((spare, shears.shape[1]), F32)] if spare else []
    right = jnp.concatenate(blank + [shears] + after, axis=0)
    right_high, right_low = split(right)
    moved = jnp.dot(left_high, right_high, preferred_element_type=F32)
    moved = moved + jnp.dot(left_low, right_high, preferred_element_type=F32)
    moved = moved + jnp.dot(left_high, right_low, preferred_element_type=F32)
    moved_lane = iota(moved.shape, 1)
    moved_row = iota(moved.shape, 0) // capacity * 16
    moved = [
        jnp.sum(jnp.where(moved_lane == moved_row + 4 * c, moved, 0.0), axis=1, keepdims=True)
        for c in range(3)
    ]
    q_free = 2.0 * q - q_old + dt2 * (drive_of(moved) - stiff)
    u_free = on_surface(2.0 * u - u_old, force)

    def finish_frames():
        motion = take_buildings(2)
        q_last_ref[...] = q_free + dt2 * drive_of([group_sum(c, motion) for c in range(3)])

    rims_last = odd & (r + h > 1)
    pl.when(rims_last)(finish_frames)
    wait_rims(1)
    total = push(u, take_rims(1, 3 * nz), lam_mu, nz)
    u_last_ref[...] = u_free + gain * total

    pl.when(jnp.logical_not(rims_last))(finish_frames)
    wait_sends()


def shards(
    rows,
    owners,
    u_now,
    u_prev,
    lame_lambda,
    lame_mu,
    buoyancy,
    q_now,
    q_prev,
    archetype,
    stiffness,
    couple,
    counts,
    footprint,
):
    nz = lame_mu.shape[0]
    slots, freedoms = q_now.shape
    capacity = slots // owners
    kinds = stiffness.shape[0]
    pairs = (5 * nz) // 2, (3 * nz) // 2
    a_width = -(-32 * owners // 128) * 128
    w_width = -(-(64 + slots) // 128) * 128
    vmem = pl.BlockSpec(memory_space=pltpu.VMEM)
    hbm = pl.BlockSpec(memory_space=pltpu.HBM)
    dma = pltpu.SemaphoreType.DMA
    tiles = (3 * nz, 8, 128)
    operands = (
        u_now.reshape(tiles),
        u_prev.reshape(3 * nz * 8, 128),
        lame_lambda,
        lame_mu,
        buoyancy.reshape(nz * 8, 128),
        q_now,
        q_prev,
        archetype.reshape(1, slots),
        stiffness.reshape(kinds * freedoms, freedoms),
        couple.transpose(1, 0, 2).reshape(3 * kinds, freedoms),
        counts,
        footprint,
    )
    results = (
        jax.ShapeDtypeStruct(u_now.shape, F32),
        jax.ShapeDtypeStruct(u_now.shape, F32),
        jax.ShapeDtypeStruct(q_now.shape, F32),
        jax.ShapeDtypeStruct(q_now.shape, F32),
    )
    held = pl.pallas_call(
        functools.partial(kernel, rows, owners),
        out_shape=tuple(pltpu.VMEM(result.shape, result.dtype) for result in results),
        in_specs=[hbm] * len(operands),
        out_specs=(vmem,) * 4,
        scratch_shapes=[
            pltpu.VMEM((2, pairs[0], 8, 128), F32),
            pltpu.VMEM((2, pairs[1], 8, 128), F32),
            pltpu.VMEM((2, pairs[0], 8, 128), F32),
            pltpu.VMEM((2, pairs[1], 8, 128), F32),
            pltpu.VMEM((STEPS, 2, 8, 128), F32),
            pltpu.VMEM((STEPS, 2, 8, 128), F32),
            pltpu.VMEM((STEPS, 2, 8, 128), F32),
            pltpu.VMEM((8, a_width), F32),
            pltpu.VMEM((owners, 8, a_width), F32),
            pltpu.VMEM((owners, capacity, w_width), F32),
            pltpu.VMEM((owners, capacity, w_width), F32),
            pltpu.VMEM((owners, 8, 128), F32),
            pltpu.VMEM((owners, 8, 128), F32),
            pltpu.VMEM((kinds * freedoms, 2 * freedoms), BF16),
        ]
        + [
            pltpu.VMEM((slots + 3 * kinds, freedoms), F32),
            pltpu.VMEM((5 * nz, 8, 128), F32),
            pltpu.VMEM((kinds * freedoms + slots + 4 * nz * 8, freedoms), F32),
            pltpu.VMEM((1, slots), jnp.int32),
            pltpu.VMEM(counts.shape, jnp.int32),
            pltpu.VMEM(footprint.shape, jnp.int32),
            dma((6,)),
            dma((1,)),
            dma((STEPS + 3,)),
            pltpu.SemaphoreType.REGULAR((len(HEARD) + owners - 2,)),
        ],
        compiler_params=pltpu.CompilerParams(
            collective_id=0, has_side_effects=True, vmem_limit_bytes=60 * 1024 * 1024
        ),
    )(*operands)
    return pl.pallas_call(
        store,
        out_shape=results,
        in_specs=[vmem] * 4,
        out_specs=(hbm,) * 4,
        scratch_shapes=[pltpu.VMEM((2 * (3 * nz * 8 + slots), 128), F32), dma((1,))],
        compiler_params=pltpu.CompilerParams(vmem_limit_bytes=2 * 1024 * 1024),
    )(*held)


def store(*refs):
    whole, done = refs[8:]
    for k in range(4):
        pltpu.make_async_copy(refs[k], refs[4 + k], done.at[0]).start()
    pltpu.make_async_copy(whole, whole, done.at[0]).wait()


def solution(mesh):
    return jax.shard_map(
        functools.partial(shards, mesh.shape["gx"], mesh.shape["gy"]),
        mesh=mesh,
        in_specs=(
            P(None, None, "gx", "gy"),
            P(None, None, "gx", "gy"),
            P(None, "gx", "gy"),
            P(None, "gx", "gy"),
            P(None, "gx", "gy"),
            P(("gx", "gy"), None),
            P(("gx", "gy"), None),
            P(("gx", "gy")),
            P(),
            P(),
            P("gx", None, None),
            P("gx", "gy", None),
        ),
        out_specs=(
            P(None, None, "gx", "gy"),
            P(None, None, "gx", "gy"),
            P(("gx", "gy"), None),
            P(("gx", "gy"), None),
        ),
        check_vma=False,
    )
```

```python
import functools

import jax
import jax.numpy as jnp
from jax import lax
from jax.experimental import pallas as pl
from jax.experimental.pallas import tpu as pltpu
from jax.sharding import PartitionSpec as P

FOOTPRINT_CELLS = 4
STEPS = 2
TIME_STEP = 0.25
RIM = 4
MESH = pl.DeviceIdType.MESH
F32 = jnp.float32
BF16 = jnp.bfloat16

X_DIRS = ((1, 0), (-1, 0))
Y_DIRS = ((-1, 1), (-1, -1), (0, 1), (0, -1), (1, 1), (1, -1))
DIRS = X_DIRS + Y_DIRS
HEARD = tuple(d for d in DIRS if d[1] > 0 or d in X_DIRS)


def iota(shape, dim):
    return lax.broadcasted_iota(jnp.int32, shape, dim)


def split(value):
    high = value.astype(BF16)
    return high, (value - high.astype(F32)).astype(BF16)


def pack_x(fields):
    half = fields.shape[0] // 2
    first, second = fields[:half], fields[half:]
    upper = iota((1, 8, 128), 1) < RIM
    to_next = jnp.where(upper, pltpu.roll(first, RIM, 1), second)
    to_before = jnp.where(upper, first, pltpu.roll(second, RIM, 1))
    return to_next, to_before


def unpack_x(from_before, from_next):
    upper = iota((1, 8, 128), 1) < RIM
    first = jnp.where(upper, from_next, pltpu.roll(from_before, RIM, 1))
    second = jnp.where(upper, pltpu.roll(from_next, RIM, 1), from_before)
    return jnp.concatenate([first, second], axis=0)


def pack_y(fields):
    lane = iota((8, 128), 1)
    ahead, behind = jnp.zeros((8, 128), F32), jnp.zeros((8, 128), F32)
    for k in range(fields.shape[0]):
        place = RIM * k
        moved = pltpu.roll(fields[k], (place + RIM) % 128, 1)
        ahead = jnp.where((lane >= place) & (lane < place + RIM), moved, ahead)
        behind = jnp.where((lane >= place + RIM) & (lane < place + 2 * RIM), moved, behind)
    return ahead, behind


def unpack_y(ahead, behind, count):
    odd = (iota((8, 128), 1) & RIM) != 0
    tiles = jnp.where(odd, behind, ahead), jnp.where(odd, ahead, behind)
    slabs = []
    for k in range(count):
        slabs.append(pltpu.roll(tiles[k % 2], (124 - RIM * k) % 128, 1))
    return jnp.stack(slabs)


def slope(here, other, axis, both):
    size = here.shape[axis]
    place = iota((1,) * (here.ndim - 2) + (8, 128), axis)

    def shifted(mine, theirs, shift):
        entering = place < shift if shift > 0 else place >= size + shift
        return pltpu.roll(jnp.where(entering, theirs, mine), (-shift) % size, axis)

    def slope_of(mine, theirs):
        return 8.0 * (shifted(mine, theirs, 1) - shifted(mine, theirs, -1)) - (
            shifted(mine, theirs, 2) - shifted(mine, theirs, -2)
        )

    if both:
        return slope_of(here, other), slope_of(other, here)
    return slope_of(here, other)


def slope_z(field):
    nothing = jnp.zeros((2,) + field.shape[1:], F32)
    padded = jnp.concatenate([nothing, field, nothing], axis=0)
    n = field.shape[0]
    return 8.0 * (padded[3 : n + 3] - padded[1 : n + 1]) - (padded[4 : n + 4] - padded[:n])


def divergence(u, rim_x, rim_y, corner, lam, mu, lam_x, mu_x, lam_y, mu_y):
    ux, uy, uz = u[0], u[1], u[2]
    x_x, x_xh = slope(ux, rim_x[0], 1, True)
    y_x, y_xh = slope(uy, rim_x[1], 1, True)
    z_x, z_xh = slope(uz, rim_x[2], 1, True)
    x_y, x_yh = slope(ux, rim_y[0], 2, True)
    y_y, y_yh = slope(uy, rim_y[1], 2, True)
    z_y, z_yh = slope(uz, rim_y[2], 2, True)
    x_z, y_z, z_z = slope_z(ux), slope_z(uy), slope_z(uz)
    spread = lam * (x_x + y_y + z_z)
    s_xx = spread + 2.0 * mu * x_x
    s_yy = spread + 2.0 * mu * y_y
    s_zz = spread + 2.0 * mu * z_z
    s_xy = mu * (x_y + y_x)
    s_xz = mu * (x_z + z_x)
    s_yz = mu * (y_z + z_y)
    x_yr = slope(rim_x[0], corner[0], 2, False)
    y_yr = slope(rim_x[1], corner[1], 2, False)
    x_zr, z_zr = slope_z(rim_x[0]), slope_z(rim_x[2])
    s_xx_r = lam_x * (x_xh + y_yr + z_zr) + 2.0 * mu_x * x_xh
    s_xy_r = mu_x * (x_yr + y_xh)
    s_xz_r = mu_x * (x_zr + z_xh)
    x_xc = slope(rim_y[0], corner[0], 1, False)
    y_xc = slope(rim_y[1], corner[1], 1, False)
    y_zc, z_zc = slope_z(rim_y[1]), slope_z(rim_y[2])
    s_yy_c = lam_y * (x_xc + y_yh + z_zc) + 2.0 * mu_y * y_yh
    s_xy_c = mu_y * (x_yh + y_xc)
    s_yz_c = mu_y * (y_zc + z_yh)
    total_x = slope(s_xx, s_xx_r, 1, False) + slope(s_xy, s_xy_c, 2, False) + slope_z(s_xz)
    total_y = slope(s_xy, s_xy_r, 1, False) + slope(s_yy, s_yy_c, 2, False) + slope_z(s_yz)
    total_z = slope(s_xz, s_xz_r, 1, False) + slope(s_yz, s_yz_c, 2, False) + slope_z(s_zz)
    return jnp.stack([total_x, total_y, total_z])


def kernel(
    rows,
    owners,
    u_hbm,
    u_prev_hbm,
    lam_hbm,
    mu_hbm,
    buoy_hbm,
    q_hbm,
    q_prev_hbm,
    arch_hbm,
    stiff_hbm,
    couple_hbm,
    counts_hbm,
    cells_hbm,
    u_last_ref,
    u_before_ref,
    q_last_ref,
    q_before_ref,
    xs0,
    xs1,
    xr0,
    xr1,
    ys,
    yr,
    cr,
    a_out,
    a_in,
    w_out,
    w_in,
    p_out,
    p_in,
    table,
    frame_ref,
    near_ref,
    wide_ref,
    far_ref,
    arch_ref,
    counts_ref,
    cells_ref,
    loaded,
    sent,
    arrived,
    entered,
):
    r, h = lax.axis_index("gx"), lax.axis_index("gy")
    nz = lam_hbm.shape[0]
    slots, freedoms = q_hbm.shape
    capacity = slots // owners
    kinds = couple_hbm.shape[0] // 3
    dt2 = TIME_STEP * TIME_STEP
    xs, xr = (xs0, xs1), (xr0, xr1)

    def target(direction):
        dx, dy = direction
        there = None
        for d, me, n in ((dx, r, rows), (dy, h, owners)):
            if d:
                ok = me + d < n if d > 0 else me > 0
                there = ok if there is None else there & ok
        return there, (r + dx, h + dy)

    def source(direction):
        return target((-direction[0], -direction[1]))

    loads = {}

    def start_load(name, ref, parts):
        sem = loaded.at[len(loads)]
        start, places = 0, {}
        for part, source_ref in parts:
            size = source_ref.shape[0]
            into = ref if len(parts) == 1 else ref.at[pl.ds(start, size)]
            pltpu.make_async_copy(source_ref, into, sem).start()
            places[part] = into
            start += size
        loads[name] = [pltpu.make_async_copy(ref, ref, sem)], places

    start_load("frame", frame_ref, (("q", q_hbm), ("couple", couple_hbm)))
    start_load("arch", arch_ref, (("arch", arch_hbm),))
    start_load("near", near_ref, (("u", u_hbm), ("lam", lam_hbm), ("mu", mu_hbm)))
    odd = lax.rem(r, 2) == 1
    even = jnp.logical_not(odd)

    def later(direction):
        dx, dy = direction
        there = target(direction)[0]
        if dy == 0 or direction == (-1, 1):
            return there & odd
        return there if dy > 0 else None

    def earlier(direction):
        dx, dy = direction
        there = target(direction)[0]
        if dy == 0 or direction == (1, -1):
            return there & even
        return there if dy < 0 else None

    barrier = pltpu.get_barrier_semaphore()
    for direction in DIRS:
        if later(direction) is not None:

            @pl.when(later(direction))
            def _(device=target(direction)[1]):
                pl.semaphore_signal(barrier, inc=1, device_id=device, device_id_type=MESH)

    for step in range(2, owners):

        @pl.when(h + step < owners)
        def _(device=(r, h + step)):
            pl.semaphore_signal(barrier, inc=1, device_id=device, device_id_type=MESH)

    arrivals = jnp.maximum(h - 1, 0)
    for direction in DIRS:
        if earlier(direction) is not None:
            arrivals = arrivals + earlier(direction).astype(jnp.int32)

    start_load("cells", cells_ref, (("cells", cells_hbm),))
    start_load("counts", counts_ref, (("counts", counts_hbm),))
    start_load("far", far_ref, (("u_prev", u_prev_hbm), ("buoy", buoy_hbm)))
    start_load("wide", wide_ref, (("stiff", stiff_hbm), ("q_prev", q_prev_hbm)))

    def half(ref, dx):
        return ref if dx == 0 else ref.at[pl.ds(RIM if dx > 0 else 0, RIM)]

    def y_place(turn, direction):
        dx, dy = direction
        k = 0 if dy > 0 else 1
        return half((cr if dx else yr).at[turn, k], dx)

    @pl.when(arrivals > 0)
    def _():
        pl.semaphore_wait(barrier, arrivals)

    def tell(direction, about):
        pl.semaphore_signal(
            entered.at[HEARD.index(about)],
            inc=1,
            device_id=target(direction)[1],
            device_id_type=MESH,
        )

    for direction in DIRS:
        if earlier(direction) is not None:

            @pl.when(earlier(direction))
            def _(direction=direction):
                tell(direction, (-direction[0], -direction[1]))

    for step in range(2, owners):

        @pl.when(h >= step)
        def _(step=step):
            pl.semaphore_signal(
                entered.at[len(HEARD) + step - 2],
                inc=1,
                device_id=(r, h - step),
                device_id_type=MESH,
            )

    for slot, direction in enumerate(X_DIRS):
        there, _ = source(direction)

        @pl.when(jnp.logical_not(there))
        def _(slot=slot):
            for buffer in xr:
                buffer[slot] = jnp.zeros(buffer.shape[1:], F32)

    for slot, direction in enumerate(Y_DIRS):
        there, _ = source(direction)

        @pl.when(jnp.logical_not(there))
        def _(direction=direction):
            for turn in range(STEPS):
                ref = y_place(turn, direction)
                ref[...] = jnp.zeros(ref.shape, F32)

    def load(part):
        for copies, places in loads.values():
            if part in places:
                while copies:
                    copies.pop().wait()
                return places[part]

    def wait_rows(sem, count):
        rows_of = wide_ref.at[pl.ds(0, count)]
        pltpu.make_async_copy(rows_of, rows_of, sem).wait()

    def wait_rows_of_rims(sem, turns, others=0):
        for nx in (1, 2):
            for ny in (1, 2):
                count = others
                for turn in turns:
                    count += nx * xs[turn].shape[1] * 8 + ny * 8 + nx * ny * RIM
                sides = [target(d)[0].astype(jnp.int32) for d in X_DIRS + ((0, 1), (0, -1))]

                @pl.when((sides[0] + sides[1] == nx) & (sides[2] + sides[3] == ny))
                def _(count=count):
                    wait_rows(sem, count)

    def x_copy(turn, slot, device):
        return pltpu.make_async_remote_copy(
            src_ref=xs[turn].at[slot],
            dst_ref=xr[turn].at[slot],
            send_sem=sent.at[0],
            recv_sem=arrived.at[turn],
            device_id=device,
            device_id_type=MESH,
        )

    def y_copy(turn, slot, device):
        return pltpu.make_async_remote_copy(
            src_ref=half(ys.at[turn, 0 if Y_DIRS[slot][1] > 0 else 1], Y_DIRS[slot][0]),
            dst_ref=y_place(turn, Y_DIRS[slot]),
            send_sem=sent.at[0],
            recv_sem=arrived.at[turn],
            device_id=device,
            device_id_type=MESH,
        )

    messages = ((a_out, a_in), (w_out, w_in), (p_out, p_in))

    def b_copy(which, step):
        other = lax.rem(h + step, owners)
        out, into = messages[which]
        return pltpu.make_async_remote_copy(
            src_ref=out if which == 0 else out.at[other],
            dst_ref=into.at[h],
            send_sem=sent.at[0],
            recv_sem=arrived.at[STEPS + which],
            device_id=(r, other),
            device_id_type=MESH,
        )

    def rim_copy(turn, direction):
        _, device = target(direction)
        if direction in X_DIRS:
            return x_copy(turn, X_DIRS.index(direction), device)
        return y_copy(turn, Y_DIRS.index(direction), device)

    def send_rim(turn, direction):
        there, _ = target(direction)

        @pl.when(there)
        def _():
            rim_copy(turn, direction).start()

    def send_rims(turn):
        for direction in X_DIRS + Y_DIRS:
            send_rim(turn, direction)

    def wait_rims(turn):
        wait_rows_of_rims(arrived.at[turn], (turn,))

    def wait_sends():
        size = 0
        for out, into in messages:
            size += into.shape[1] * into.shape[2] // 128
        wait_rows_of_rims(sent.at[0], range(STEPS), (owners - 1) * size)

    def put_rims(turn, fields):
        to_next, to_before = pack_x(fields)
        xs[turn][0] = to_next
        xs[turn][1] = to_before
        ys[turn, 0], ys[turn, 1] = pack_y(fields)

    def take_rims(turn, count):
        rim_x = unpack_x(xr[turn][0], xr[turn][1])
        rim_y = unpack_y(yr[turn, 0], yr[turn, 1], count)
        return rim_x, rim_y, unpack_y(cr[turn, 0], cr[turn, 1], 3 * nz)

    def send_buildings(which):
        for step in range(owners // 2, 0, -1):
            b_copy(which, step).start()
            if owners - step != step:
                b_copy(which, owners - step).start()

    def take_buildings(which):
        into = messages[which][1]
        others = into.at[pl.ds(0, owners - 1)]
        pltpu.make_async_copy(others, others, arrived.at[STEPS + which]).wait()
        into = into[...]
        if into.shape[1] < capacity:
            into = jnp.concatenate([into, pltpu.roll(into, into.shape[2] // 2, 2)], axis=1)
        return into.reshape(slots, into.shape[2])

    lane = iota((slots, 128), 1)
    part = lane & 31
    slot_row = iota((slots, 1), 0)
    square = (slots, slots)

    couple = load("couple")[...].reshape(3, kinds, freedoms)
    arch = jnp.sum(
        jnp.where(iota(square, 0) == iota(square, 1), load("arch")[...].astype(F32), 0.0),
        axis=1,
        keepdims=True,
    )
    is_kind = [arch == float(a) for a in range(kinds)]
    coupling = []
    for c in range(3):
        chosen = jnp.zeros((slots, freedoms), F32)
        for a in range(kinds):
            chosen = jnp.where(is_kind[a], couple[c, a : a + 1, :], chosen)
        coupling.append(chosen)

    def couple_sum(c, state):
        return jnp.sum(coupling[c] * state, axis=1, keepdims=True)

    q = load("q")[...]
    shear = [couple_sum(c, q) for c in range(3)]
    word = lane & 15
    shear = jnp.where(word < 4, shear[0], jnp.where(word < 8, shear[1], shear[2]))
    shear = shear.reshape(owners, 2, 8, 128)
    group = iota((8, 128), 1) // 16
    a_width = a_out.shape[1]
    for t in range(a_width // 128):
        tile = jnp.zeros((8, 128), F32)
        for k in range(8):
            which, home = divmod(8 * t + k, a_width // 32)
            if home < owners:
                tile = jnp.where(group == k, shear[home, which], tile)
        a_out[:, 128 * t : 128 * (t + 1)] = tile
    a_in[h] = a_out[...]
    for step in range(1, owners):

        @pl.when(h + step >= owners)
        def _(step=step):
            b_copy(0, step).start()

    u = load("u")[...].reshape(3, nz, 8, 128)
    lam, mu = load("lam")[...] * (1.0 / 144.0), load("mu")[...] * (1.0 / 144.0)
    put_rims(0, jnp.concatenate([u.reshape(3 * nz, 8, 128), lam, mu], axis=0))
    for direction in DIRS:
        if earlier(direction) is not None:

            @pl.when(earlier(direction))
            def _(direction=direction):
                rim_copy(0, direction).start()

    def send_later(direction, when):
        @pl.when(when)
        def _():
            pl.semaphore_wait(entered.at[HEARD.index(direction)], 1)
            if direction == (0, 1):
                b_copy(0, 1).start()
            rim_copy(0, direction).start()

    send_later((-1, 0), later((-1, 0)))

    cells = load("cells")[0].astype(F32)
    wide = (slots, slots * FOOTPRINT_CELLS)
    own = (iota(wide, 1) // FOOTPRINT_CELLS) == iota(wide, 0)
    corner_cell = jnp.min(jnp.where(own, cells, 1e9), axis=1, keepdims=True)
    corner_x = jnp.floor(corner_cell * (1.0 / 128.0))
    corner_y = corner_cell - 128.0 * corner_x
    along_y = lane.astype(F32) - corner_y
    in_y = ((along_y == 0.0) | (along_y == 1.0)).astype(F32)
    window_y = in_y.astype(BF16)
    along_x = (lane & 7).astype(F32) - corner_x
    row_counts = load("counts")[0, pl.ds(h, 1), :].astype(F32)
    pairs = (slots, owners)
    live_count = jnp.sum(
        jnp.where(iota(pairs, 0) // capacity == iota(pairs, 1), row_counts, 0.0),
        axis=1,
        keepdims=True,
    )
    live = (slot_row % capacity).astype(F32) < live_count
    weight = jnp.where(
        live & ((along_x == 0.0) | (along_x == 1.0)) & (part < 24), 1.0 / FOOTPRINT_CELLS, 0.0
    )
    base_weight = jnp.where(lane < 64, weight, 0.0)
    mine = [(lane < 64) & (part >= 8 * c) & (part < 8 * c + 8) for c in range(3)]

    def group_sum(c, value):
        return jnp.sum(jnp.where(mine[c], value, 0.0), axis=1, keepdims=True)

    def surface_motion(field):
        surface = field[:, 0]
        high = surface.astype(BF16).astype(F32)
        nothing = jnp.zeros((8, 128), F32)
        stacked = jnp.concatenate(
            [high.reshape(24, 128), nothing, (surface - high).reshape(24, 128), nothing]
            + [nothing] * 8,
            axis=0,
        ).astype(BF16)
        gathered = lax.dot_general(
            window_y, stacked, (((1,), (1,)), ((), ())), preferred_element_type=F32
        )
        return gathered * base_weight

    def halves(pull):
        high = pull.astype(BF16).astype(F32)
        return jnp.where((lane & 32) == 0, high, pull - high)

    def surface_force(pull):
        spread = lax.dot_general(
            pull.T.astype(BF16), window_y, (((1,), (0,)), ((), ())), preferred_element_type=F32
        )
        return (spread[0:24] + spread[32:56]).reshape(3, 8, 128)

    def drive_of(base):
        drive = coupling[0] * base[0]
        for c in range(1, 3):
            drive = drive + coupling[c] * base[c]
        return drive

    def stiff_term(state):
        high, low = split(state)
        stacked = jnp.concatenate([high.astype(F32), low.astype(F32)], axis=0)
        twice = jnp.concatenate([arch, arch], axis=0)
        spread = jnp.concatenate(
            [jnp.where(twice == float(a), stacked, 0.0).astype(BF16) for a in range(kinds)],
            axis=1,
        )
        product = jnp.dot(spread, table[...], preferred_element_type=F32)
        product = product[:, :freedoms] + product[:, freedoms:]
        return product[:slots] + product[slots:]

    base = surface_motion(u)
    home_base = [group_sum(c, base) for c in range(3)]

    gain = load("buoy")[...] * dt2
    overlap_left, overlap_right = [], []
    for x in range(8):
        there = live & ((corner_x == float(x)) | (corner_x == float(x - 1)))
        window = jnp.where(there, in_y, 0.0)
        overlap_right.append(window)
        overlap_left.append(window * (gain[0, x : x + 1, :] * (1.0 / FOOTPRINT_CELLS**2)))
    left_high, left_low = split(jnp.concatenate(overlap_left, axis=1))
    right = jnp.concatenate(overlap_right, axis=1)
    width = w_out.shape[2]
    blank = [jnp.zeros((64, right.shape[1]), F32)]
    spare = width - 64 - slots
    after = [jnp.zeros((spare, right.shape[1]), F32)] if spare else []
    right = jnp.concatenate(blank + [right] + after, axis=0).astype(BF16)
    nt = (((1,), (1,)), ((), ()))
    overlap = lax.dot_general(left_high, right, nt, preferred_element_type=F32)
    overlap = overlap + lax.dot_general(left_low, right, nt, preferred_element_type=F32)

    def send_corner(direction, side):
        @pl.when(target(direction)[0] & side)
        def _():
            rim_copy(0, direction).start()

    send_later((0, 1), later((0, 1)))
    send_corner((-1, 1), even)
    send_later((-1, 1), later((-1, 1)))
    send_later((1, 0), later((1, 0)))
    send_corner((1, -1), odd)

    stiff_high, stiff_low = split(load("stiff")[...])
    table[:, :freedoms] = stiff_high
    table[:, freedoms:] = stiff_low
    coasting = 2.0 * q - load("q_prev")[...] - dt2 * stiff_term(q)
    fields = base
    columns = [couple_sum(c, coasting) for c in range(3)]
    pairs_of = ((0, 0), (0, 1), (0, 2), (1, 1), (1, 2), (2, 2))
    columns += [dt2 * couple_sum(c, coupling[d]) for c, d in pairs_of]
    places = (24, 25, 26, 27, 28, 29, 30, 31, 56)
    for place, column in zip(places, columns):
        fields = jnp.where(lane == place, column, fields)
    first = jnp.where(lane < 64, fields, overlap[:, :128])
    if width > 128:
        first = jnp.concatenate([first, overlap[:, 128:]], axis=1)
    w_out[...] = first.reshape(owners, capacity, width)
    w_in[h] = w_out[h]
    send_later((1, 1), later((1, 1)))
    for step in range(2, owners):

        @pl.when(h + step < owners)
        def _(step=step):
            pl.semaphore_wait(entered.at[len(HEARD) + step - 2], 1)
            b_copy(0, step).start()

    send_buildings(1)

    u_old = load("u_prev")[...].reshape(3, nz, 8, 128)

    shape = (3, nz, 8, 128)

    def push(field, rims, lam_mu, levels):
        fields = [part.reshape(shape)[:, :levels] for part in (field,) + rims]
        return divergence(*fields, *[part[:levels] for part in (lam, mu) + lam_mu])

    def on_surface(field, force):
        return jnp.concatenate([field[:, :1] + (gain[0] * force)[:, None], field[:, 1:]], axis=1)

    wait_rims(0)
    rim_x, rim_y, corner = take_rims(0, 5 * nz)
    lam_mu = rim_x[3 * nz : 4 * nz], rim_x[4 * nz :], rim_y[3 * nz : 4 * nz], rim_y[4 * nz :]
    rims = rim_x[: 3 * nz], rim_y[: 3 * nz], corner
    coast = 2.0 * u - u_old
    top = push(u, rims, lam_mu, min(nz, 5))[:, :1]
    motion = surface_motion(coast[:, :1] + gain[:1] * top).reshape(owners, 2, 8, 128)
    p_out[...] = jnp.where(
        iota((owners, 8, 128), 2) < 64, motion[:, 0], pltpu.roll(motion[:, 1], 64, 2)
    )
    p_in[h] = p_out[h]

    @pl.when(h >= 0)
    def _():
        send_buildings(2)

    free = coast + gain * push(u, rims, lam_mu, nz)

    shears = take_buildings(0)
    place = iota(shears.shape, 1) - 16 * h
    first = [
        jnp.sum(jnp.where(place == 4 * c, shears, 0.0), axis=1, keepdims=True) for c in range(3)
    ]
    pull = jnp.where(part < 8, first[0], jnp.where(part < 16, first[1], first[2]))
    u_new = on_surface(free, surface_force(halves(pull * weight)))
    u, u_old = u_new, u
    put_rims(1, u.reshape(3 * nz, 8, 128))
    send_rims(1)
    u_before_ref[...] = u

    words = take_buildings(1)
    low_words = words[:, :128]
    drive = drive_of([group_sum(c, low_words) for c in range(3)])
    q, q_old = coasting + dt2 * drive, q
    q_before_ref[...] = q
    stiff = stiff_term(q)

    gram = {}
    for place, pair in zip(places[3:], pairs_of):
        gram[pair] = gram[pair[::-1]] = low_words[:, place : place + 1]
    later = []
    for c in range(3):
        value = low_words[:, 24 + c : 25 + c]
        for d in range(3):
            value = value + gram[c, d] * home_base[d]
        later.append(value)
    later = jnp.where(part < 8, later[0], jnp.where(part < 16, later[1], later[2]))
    force = surface_force(halves(later * weight))

    left_high, left_low = split(words)
    blank = [jnp.zeros((64, shears.shape[1]), F32)]
    after = [jnp.zeros((spare, shears.shape[1]), F32)] if spare else []
    right = jnp.concatenate(blank + [shears] + after, axis=0)
    right_high, right_low = split(right)
    moved = jnp.dot(left_high, right_high, preferred_element_type=F32)
    moved = moved + jnp.dot(left_low, right_high, preferred_element_type=F32)
    moved = moved + jnp.dot(left_high, right_low, preferred_element_type=F32)
    moved_lane = iota(moved.shape, 1)
    moved_row = iota(moved.shape, 0) // capacity * 16
    moved = [
        jnp.sum(jnp.where(moved_lane == moved_row + 4 * c, moved, 0.0), axis=1, keepdims=True)
        for c in range(3)
    ]
    q_free = 2.0 * q - q_old + dt2 * (drive_of(moved) - stiff)
    u_free = on_surface(2.0 * u - u_old, force)

    def finish_frames():
        motion = take_buildings(2)
        q_last_ref[...] = q_free + dt2 * drive_of([group_sum(c, motion) for c in range(3)])

    rims_last = odd & (r + h > 1)
    pl.when(rims_last)(finish_frames)
    wait_rims(1)
    total = push(u, take_rims(1, 3 * nz), lam_mu, nz)
    u_last_ref[...] = u_free + gain * total

    pl.when(jnp.logical_not(rims_last))(finish_frames)
    wait_sends()


def shards(
    rows,
    owners,
    u_now,
    u_prev,
    lame_lambda,
    lame_mu,
    buoyancy,
    q_now,
    q_prev,
    archetype,
    stiffness,
    couple,
    counts,
    footprint,
):
    nz = lame_mu.shape[0]
    slots, freedoms = q_now.shape
    capacity = slots // owners
    kinds = stiffness.shape[0]
    pairs = (5 * nz) // 2, (3 * nz) // 2
    a_width = -(-32 * owners // 128) * 128
    w_width = -(-(64 + slots) // 128) * 128
    vmem = pl.BlockSpec(memory_space=pltpu.VMEM)
    hbm = pl.BlockSpec(memory_space=pltpu.HBM)
    dma = pltpu.SemaphoreType.DMA
    tiles = (3 * nz, 8, 128)
    operands = (
        u_now.reshape(tiles),
        u_prev.reshape(tiles),
        lame_lambda,
        lame_mu,
        buoyancy,
        q_now,
        q_prev,
        archetype.reshape(1, slots),
        stiffness.reshape(kinds * freedoms, freedoms),
        couple.transpose(1, 0, 2).reshape(3 * kinds, freedoms),
        counts,
        footprint,
    )
    results = (
        jax.ShapeDtypeStruct(u_now.shape, F32),
        jax.ShapeDtypeStruct(u_now.shape, F32),
        jax.ShapeDtypeStruct(q_now.shape, F32),
        jax.ShapeDtypeStruct(q_now.shape, F32),
    )
    held = pl.pallas_call(
        functools.partial(kernel, rows, owners),
        out_shape=tuple(pltpu.VMEM(result.shape, result.dtype) for result in results),
        in_specs=[hbm] * len(operands),
        out_specs=(vmem,) * 4,
        scratch_shapes=[
            pltpu.VMEM((2, pairs[0], 8, 128), F32),
            pltpu.VMEM((2, pairs[1], 8, 128), F32),
            pltpu.VMEM((2, pairs[0], 8, 128), F32),
            pltpu.VMEM((2, pairs[1], 8, 128), F32),
            pltpu.VMEM((STEPS, 2, 8, 128), F32),
            pltpu.VMEM((STEPS, 2, 8, 128), F32),
            pltpu.VMEM((STEPS, 2, 8, 128), F32),
            pltpu.VMEM((8, a_width), F32),
            pltpu.VMEM((owners, 8, a_width), F32),
            pltpu.VMEM((owners, capacity, w_width), F32),
            pltpu.VMEM((owners, capacity, w_width), F32),
            pltpu.VMEM((owners, 8, 128), F32),
            pltpu.VMEM((owners, 8, 128), F32),
            pltpu.VMEM((kinds * freedoms, 2 * freedoms), BF16),
        ]
        + [
            pltpu.VMEM((slots + 3 * kinds, freedoms), F32),
            pltpu.VMEM((5 * nz, 8, 128), F32),
            pltpu.VMEM((kinds * freedoms + slots, freedoms), F32),
            pltpu.VMEM((4 * nz, 8, 128), F32),
            pltpu.VMEM((1, slots), jnp.int32),
            pltpu.VMEM(counts.shape, jnp.int32),
            pltpu.VMEM(footprint.shape, jnp.int32),
            dma((7,)),
            dma((1,)),
            dma((STEPS + 3,)),
            pltpu.SemaphoreType.REGULAR((len(HEARD) + owners - 2,)),
        ],
        compiler_params=pltpu.CompilerParams(
            collective_id=0, has_side_effects=True, vmem_limit_bytes=60 * 1024 * 1024
        ),
    )(*operands)
    return pl.pallas_call(
        store,
        out_shape=results,
        in_specs=[vmem] * 4,
        out_specs=(hbm,) * 4,
        scratch_shapes=[pltpu.VMEM((2 * (3 * nz * 8 + slots), 128), F32), dma((1,))],
        compiler_params=pltpu.CompilerParams(vmem_limit_bytes=2 * 1024 * 1024),
    )(*held)


def store(*refs):
    whole, done = refs[8:]
    for k in range(4):
        pltpu.make_async_copy(refs[k], refs[4 + k], done.at[0]).start()
    pltpu.make_async_copy(whole, whole, done.at[0]).wait()


def solution(mesh):
    return jax.shard_map(
        functools.partial(shards, mesh.shape["gx"], mesh.shape["gy"]),
        mesh=mesh,
        in_specs=(
            P(None, None, "gx", "gy"),
            P(None, None, "gx", "gy"),
            P(None, "gx", "gy"),
            P(None, "gx", "gy"),
            P(None, "gx", "gy"),
            P(("gx", "gy"), None),
            P(("gx", "gy"), None),
            P(("gx", "gy")),
            P(),
            P(),
            P("gx", None, None),
            P("gx", "gy", None),
        ),
        out_specs=(
            P(None, None, "gx", "gy"),
            P(None, None, "gx", "gy"),
            P(("gx", "gy"), None),
            P(("gx", "gy"), None),
        ),
        check_vma=False,
    )
```
